128 devices in a mesh: grp: 4 (over y_lo, core), gx: 32 (over x, z, y_hi).
Axes of the slice: x: 4, y: 4 (y_hi: 2, y_lo: 2; y = y_hi * 2 + y_lo), z: 4, core: 2. Of those that a mesh axis runs over, the one named last changes fastest.
Arguments:
- atmosphere: float32 [40, 64, 4096], P(None, 'grp', 'gx'), may hold values from -6 to 6
- diffusion: float32 [64, 4096], P('grp', 'gx'), may hold values from 0.01 to 0.09
- coriolis: float32 [64], P('grp'), may hold values from -0.25 to 0.25
- mixing: float32 [10], replicated, may hold values from 0.02 to 0.2
- stencil_owner: int32 [32, 3, 288], replicated, may hold values from 0 to 95, as said below
- stencil_cell: int32 [32, 3, 288], replicated, may hold values from 0 to 2047, as said below
- stencil_weight: float32 [32, 3, 288], replicated, as said below
- feedback_owner: int32 [32, 128], replicated, may hold values from 0 to 95, as said below
- feedback_cell: int32 [32, 128], replicated, may hold values from 0 to 2047, as said below
Outputs:
- evolved: float32 [40, 64, 4096], P(None, 'grp', 'gx')
The draws below stay inside these ranges and needn't reach their ends.
Inputs may be any that keep to these rules, and one draw needn't show every extreme that they name: `stencil_owner`: parent devices; any parent device may serve any cycle point. The 3 pairs of one cycle point name different cells. `stencil_cell`: cells of the owners in stencil_owner. `stencil_weight`: Positive; the 3 weights of a cycle point sum to one. `feedback_owner`: parent devices; no parent cell is named by two feedback entries. `feedback_cell`: cells of the owners in feedback_owner.
All inputs are finite; a program needn't handle non-finite values.
Results may differ from the reference program's by a relative error of at most 0.0001.
Values sent between devices are 32-bit elements; how exact they have to be, the bound alone decides.
No kernel may reach another device: no remote copies, remote signals or barrier semaphores. Data moves between devices by JAX's collectives and lax.ppermute only.
A program may use at most 128 MiB of HBM per device.

```python
import math
import jax
import jax.numpy as jnp

ROWS_DEV = 16
COLS_DEV = 128
FIELDS = 4
LEVELS = 10
STENCIL = 3
SUBSTEPS = 2
PERIM = 288
COARSE = 128
N_GRP = 4
N_GX = 32


def locate(positions):
    width_all = N_GX * COLS_DEV
    grid_rows = positions // width_all
    grid_cols = positions % width_all
    owners = grid_rows // ROWS_DEV * N_GX + grid_cols // COLS_DEV
    targets = grid_rows % ROWS_DEV * COLS_DEV + grid_cols % COLS_DEV
    return (owners.astype(jnp.int32), targets.astype(jnp.int32))


def position_of(owners, targets):
    width_all = N_GX * COLS_DEV
    grid_row = owners // N_GX * ROWS_DEV + targets // COLS_DEV
    grid_col = owners % N_GX * COLS_DEV + targets % COLS_DEV
    return (grid_row * width_all + grid_col).astype(jnp.int32)


def stencil_positions(key):
    key = jax.random.fold_in(key, 11)
    total = (N_GRP - 1) * N_GX * ROWS_DEV * COLS_DEV
    half_total = total // 2
    first_key, second_key, third_key, fourth_key = jax.random.split(key, 4)
    first = jax.random.randint(first_key, (N_GX, PERIM), 0, total, dtype=jnp.int32)
    blocks = jnp.arange(N_GX, dtype=jnp.int32)
    forced_owner = jnp.stack([blocks, blocks + N_GX, blocks + 2 * N_GX, jnp.zeros_like(blocks)], axis=1)
    forced_cell = jax.random.randint(fourth_key, (N_GX, 4), 0, ROWS_DEV * COLS_DEV, dtype=jnp.int32)
    first = first.at[:, 2:6].set(position_of(forced_owner, forced_cell))
    first = first.at[0, 0].set(total - 1).at[0, 1].set(0)
    step_near = jax.random.randint(second_key, (N_GX, PERIM), 1, half_total, dtype=jnp.int32)
    step_far = jax.random.randint(third_key, (N_GX, PERIM), half_total, total, dtype=jnp.int32)
    members = jnp.stack([first, (first + step_near) % total, (first + step_far) % total], axis=1)
    return locate(members.astype(jnp.int32))


def feedback_positions(key):
    key = jax.random.fold_in(key, 13)
    total = (N_GRP - 1) * N_GX * ROWS_DEV * COLS_DEV
    needed = N_GX * COARSE
    first_key, second_key = jax.random.split(key)
    inner = 1 + jax.random.permutation(first_key, jnp.arange(total - 2, dtype=jnp.int32))[:needed - 2]
    chosen = jnp.concatenate([jnp.array([0, total - 1], dtype=jnp.int32), inner.astype(jnp.int32)])
    order = jax.random.permutation(second_key, jnp.arange(needed, dtype=jnp.int32))
    chosen = chosen[order]
    return locate(chosen.reshape(N_GX, COARSE))


def draw_stencil_owner(key, part):
    return stencil_positions(key)[0]


def draw_stencil_cell(key, part):
    return stencil_positions(key)[1]


def draw_stencil_weight(key, part):
    key = jax.random.fold_in(key, 7)
    raw = jax.random.uniform(key, (N_GX, STENCIL, PERIM), jnp.float32, 0.2, 1.0)
    return raw / jnp.sum(raw, axis=1, keepdims=True)


def draw_feedback_owner(key, part):
    return feedback_positions(key)[0]


def draw_feedback_cell(key, part):
    return feedback_positions(key)[1]


def shard_levels(rng, dims, pieces, low, largest):
    loudness, own = 1.0, jax.random.fold_in(rng, 6)
    for axis_at, shards_of in pieces:
        heights = jnp.exp(jax.random.uniform(jax.random.fold_in(own, axis_at), (shards_of,), jnp.float32, low / len(pieces), largest / len(pieces)))
        loudness = loudness * jnp.repeat(heights, dims[axis_at] // shards_of).reshape([-1 if axis == axis_at else 1 for axis in range(len(dims))])
    return loudness


def bell_draw(rng, shape, spread, reach, cuts=(), held_as=jnp.bfloat16):
    entries = spread * jax.random.normal(rng, shape, jnp.float32)
    if cuts:
        entries = entries * shard_levels(rng, shape, cuts, -0.22, 0.18)
    return jnp.clip(entries, -reach, reach).astype(held_as)


def setup_inputs(seed: int = 0) -> dict:
    streams_of = jax.random.split(jax.random.key(seed), 10)
    return {
        "atmosphere": bell_draw(streams_of[0], (FIELDS * LEVELS, N_GRP * ROWS_DEV, N_GX * COLS_DEV), 1.0, 6.0, ((1, 4), (2, 32)), jnp.float32),
        "diffusion": jnp.clip(jnp.exp(math.log(0.09) - 2.1972246 * jax.random.uniform(streams_of[1], (N_GRP * ROWS_DEV, N_GX * COLS_DEV), jnp.float32) ** shard_levels(streams_of[1], (N_GRP * ROWS_DEV, N_GX * COLS_DEV), ((0, 4), (1, 32)), -0.2, 0.2)), 0.01, 0.09),
        "coriolis": jnp.clip(jax.random.uniform(streams_of[2], (N_GRP * ROWS_DEV,), jnp.float32, -0.25, 0.25) * shard_levels(streams_of[2], (N_GRP * ROWS_DEV,), ((0, 4),), -0.4, 0.0), -0.25, 0.25),
        "mixing": jnp.clip(jnp.exp(jax.random.uniform(streams_of[3], (LEVELS,), jnp.float32, math.log(0.02), math.log(0.2))), 0.02, 0.2),
        "stencil_owner": draw_stencil_owner(jax.random.fold_in(streams_of[9], 71), 0),
        "stencil_cell": draw_stencil_cell(jax.random.fold_in(streams_of[9], 71), 0),
        "stencil_weight": draw_stencil_weight(jax.random.fold_in(streams_of[9], 71), 0),
        "feedback_owner": draw_feedback_owner(jax.random.fold_in(streams_of[9], 71), 0),
        "feedback_cell": draw_feedback_cell(jax.random.fold_in(streams_of[9], 71), 0),
    }


def advance(extended, center, diffusion, coriolis, mixing):
    neighbours = (extended[:, 1:-1, :-2] + extended[:, 1:-1, 2:] + extended[:, :-2, 1:-1]
                  + extended[:, 2:, 1:-1] + extended[:, :-2, 2:] + extended[:, 2:, :-2])
    laplace = neighbours - 6.0 * center
    lane_count, row_count, col_count = center.shape
    level_count = mixing.shape[0]
    stacked = center.reshape(lane_count // level_count, level_count, row_count, col_count)
    upper = jnp.concatenate([stacked[:, 1:], stacked[:, -1:]], axis=1)
    lower = jnp.concatenate([stacked[:, :1], stacked[:, :-1]], axis=1)
    vertical = mixing[None, :, None, None] * (upper - 2.0 * stacked + lower)
    rotation = jnp.concatenate([(coriolis[:, None] * stacked[1])[None],
                                (-coriolis[:, None] * stacked[0])[None],
                                jnp.zeros_like(stacked[2:])], axis=0)
    return center + diffusion * laplace + (vertical + rotation).reshape(center.shape)


def global_position(owners, targets):
    width_all = N_GX * COLS_DEV
    grid_row = (owners // N_GX) * ROWS_DEV + targets // COLS_DEV
    grid_col = (owners % N_GX) * COLS_DEV + targets % COLS_DEV
    return (grid_row * width_all + grid_col).astype(jnp.int32)


def reference(atmosphere, diffusion, coriolis, mixing, stencil_owner, stencil_cell, stencil_weight, feedback_owner, feedback_cell):
    lane_count = atmosphere.shape[0]
    parent_rows = (N_GRP - 1) * ROWS_DEV
    width_all = N_GX * COLS_DEV
    parent = atmosphere[:, :parent_rows]
    nested = atmosphere[:, parent_rows:]
    parent_diff, nest_diff = diffusion[:parent_rows], diffusion[parent_rows:]
    parent_cor, nest_cor = coriolis[:parent_rows], coriolis[parent_rows:]
    cycle_index = [global_position(stencil_owner[:, member, :], stencil_cell[:, member, :]).reshape(-1)
                  for member in range(STENCIL)]
    feed_index = global_position(feedback_owner, feedback_cell).reshape(-1)
    perimeter = stencil_owner.shape[2]
    for substep in range(SUBSTEPS):
        parent_flat = parent.reshape(lane_count, -1)
        cycle = jnp.zeros((lane_count, N_GX * perimeter), jnp.float32)
        for member in range(STENCIL):
            cycle = cycle + parent_flat[:, cycle_index[member]] * stencil_weight[:, member, :].reshape(-1)
        cycle = cycle.reshape(lane_count, N_GX, perimeter)
        padded = jnp.pad(parent, ((0, 0), (1, 1), (0, 0)), mode="edge")
        padded = jnp.pad(padded, ((0, 0), (0, 0), (1, 1)), mode="wrap")
        parent_new = advance(padded, parent, parent_diff, parent_cor, mixing)
        nest_pad = jnp.pad(nested, ((0, 0), (1, 1), (1, 1)))
        nest_new = advance(nest_pad, nested, nest_diff, nest_cor, mixing)
        nest_new = nest_new.at[:, :, 0].set(cycle[:, 0, 2 * COLS_DEV:2 * COLS_DEV + ROWS_DEV])
        nest_new = nest_new.at[:, :, -1].set(cycle[:, N_GX - 1, 2 * COLS_DEV + ROWS_DEV:])
        nest_new = nest_new.at[:, 0, :].set(cycle[:, :, :COLS_DEV].reshape(lane_count, -1))
        nest_new = nest_new.at[:, -1, :].set(cycle[:, :, COLS_DEV:2 * COLS_DEV].reshape(lane_count, -1))
        coarse = nest_new.reshape(lane_count, ROWS_DEV // 4, 4, width_all // 4, 4).mean(axis=(2, 4))
        coarse = coarse.reshape(lane_count, ROWS_DEV // 4, N_GX, COLS_DEV // 4)
        coarse = coarse.transpose(0, 2, 1, 3).reshape(lane_count, -1)
        parent = parent_new.reshape(lane_count, -1).at[:, feed_index].set(coarse).reshape(parent_new.shape)
        nested = nest_new
    return jnp.concatenate([parent, nested], axis=1)
```

```python
import jax
import jax.numpy as jnp
from jax import lax
from jax.experimental import pallas as pl
from jax.experimental.pallas import tpu as pltpu
from jax.sharding import PartitionSpec as P

SUBSTEPS = 2
F32 = jnp.float32
LANES = 40
ROWS = 16
COLS = 128
LEVELS = 10
GX = 32
PARENTS = 96
DEVICES = 128
PERIM = 288
TILES = 9
SLOTS = 25
HITS = 8
EDGE = 40
FG = 5
T1_ROW = 128
T2_ROW = 144
TAB_ROWS = 160
PGROUPS = 20
GROUPS = 22
VMEM_LIMIT = 48 * 1024 * 1024


def padded(cells, sides, width):
    for axis, dim in sides:
        count = lax.axis_size(axis)
        head = lax.slice_in_dim(cells, 0, width, axis=dim)
        tail = lax.slice_in_dim(cells, cells.shape[dim] - width, cells.shape[dim], axis=dim)
        cells = jnp.concatenate(
            [
                lax.ppermute(tail, axis, [(i, (i + 1) % count) for i in range(count)]),
                cells,
                lax.ppermute(head, axis, [((i + 1) % count, i) for i in range(count)]),
            ],
            axis=dim,
        )
    return cells


def broadcast(value, axis, source):
    kept = jnp.where(lax.axis_index(axis) == source, value, 0).astype(value.dtype)
    return lax.psum(kept, axis)


def advance(extended, center, diffusion, coriolis, mixing):
    neighbours = (
        extended[:, 1:-1, :-2]
        + extended[:, 1:-1, 2:]
        + extended[:, :-2, 1:-1]
        + extended[:, 2:, 1:-1]
        + extended[:, :-2, 2:]
        + extended[:, 2:, :-2]
    )
    laplace = neighbours - 6.0 * center
    lane_count, row_count, col_count = center.shape
    level_count = mixing.shape[0]
    stacked = center.reshape(lane_count // level_count, level_count, row_count, col_count)
    upper = jnp.concatenate([stacked[:, 1:], stacked[:, -1:]], axis=1)
    lower = jnp.concatenate([stacked[:, :1], stacked[:, :-1]], axis=1)
    vertical = mixing[None, :, None, None] * (upper - 2.0 * stacked + lower)
    rotation = jnp.concatenate(
        [
            (coriolis[:, None] * stacked[1])[None],
            (-coriolis[:, None] * stacked[0])[None],
            jnp.zeros_like(stacked[2:]),
        ],
        axis=0,
    )
    return center + diffusion * laplace + (vertical + rotation).reshape(center.shape)


def dense_plan(
    atmosphere,
    diffusion,
    coriolis,
    mixing,
    stencil_owner,
    stencil_cell,
    stencil_weight,
    feedback_owner,
    feedback_cell,
):
    lane_count, row_count, col_count = atmosphere.shape
    cell_count = row_count * col_count
    column_count = lax.axis_size("gx")
    group_count = lax.axis_size("grp")
    group_index = lax.axis_index("grp")
    column_index = lax.axis_index("gx")
    own_rank = group_index * column_count + column_index
    is_nested = group_index == group_count - 1
    perimeter = stencil_owner.shape[2]
    owner_flat = feedback_owner.reshape(-1)
    target_flat = feedback_cell.reshape(-1)
    current = atmosphere
    for substep in range(SUBSTEPS):
        flat_now = current.reshape(lane_count, cell_count)
        cycle_terms = jnp.zeros((lane_count, column_count * perimeter), jnp.float32)
        for member in range(stencil_owner.shape[1]):
            mine = stencil_owner[:, member, :].reshape(-1) == own_rank
            positions = jnp.where(mine, stencil_cell[:, member, :].reshape(-1), 0)
            weights = jnp.where(mine, stencil_weight[:, member, :].reshape(-1), 0.0)
            cycle_terms = cycle_terms + jnp.take(flat_now, positions, axis=1) * weights
        padding = jnp.zeros((lane_count, (group_count - 1) * column_count * perimeter), jnp.float32)
        everything = jnp.concatenate([padding, cycle_terms], axis=1)
        cycle = lax.psum_scatter(everything, ("grp", "gx"), scatter_dimension=1, tiled=True)
        extended = padded(current, (("grp", 1), ("gx", 2)), 1)
        upper_rim = jnp.where(group_index == 0, extended[:, 1:2, :], extended[:, 0:1, :])
        lower_rim = jnp.where(
            group_index == group_count - 2, extended[:, -2:-1, :], extended[:, -1:, :]
        )
        extended = jnp.concatenate([upper_rim, extended[:, 1:-1, :], lower_rim], axis=1)
        fresh = advance(extended, current, diffusion, coriolis, mixing)
        left_edge = jnp.where(
            column_index == 0, cycle[:, 2 * col_count : 2 * col_count + row_count], fresh[:, :, 0]
        )
        right_edge = jnp.where(
            column_index == column_count - 1, cycle[:, 2 * col_count + row_count :], fresh[:, :, -1]
        )
        framed = fresh.at[:, :, 0].set(left_edge).at[:, :, -1].set(right_edge)
        framed = (
            framed.at[:, 0, :]
            .set(cycle[:, :col_count])
            .at[:, -1, :]
            .set(cycle[:, col_count : 2 * col_count])
        )
        fresh = jnp.where(is_nested, framed, fresh)
        coarse = fresh.reshape(lane_count, row_count // 4, 4, col_count // 4, 4).mean(axis=(2, 4))
        coarse = coarse.reshape(lane_count, -1)
        fresh_flat = fresh.reshape(lane_count, cell_count)
        shared = broadcast(coarse, "grp", group_count - 1)
        place_positions = jnp.where(owner_flat == own_rank, target_flat, cell_count)
        result_flat = fresh_flat.at[:, place_positions].set(
            lax.all_gather(shared, "gx", axis=1, tiled=True), mode="drop"
        )
        current = result_flat.reshape(lane_count, row_count, col_count)
    return current


def iota(shape, dim):
    return lax.broadcasted_iota(jnp.int32, shape, dim)


def chunks(count, step, body):
    def run(c, carry):
        for s in range(step):
            body(c * step + s)
        return carry

    lax.fori_loop(0, count // step, run, 0)


def take(tile, index):
    return jnp.take_along_axis(tile, index, axis=1, mode="promise_in_bounds")


def ranks(masks):
    rows = masks[0].shape[0]
    stacked = jnp.concatenate([jnp.where(m, 1.0, 0.0) for m in masks], axis=0)
    stacked = stacked.astype(jnp.bfloat16)
    before = jnp.where(iota((128, 128), 0) < iota((128, 128), 1), 1.0, 0.0).astype(jnp.bfloat16)
    ones = jnp.ones((128, 128), jnp.bfloat16)
    within = jnp.dot(stacked, before, preferred_element_type=F32)
    totals = jnp.dot(stacked, ones, preferred_element_type=F32)
    carry = jnp.zeros((rows, 128), F32)
    found = []
    for t in range(len(masks)):
        found.append(within[t * rows : (t + 1) * rows] + carry)
        carry = carry + totals[t * rows : (t + 1) * rows]
    return found, carry


def slot_table(masks, values, slots, mark_s, value_s):
    found, total = ranks(masks)
    for t in range(TILES):
        mark_s[t] = jnp.where(masks[t], found[t], -1.0)
        value_s[t] = values[t]
    slot_of = lax.rem(iota((8, 128), 1), slots)
    parts = []
    for part in range(GX // 8):
        span = slice(8 * part, 8 * part + 8)
        marks = [mark_s[t, span, :] for t in range(TILES)]
        vals = [value_s[t, span, :] for t in range(TILES)]
        table = jnp.zeros((8, 128), F32)
        for j in range(slots):
            picked = [jnp.where(m == float(j), v, 0.0) for m, v in zip(marks, vals)]
            while len(picked) > 1:
                picked = [sum(picked[k : k + 2]) for k in range(0, len(picked), 2)]
            table = jnp.where(slot_of == j, jnp.sum(picked[0], axis=1, keepdims=True), table)
        parts.append(table)
    return jnp.concatenate(parts, axis=0), total


def send_cells(rows_s, table_ref, send_ref, flag):
    lane = iota((8, 128), 1)
    group_of = lane // SLOTS
    table = table_ref[0:GX, :]
    for g in range(7):
        index = jnp.zeros((1, 128), jnp.int32)
        members = [q for q in range(5 * g, 5 * g + 5) if q < GX]
        for q in members:
            index = jnp.where(group_of[0:1] == q - 5 * g, table[q : q + 1, :], index)
        index = jnp.broadcast_to(index, (8, 128))
        col = jnp.bitwise_and(index, 127)
        row = jnp.right_shift(index, 7)
        cells = [jnp.zeros((8, 128), F32) for _ in range(FG)]
        for r in range(ROWS):
            here = row == r
            for k in range(FG):
                cells[k] = jnp.where(here, take(rows_s[r, 8 * k : 8 * k + 8, :], col), cells[k])
        for q in members:
            block = jnp.zeros((8, 128), F32) if flag is None else flag
            for k in range(FG):
                shift = (SLOTS * (k - (q - 5 * g))) % 128
                moved = cells[k] if shift == 0 else pltpu.roll(cells[k], shift, 1)
                block = jnp.where(group_of == k, moved, block)
            send_ref[PARENTS + q] = block


def edge_block(x_ref, col, base):
    lane = iota((8, 128), 1)
    block = base
    for h in range(2):
        for f in range(LANES):
            edge = x_ref[f, 8 * h : 8 * h + 8, col : col + 1]
            block = jnp.where(lane == EDGE + h * LANES + f, edge, block)
    return block


def send_parent_edges(x_ref, send_ref, grp, gx, base):
    first = edge_block(x_ref, 0, base)
    last = edge_block(x_ref, COLS - 1, base)
    right = lax.rem(gx + 1, GX)
    left = lax.rem(gx + GX - 1, GX)
    send_ref[grp * GX + right] = last
    send_ref[grp * GX + left] = first

    @pl.when(grp > 0)
    def _():
        send_ref[(grp - 1) * GX + right] = last

    @pl.when(grp < 2)
    def _():
        send_ref[(grp + 1) * GX + left] = first


def unpack_edge(block):
    return jnp.concatenate([block, pltpu.roll(block, 128 - LANES, 1)], axis=0)


def update(x_ref, out_ref, recv_ref, above_ref, below_ref, diff_ref, cor_ref, mix_ref, grp, gx):
    nest = grp == 3
    right = lax.rem(gx + 1, GX)
    left = lax.rem(gx + GX - 1, GX)
    lane = iota((ROWS, COLS), 1)
    row = iota((ROWS, COLS), 0)
    from_left = unpack_edge(recv_ref[grp * GX + left])
    from_right = unpack_edge(recv_ref[grp * GX + right])
    top_right = unpack_edge(recv_ref[jnp.maximum(grp - 1, 0) * GX + right])[ROWS - 1 : ROWS]
    low_left = unpack_edge(recv_ref[jnp.minimum(grp + 1, 3) * GX + left])[0:1]
    top_right = jnp.where(grp == 0, from_right[0:1], top_right)
    low_left = jnp.where(grp == 2, from_left[ROWS - 1 : ROWS], low_left)
    left_sum = from_left + jnp.where(row == ROWS - 1, low_left, pltpu.roll(from_left, ROWS - 1, 0))
    right_sum = from_right + jnp.where(row == 0, top_right, pltpu.roll(from_right, 1, 0))
    nest_left = from_left + jnp.where(row == ROWS - 1, 0.0, pltpu.roll(from_left, ROWS - 1, 0))
    nest_right = from_right + jnp.where(row == 0, 0.0, pltpu.roll(from_right, 1, 0))
    left_sum = jnp.where(nest, jnp.where(gx == 0, 0.0, nest_left), left_sum)
    right_sum = jnp.where(nest, jnp.where(gx == GX - 1, 0.0, nest_right), right_sum)
    diff = diff_ref[...]
    cor = jnp.zeros((ROWS, COLS), F32)
    for r in range(ROWS):
        cor = jnp.where(row == r, cor_ref[r], cor)
    for f in range(LANES):
        level = f % LEVELS
        x = x_ref[f]
        if above_ref is None:
            above = jnp.zeros((1, COLS), F32)
            below = jnp.zeros((1, COLS), F32)
        else:
            above = jnp.where(grp == 0, x[0:1], above_ref[f : f + 1, :])
            below = jnp.where(grp == 2, x[ROWS - 1 : ROWS], below_ref[f : f + 1, :])
            above = jnp.where(nest, 0.0, above)
            below = jnp.where(nest, 0.0, below)
        up = jnp.where(row == 0, above, pltpu.roll(x, 1, 0))
        down = jnp.where(row == ROWS - 1, below, pltpu.roll(x, ROWS - 1, 0))
        at = EDGE + f
        westward = jnp.where(lane == 0, left_sum[:, at : at + 1], pltpu.roll(x + down, 1, 1))
        eastward = jnp.where(
            lane == COLS - 1, right_sum[:, at : at + 1], pltpu.roll(x + up, COLS - 1, 1)
        )
        laplace = (westward + eastward) + (up + down) - 6.0 * x
        upper = x if level == LEVELS - 1 else x_ref[f + 1]
        lower = x if level == 0 else x_ref[f - 1]
        extra = mix_ref[level] * (upper - 2.0 * x + lower)
        if f < LEVELS:
            extra = extra + cor * x_ref[f + LEVELS]
        elif f < 2 * LEVELS:
            extra = extra - cor * x_ref[f - LEVELS]
        out_ref[f] = x + diff * laplace + extra


def regroup(recv_ref, base, groups, per, width, group_s, first):
    lane = iota((8, 128), 1)
    member_of = lane // width

    def body(g):
        tiles = [jnp.zeros((8, 128), F32) for _ in range(FG)]
        for i in range(per):
            block = recv_ref[jnp.minimum(base + g * per + i, DEVICES - 1)]
            for k in range(FG):
                shift = (width * (i - k)) % 128
                moved = block if shift == 0 else pltpu.roll(block, shift, 1)
                tiles[k] = jnp.where(member_of == i, moved, tiles[k])
        for k in range(FG):
            group_s[first + g, 8 * k : 8 * k + 8, :] = tiles[k]

    chunks(groups, 2 if groups % 2 == 0 else 1, body)


def interpolate(tabs_ref, first_row, weight_s, group_s, groups, cycle_s):
    cycle_s[...] = jnp.zeros((3, LANES, 128), F32)

    def body(t):
        code = jnp.broadcast_to(tabs_ref[pl.ds(first_row + t, 1), :], (8, 128))
        index = jnp.bitwise_and(code, 127)
        group = jnp.right_shift(code, 7)
        cells = [jnp.zeros((8, 128), F32) for _ in range(FG)]
        for g in range(groups):
            here = group == g
            for k in range(FG):
                cells[k] = jnp.where(here, take(group_s[g, 8 * k : 8 * k + 8, :], index), cells[k])
        weight = weight_s[pl.ds(t, 1), :]
        span = lax.rem(t, 3)
        for k in range(FG):
            cycle_s[span, 8 * k : 8 * k + 8, :] += weight * cells[k]

    chunks(TILES, 1, body)


def load_weights(weight_ref, weight_s, gx):
    weight_s[...] = jnp.zeros((16, 128), F32)
    for k in range(3):
        own = weight_ref[pl.ds(gx, 1), k, :]
        weight_s[3 * k : 3 * k + 1, :] = own[:, 0:128]
        weight_s[3 * k + 1 : 3 * k + 2, :] = own[:, 128:256]
        weight_s[3 * k + 2 : 3 * k + 3, 0:32] = own[:, 256:288]


def prescribe(out_ref, cycle_s, gx):
    lane = iota((ROWS, COLS), 1)

    @pl.when(jnp.logical_or(gx == 0, gx == GX - 1))
    def _():
        turned = jnp.concatenate([cycle_s[2], jnp.zeros((88, 128), F32)], axis=0).T
        column = jnp.where(gx == 0, turned[0:ROWS, :], turned[ROWS : 2 * ROWS, :])
        at = jnp.where(gx == 0, 0, COLS - 1)
        for f in range(LANES):
            out_ref[f] = jnp.where(lane == at, column[:, f : f + 1], out_ref[f])

    out_ref[:, 0, :] = cycle_s[0]
    out_ref[:, ROWS - 1, :] = cycle_s[1]


def coarsen(out_ref):
    coarse = jnp.zeros((LANES, 128), F32)
    for i in range(4):
        total = (out_ref[:, 4 * i, :] + out_ref[:, 4 * i + 1, :]) + (
            out_ref[:, 4 * i + 2, :] + out_ref[:, 4 * i + 3, :]
        )
        mean = jnp.where(iota((128, 128), 1) == 32 * i + iota((128, 128), 0) // 4, 1.0 / 16.0, 0.0)
        coarse = coarse + jnp.dot(
            total, mean, precision=lax.Precision.HIGHEST, preferred_element_type=F32
        )
    return coarse


def send_coarse(coarse, tabs_ref, send_ref):
    group_of = iota((8, 128), 1) // SLOTS

    def body(o):
        index = jnp.broadcast_to(tabs_ref[pl.ds(o, 1), :], (8, 128))
        block = take(coarse[0:8], index)
        for k in range(1, FG):
            block = jnp.where(group_of == k, take(coarse[8 * k : 8 * k + 8], index), block)
        send_ref[o] = block

    chunks(PARENTS, 8, body)


def send_hits(coarse, tabs_ref, send_ref, base):
    group_of = iota((8, 128), 1) // HITS

    def body(q):
        index = jnp.broadcast_to(tabs_ref[pl.ds(PARENTS + q, 1), :], (8, 128))
        block = base
        for k in range(FG):
            block = jnp.where(group_of == k, take(coarse[8 * k : 8 * k + 8], index), block)
        send_ref[PARENTS + q] = block

    chunks(GX, 8, body)


def feed_back(src_ref, out_ref, recv_ref, map_ref, group_s):
    regroup(recv_ref, PARENTS, 7, 5, SLOTS, group_s, 0)
    for r in range(ROWS):
        code = jnp.broadcast_to(map_ref[r : r + 1, :], (8, 128))
        index = jnp.bitwise_and(code, 127)
        group = jnp.right_shift(code, 7)
        cells = [src_ref[8 * k : 8 * k + 8, r, :] for k in range(FG)]
        for g in range(7):
            here = group == g
            for k in range(FG):
                cells[k] = jnp.where(here, take(group_s[g, 8 * k : 8 * k + 8, :], index), cells[k])
        for k in range(FG):
            out_ref[8 * k : 8 * k + 8, r, :] = cells[k]


def feedback_map(owner_ref, cell_ref, map_ref, me):
    owner = owner_ref[...]
    cell = cell_ref[...]
    own = owner == me
    found, _ = ranks([own])
    slot = jnp.minimum(found[0], float(SLOTS - 1))
    row = jnp.where(own, jnp.right_shift(cell, 7), -1)
    col = jnp.bitwise_and(cell, 127)
    planes = jnp.zeros((2 * ROWS, 128), F32)
    for q in range(GX):
        here = iota((ROWS, 128), 0) == row[q : q + 1, :]
        codes = jnp.concatenate(
            [jnp.where(here, float(q + 1), 0.0), jnp.where(here, slot[q : q + 1, :], 0.0)], axis=0
        )
        hot = jnp.where(iota((128, 128), 0) == col[q : q + 1, :], 1.0, 0.0)
        planes = planes + lax.dot_general(
            codes.astype(jnp.bfloat16),
            hot.astype(jnp.bfloat16),
            (((1,), (1,)), ((), ())),
            preferred_element_type=F32,
        )
    block = planes[0:ROWS].astype(jnp.int32) - 1
    slots = planes[ROWS : 2 * ROWS].astype(jnp.int32)
    group = jnp.right_shift(block * 205, 10)
    code = group * 128 + (block - 5 * group) * SLOTS + slots
    map_ref[...] = jnp.where(block < 0, -1, code)


def first_kernel(
    x_ref,
    owner_ref,
    cell_ref,
    fb_owner_ref,
    fb_cell_ref,
    fb_owner_sm,
    fb_cell_sm,
    send_ref,
    tabs_ref,
    last_row_ref,
    first_row_ref,
    gid_s,
    mark_s,
    value_s,
    rows_s,
    turned_s,
):
    grp = lax.axis_index("grp")
    gx = lax.axis_index("gx")
    me = grp * GX + gx
    lane = iota((8, 128), 1)
    last_row_ref[...] = x_ref[:, ROWS - 1, :]
    first_row_ref[...] = x_ref[:, 0, :]
    for k in range(3):
        gid = owner_ref[:, k, :] * 2048 + cell_ref[:, k, :]
        gid_s[3 * k] = gid[:, 0:128]
        gid_s[3 * k + 1] = gid[:, 128:256]
        gid_s[3 * k + 2] = jnp.full((GX, 128), -1, jnp.int32)
        gid_s[3 * k + 2, :, 0:32] = gid[:, 256:288]

    def flag_block(over):
        worst = jnp.max(over, axis=0, keepdims=True)
        flag = jnp.where(worst > 0.5, 1.0, 0.0)
        return jnp.where(lane == 127, jnp.broadcast_to(flag, (8, 128)), 0.0)

    @pl.when(grp < 3)
    def _():
        gids = [gid_s[t] for t in range(TILES)]
        masks = [jnp.right_shift(g, 11) == me for g in gids]
        values = [jnp.bitwise_and(g, 2047).astype(F32) for g in gids]
        table, total = slot_table(masks, values, SLOTS, mark_s, value_s)
        tabs_ref[0:GX, :] = table.astype(jnp.int32)
        base = flag_block(jnp.where(total > float(SLOTS), 1.0, 0.0))
        send_ref[...] = jnp.broadcast_to(base[None], (DEVICES, 8, 128))
        for r in range(ROWS):
            rows_s[r] = x_ref[:, r, :]
        send_cells(rows_s, tabs_ref, send_ref, base)
        send_parent_edges(x_ref, send_ref, grp, gx, base)

    @pl.when(grp == 3)
    def _():
        own = fb_owner_ref[pl.ds(gx, 1), :]
        hot = iota((PARENTS, 128), 0) == own
        found, total = ranks([hot])
        over = jnp.max(jnp.where(total > float(SLOTS), 1.0, 0.0), axis=0, keepdims=True)
        rank = jnp.sum(jnp.where(hot, found[0], 0.0), axis=0, keepdims=True)
        slot_of = lax.rem(iota((128, 128), 0), SLOTS).astype(F32)
        chosen = jnp.where(slot_of == rank, iota((128, 128), 1).astype(F32), 0.0)
        table = lax.dot_general(
            jnp.where(hot, 1.0, 0.0).astype(jnp.bfloat16),
            chosen.astype(jnp.bfloat16),
            (((1,), (1,)), ((), ())),
            preferred_element_type=F32,
        )
        tabs_ref[0:PARENTS, :] = table.astype(jnp.int32)

        terms = [gid_s[t, pl.ds(gx, 1), :] for t in range(TILES)]
        owners = [jnp.right_shift(t, 11) for t in terms]
        hots = [iota((PARENTS, 128), 0) == o for o in owners]
        found, _ = ranks(hots)
        codes = []
        for t in range(TILES):
            slot = jnp.sum(jnp.where(hots[t], found[t], 0.0), axis=0, keepdims=True)
            slot = jnp.minimum(slot.astype(jnp.int32), SLOTS - 1)
            group = jnp.right_shift(owners[t] * 205, 10)
            codes.append(group * 128 + (owners[t] - 5 * group) * SLOTS + slot)
            tabs_ref[T1_ROW + t : T1_ROW + t + 1, :] = codes[t]

        def seek(c, found_at):
            for s in range(4):
                b = 4 * c + s
                wanted = fb_owner_sm[gx, b] * 2048 + fb_cell_sm[gx, b]
                found_at = [jnp.where(gid_s[t] == wanted, b, found_at[t]) for t in range(TILES)]
            return found_at

        none = [jnp.full((GX, 128), -1, jnp.int32) for _ in range(TILES)]
        found_at = lax.fori_loop(0, 32, seek, none)
        table, total = slot_table(
            [f >= 0 for f in found_at], [f.astype(F32) for f in found_at], HITS, mark_s, value_s
        )
        tabs_ref[PARENTS : PARENTS + GX, :] = table.astype(jnp.int32)
        over = jnp.maximum(
            over,
            jnp.max(jnp.where(total > float(HITS), 1.0, 0.0), axis=0, keepdims=True),
        )

        fed = (fb_owner_ref[...] * 2048 + fb_cell_ref[...]).astype(F32)
        turned_s[...] = jnp.concatenate([fed, jnp.full((96, 128), -2.0, F32)], axis=0).T
        wide = [jnp.broadcast_to(t.astype(F32), (8, 128)) for t in terms]

        def match(q, from_block):
            column = pltpu.roll(turned_s[...], lax.rem(128 - q, 128), 1)[:, 0:1]
            for s in range(16):
                part = jnp.broadcast_to(column[8 * s : 8 * s + 8, :], (8, 128))
                from_block = [jnp.where(part == w, q, f) for w, f in zip(wide, from_block)]
            return from_block

        none = [jnp.full((8, 128), -1, jnp.int32) for _ in range(TILES)]
        from_block = lax.fori_loop(0, GX, match, none)
        sources = [jnp.max(f, axis=0, keepdims=True) for f in from_block]
        hots = [iota((GX, 128), 0) == s for s in sources]
        found, _ = ranks(hots)
        for t in range(TILES):
            slot = jnp.sum(jnp.where(hots[t], found[t], 0.0), axis=0, keepdims=True)
            slot = jnp.minimum(slot.astype(jnp.int32), HITS - 1)
            code = (PGROUPS + jnp.right_shift(sources[t], 4)) * 128
            code = code + jnp.bitwise_and(sources[t], 15) * HITS + slot
            tabs_ref[T2_ROW + t : T2_ROW + t + 1, :] = jnp.where(sources[t] >= 0, code, codes[t])

        base = flag_block(over)
        send_ref[...] = jnp.broadcast_to(base[None], (DEVICES, 8, 128))
        send_ref[PARENTS + lax.rem(gx + 1, GX)] = edge_block(x_ref, COLS - 1, base)
        send_ref[PARENTS + lax.rem(gx + GX - 1, GX)] = edge_block(x_ref, 0, base)


def second_kernel(
    recv_ref,
    x_ref,
    diff_ref,
    cor_ref,
    mix_ref,
    above_ref,
    below_ref,
    weight_ref,
    tabs_ref,
    fb_owner_ref,
    fb_cell_ref,
    out_ref,
    send_ref,
    flag_ref,
    map_ref,
    rows_s,
    group_s,
    cycle_s,
    weight_s,
):
    grp = lax.axis_index("grp")
    gx = lax.axis_index("gx")
    flag = recv_ref[0]
    for d in range(1, DEVICES):
        flag = jnp.maximum(flag, recv_ref[d])
    flag_ref[...] = flag
    update(x_ref, out_ref, recv_ref, above_ref, below_ref, diff_ref, cor_ref, mix_ref, grp, gx)

    @pl.when(grp < 3)
    def _():
        for r in range(ROWS):
            rows_s[r] = out_ref[:, r, :]
        send_cells(rows_s, tabs_ref, send_ref, None)
        feedback_map(fb_owner_ref, fb_cell_ref, map_ref, grp * GX + gx)

    @pl.when(grp == 3)
    def _():
        load_weights(weight_ref, weight_s, gx)
        regroup(recv_ref, 0, PGROUPS, 5, SLOTS, group_s, 0)
        interpolate(tabs_ref, T1_ROW, weight_s, group_s, PGROUPS, cycle_s)
        prescribe(out_ref, cycle_s, gx)
        coarse = coarsen(out_ref)
        send_coarse(coarse, tabs_ref, send_ref)
        blank = jnp.zeros((8, 128), F32)
        first = edge_block(out_ref, 0, blank)
        last = edge_block(out_ref, COLS - 1, blank)
        send_hits(coarse, tabs_ref, send_ref, blank)
        lane = iota((8, 128), 1)
        right = PARENTS + lax.rem(gx + 1, GX)
        left = PARENTS + lax.rem(gx + GX - 1, GX)
        send_ref[right] = jnp.where(lane < EDGE, send_ref[right], last)
        send_ref[left] = jnp.where(lane < EDGE, send_ref[left], first)


def third_kernel(
    recv_ref,
    x_ref,
    diff_ref,
    cor_ref,
    mix_ref,
    weight_ref,
    tabs_ref,
    map_ref,
    out_ref,
    send_ref,
    last_row_ref,
    first_row_ref,
    group_s,
    cycle_s,
    weight_s,
):
    grp = lax.axis_index("grp")
    gx = lax.axis_index("gx")

    @pl.when(grp < 3)
    def _():
        feed_back(x_ref, out_ref, recv_ref, map_ref, group_s)
        send_parent_edges(out_ref, send_ref, grp, gx, jnp.zeros((8, 128), F32))
        last_row_ref[...] = out_ref[:, ROWS - 1, :]
        first_row_ref[...] = out_ref[:, 0, :]

    @pl.when(grp == 3)
    def _():
        update(x_ref, out_ref, recv_ref, None, None, diff_ref, cor_ref, mix_ref, grp, gx)
        load_weights(weight_ref, weight_s, gx)
        regroup(recv_ref, 0, PGROUPS, 5, SLOTS, group_s, 0)
        regroup(recv_ref, PARENTS, 2, 16, HITS, group_s, PGROUPS)
        interpolate(tabs_ref, T2_ROW, weight_s, group_s, GROUPS, cycle_s)
        prescribe(out_ref, cycle_s, gx)
        send_coarse(coarsen(out_ref), tabs_ref, send_ref)


def fourth_kernel(
    recv_ref,
    x_ref,
    diff_ref,
    cor_ref,
    mix_ref,
    above_ref,
    below_ref,
    map_ref,
    out_ref,
    group_s,
):
    grp = lax.axis_index("grp")
    gx = lax.axis_index("gx")

    @pl.when(grp < 3)
    def _():
        update(x_ref, out_ref, recv_ref, above_ref, below_ref, diff_ref, cor_ref, mix_ref, grp, gx)
        feed_back(out_ref, out_ref, recv_ref, map_ref, group_s)

    @pl.when(grp == 3)
    def _():
        out_ref[...] = x_ref[...]


def call(kernel, name, ins, spaces, outs, scratch):
    return pl.pallas_call(
        kernel,
        name=name,
        in_specs=[
            pl.BlockSpec(memory_space=pltpu.SMEM if s == "s" else pltpu.VMEM) for s in spaces
        ],
        out_specs=[pl.BlockSpec(memory_space=pltpu.VMEM) for _ in outs],
        out_shape=[jax.ShapeDtypeStruct(s, d) for s, d in outs],
        scratch_shapes=[pltpu.VMEM(s, d) for s, d in scratch],
        compiler_params=pltpu.CompilerParams(vmem_limit_bytes=VMEM_LIMIT),
    )(*ins)


STATE = ((LANES, ROWS, COLS), F32)
BLOCKS = ((DEVICES, 8, 128), F32)
RIM = ((LANES, COLS), F32)
ROWMAJOR = ((ROWS, LANES, COLS), F32)
GROUPED = ((GROUPS, LANES, 128), F32)
CYCLE = ((3, LANES, 128), F32)
WEIGHTS = ((16, 128), F32)
TABS = ((TAB_ROWS, 128), jnp.int32)
MAP = ((ROWS, 128), jnp.int32)
TERMS = ((TILES, GX, 128), F32)


def exchange(blocks):
    return lax.all_to_all(blocks, ("grp", "gx"), 0, 0, tiled=True)


def rims(last_row, first_row):
    above = lax.ppermute(last_row, "grp", [(0, 1), (1, 2)])
    below = lax.ppermute(first_row, "grp", [(1, 0), (2, 1)])
    return above, below


def shards(atmosphere, diffusion, coriolis, mixing, owner, cell, weight, fb_owner, fb_cell):
    send, tabs, last_row, first_row = call(
        first_kernel,
        "tables",
        (atmosphere, owner, cell, fb_owner, fb_cell, fb_owner, fb_cell),
        "vvvvvss",
        (BLOCKS, TABS, RIM, RIM),
        (((TILES, GX, 128), jnp.int32), TERMS, TERMS, ROWMAJOR, ((128, 128), F32)),
    )
    above, below = rims(last_row, first_row)
    recv = exchange(send)
    state, send, flag, place = call(
        second_kernel,
        "substep_one",
        (recv, atmosphere, diffusion, coriolis, mixing, above, below, weight, tabs, fb_owner, fb_cell),
        "vvvssvvvvvv",
        (STATE, BLOCKS, ((8, 128), F32), MAP),
        (ROWMAJOR, GROUPED, CYCLE, WEIGHTS),
    )
    recv = exchange(send)
    state, send, last_row, first_row = call(
        third_kernel,
        "substep_two",
        (recv, state, diffusion, coriolis, mixing, weight, tabs, place),
        "vvvssvvv",
        (STATE, BLOCKS, RIM, RIM),
        (GROUPED, CYCLE, WEIGHTS),
    )
    above, below = rims(last_row, first_row)
    recv = exchange(send)
    (state,) = call(
        fourth_kernel,
        "finish",
        (recv, state, diffusion, coriolis, mixing, above, below, place),
        "vvvssvvv",
        (STATE,),
        (GROUPED,),
    )
    inputs = (atmosphere, diffusion, coriolis, mixing, owner, cell, weight, fb_owner, fb_cell)
    return lax.cond(flag[0, 127] > 0.5, lambda s, *a: dense_plan(*a), lambda s, *a: s, state, *inputs)


def solution(mesh):
    placed = (P(None, "grp", "gx"), P("grp", "gx"), P("grp"), P(), P(), P(), P(), P(), P())
    return jax.shard_map(
        shards, mesh=mesh, in_specs=placed, out_specs=P(None, "grp", "gx"), check_vma=False
    )
```

```python
import jax
import jax.numpy as jnp
from jax import lax
from jax.experimental import pallas as pl
from jax.experimental.pallas import tpu as pltpu
from jax.sharding import PartitionSpec as P

SUBSTEPS = 2
F32 = jnp.float32
LANES = 40
ROWS = 16
COLS = 128
LEVELS = 10
GX = 32
PARENTS = 96
DEVICES = 128
PERIM = 288
TILES = 9
SLOTS = 25
HITS = 8
EDGE = 40
FG = 5
T1_ROW = 128
TAB_ROWS = 144
PGROUPS = 20
GROUPS = 22
VMEM_LIMIT = 48 * 1024 * 1024


def padded(cells, sides, width):
    for axis, dim in sides:
        count = lax.axis_size(axis)
        head = lax.slice_in_dim(cells, 0, width, axis=dim)
        tail = lax.slice_in_dim(cells, cells.shape[dim] - width, cells.shape[dim], axis=dim)
        cells = jnp.concatenate(
            [
                lax.ppermute(tail, axis, [(i, (i + 1) % count) for i in range(count)]),
                cells,
                lax.ppermute(head, axis, [((i + 1) % count, i) for i in range(count)]),
            ],
            axis=dim,
        )
    return cells


def broadcast(value, axis, source):
    kept = jnp.where(lax.axis_index(axis) == source, value, 0).astype(value.dtype)
    for other in range(lax.axis_size(axis)):
        if other != source:
            kept = kept + lax.ppermute(jnp.where(lax.axis_index(axis) == source, value, 0), axis, [(source, other)])
    return kept


def gather_columns(value, axis):
    count = lax.axis_size(axis)
    copies = jnp.broadcast_to(value[None], (count,) + value.shape)
    blocks = lax.all_to_all(copies, axis, 0, 0, tiled=True)
    return blocks.transpose(1, 0, 2).reshape(value.shape[0], -1)


def reduce_cycle(terms, column_count, group_count):
    blocks = terms.reshape(terms.shape[0], column_count, -1).transpose(1, 0, 2)
    partial = lax.all_to_all(blocks, "gx", 0, 0, tiled=True).sum(axis=0)
    total = partial
    for group in range(group_count - 1):
        total = total + lax.ppermute(partial, "grp", [(group, group_count - 1)])
    return total


def advance(extended, center, diffusion, coriolis, mixing):
    neighbours = (
        extended[:, 1:-1, :-2]
        + extended[:, 1:-1, 2:]
        + extended[:, :-2, 1:-1]
        + extended[:, 2:, 1:-1]
        + extended[:, :-2, 2:]
        + extended[:, 2:, :-2]
    )
    laplace = neighbours - 6.0 * center
    lane_count, row_count, col_count = center.shape
    level_count = mixing.shape[0]
    stacked = center.reshape(lane_count // level_count, level_count, row_count, col_count)
    upper = jnp.concatenate([stacked[:, 1:], stacked[:, -1:]], axis=1)
    lower = jnp.concatenate([stacked[:, :1], stacked[:, :-1]], axis=1)
    vertical = mixing[None, :, None, None] * (upper - 2.0 * stacked + lower)
    rotation = jnp.concatenate(
        [
            (coriolis[:, None] * stacked[1])[None],
            (-coriolis[:, None] * stacked[0])[None],
            jnp.zeros_like(stacked[2:]),
        ],
        axis=0,
    )
    return center + diffusion * laplace + (vertical + rotation).reshape(center.shape)


def dense_plan(
    atmosphere,
    diffusion,
    coriolis,
    mixing,
    stencil_owner,
    stencil_cell,
    stencil_weight,
    feedback_owner,
    feedback_cell,
):
    lane_count, row_count, col_count = atmosphere.shape
    cell_count = row_count * col_count
    column_count = lax.axis_size("gx")
    group_count = lax.axis_size("grp")
    group_index = lax.axis_index("grp")
    column_index = lax.axis_index("gx")
    own_rank = group_index * column_count + column_index
    is_nested = group_index == group_count - 1
    perimeter = stencil_owner.shape[2]
    owner_flat = feedback_owner.reshape(-1)
    target_flat = feedback_cell.reshape(-1)
    current = atmosphere
    for substep in range(SUBSTEPS):
        flat_now = current.reshape(lane_count, cell_count)
        cycle_terms = jnp.zeros((lane_count, column_count * perimeter), jnp.float32)
        for member in range(stencil_owner.shape[1]):
            mine = stencil_owner[:, member, :].reshape(-1) == own_rank
            positions = jnp.where(mine, stencil_cell[:, member, :].reshape(-1), 0)
            weights = jnp.where(mine, stencil_weight[:, member, :].reshape(-1), 0.0)
            cycle_terms = cycle_terms + jnp.take(flat_now, positions, axis=1) * weights
        cycle = reduce_cycle(cycle_terms, column_count, group_count)
        extended = padded(current, (("grp", 1), ("gx", 2)), 1)
        upper_rim = jnp.where(group_index == 0, extended[:, 1:2, :], extended[:, 0:1, :])
        lower_rim = jnp.where(
            group_index == group_count - 2, extended[:, -2:-1, :], extended[:, -1:, :]
        )
        extended = jnp.concatenate([upper_rim, extended[:, 1:-1, :], lower_rim], axis=1)
        fresh = advance(extended, current, diffusion, coriolis, mixing)
        left_edge = jnp.where(
            column_index == 0, cycle[:, 2 * col_count : 2 * col_count + row_count], fresh[:, :, 0]
        )
        right_edge = jnp.where(
            column_index == column_count - 1, cycle[:, 2 * col_count + row_count :], fresh[:, :, -1]
        )
        framed = fresh.at[:, :, 0].set(left_edge).at[:, :, -1].set(right_edge)
        framed = (
            framed.at[:, 0, :]
            .set(cycle[:, :col_count])
            .at[:, -1, :]
            .set(cycle[:, col_count : 2 * col_count])
        )
        fresh = jnp.where(is_nested, framed, fresh)
        coarse = fresh.reshape(lane_count, row_count // 4, 4, col_count // 4, 4).mean(axis=(2, 4))
        coarse = coarse.reshape(lane_count, -1)
        fresh_flat = fresh.reshape(lane_count, cell_count)
        shared = broadcast(coarse, "grp", group_count - 1)
        place_positions = jnp.where(owner_flat == own_rank, target_flat, cell_count)
        result_flat = fresh_flat.at[:, place_positions].set(
            gather_columns(shared, "gx"), mode="drop"
        )
        current = result_flat.reshape(lane_count, row_count, col_count)
    return current


def iota(shape, dim):
    return lax.broadcasted_iota(jnp.int32, shape, dim)


def chunks(count, step, body):
    def run(c, carry):
        for s in range(step):
            body(c * step + s)
        return carry

    lax.fori_loop(0, count // step, run, 0)


def take(tile, index):
    return jnp.take_along_axis(tile, index, axis=1, mode="promise_in_bounds")


def ranks(masks):
    rows = masks[0].shape[0]
    stacked = jnp.concatenate([jnp.where(m, 1.0, 0.0) for m in masks], axis=0)
    stacked = stacked.astype(jnp.bfloat16)
    before = jnp.where(iota((128, 128), 0) < iota((128, 128), 1), 1.0, 0.0).astype(jnp.bfloat16)
    ones = jnp.ones((128, 128), jnp.bfloat16)
    within = jnp.dot(stacked, before, preferred_element_type=F32)
    totals = jnp.dot(stacked, ones, preferred_element_type=F32)
    carry = jnp.zeros((rows, 128), F32)
    found = []
    for t in range(len(masks)):
        found.append(within[t * rows : (t + 1) * rows] + carry)
        carry = carry + totals[t * rows : (t + 1) * rows]
    return found, carry


def slot_table(masks, values, slots, mark_s, value_s):
    found, total = ranks(masks)
    for t in range(TILES):
        mark_s[t] = jnp.where(masks[t], found[t], -1.0)
        value_s[t] = values[t]
    slot_of = lax.rem(iota((8, 128), 1), slots)
    parts = []
    for part in range(GX // 8):
        span = slice(8 * part, 8 * part + 8)
        marks = [mark_s[t, span, :] for t in range(TILES)]
        vals = [value_s[t, span, :] for t in range(TILES)]
        table = jnp.zeros((8, 128), F32)
        for j in range(slots):
            picked = [jnp.where(m == float(j), v, 0.0) for m, v in zip(marks, vals)]
            while len(picked) > 1:
                picked = [sum(picked[k : k + 2]) for k in range(0, len(picked), 2)]
            table = jnp.where(slot_of == j, jnp.sum(picked[0], axis=1, keepdims=True), table)
        parts.append(table)
    return jnp.concatenate(parts, axis=0), total


def send_cells(rows_s, table_ref, send_ref, flag):
    lane = iota((8, 128), 1)
    group_of = lane // SLOTS
    table = table_ref[0:GX, :]
    for g in range(7):
        index = jnp.zeros((1, 128), jnp.int32)
        members = [q for q in range(5 * g, 5 * g + 5) if q < GX]
        for q in members:
            index = jnp.where(group_of[0:1] == q - 5 * g, table[q : q + 1, :], index)
        index = jnp.broadcast_to(index, (8, 128))
        col = jnp.bitwise_and(index, 127)
        row = jnp.right_shift(index, 7)
        cells = [jnp.zeros((8, 128), F32) for _ in range(FG)]
        for r in range(ROWS):
            here = row == r
            for k in range(FG):
                cells[k] = jnp.where(here, take(rows_s[r, 8 * k : 8 * k + 8, :], col), cells[k])
        for q in members:
            block = jnp.zeros((8, 128), F32) if flag is None else flag
            for k in range(FG):
                shift = (SLOTS * (k - (q - 5 * g))) % 128
                moved = cells[k] if shift == 0 else pltpu.roll(cells[k], shift, 1)
                block = jnp.where(group_of == k, moved, block)
            send_ref[PARENTS + q] = block


def edge_block(x_ref, col, base):
    lane = iota((8, 128), 1)
    block = base
    for h in range(2):
        for f in range(LANES):
            edge = x_ref[f, 8 * h : 8 * h + 8, col : col + 1]
            block = jnp.where(lane == EDGE + h * LANES + f, edge, block)
    return block


def send_parent_edges(x_ref, send_ref, grp, gx, base):
    first = edge_block(x_ref, 0, base)
    last = edge_block(x_ref, COLS - 1, base)
    right = lax.rem(gx + 1, GX)
    left = lax.rem(gx + GX - 1, GX)
    send_ref[grp * GX + right] = last
    send_ref[grp * GX + left] = first

    @pl.when(grp > 0)
    def _():
        send_ref[(grp - 1) * GX + right] = last

    @pl.when(grp < 2)
    def _():
        send_ref[(grp + 1) * GX + left] = first


def unpack_edge(block):
    return jnp.concatenate([block, pltpu.roll(block, 128 - LANES, 1)], axis=0)


def update(x_ref, out_ref, diff_ref, cor_ref, mix_ref):
    lane = iota((ROWS, COLS), 1)
    row = iota((ROWS, COLS), 0)
    diff = diff_ref[...]
    cor = jnp.zeros((ROWS, COLS), F32)
    for r in range(ROWS):
        cor = jnp.where(row == r, cor_ref[r], cor)
    for f in range(LANES):
        level = f % LEVELS
        x = x_ref[f]
        up = jnp.where(row == 0, 0.0, pltpu.roll(x, 1, 0))
        down = jnp.where(row == ROWS - 1, 0.0, pltpu.roll(x, ROWS - 1, 0))
        westward = jnp.where(lane == 0, 0.0, pltpu.roll(x + down, 1, 1))
        eastward = jnp.where(lane == COLS - 1, 0.0, pltpu.roll(x + up, COLS - 1, 1))
        laplace = (westward + eastward) + (up + down) - 6.0 * x
        upper = x if level == LEVELS - 1 else x_ref[f + 1]
        lower = x if level == 0 else x_ref[f - 1]
        extra = mix_ref[level] * (upper - 2.0 * x + lower)
        if f < LEVELS:
            extra = extra + cor * x_ref[f + LEVELS]
        elif f < 2 * LEVELS:
            extra = extra - cor * x_ref[f - LEVELS]
        out_ref[f] = x + diff * laplace + extra


def add_columns(from_ref, out_ref, recv_ref, diff_ref, grp, gx):
    nest = grp == 3
    right = lax.rem(gx + 1, GX)
    left = lax.rem(gx + GX - 1, GX)
    lane = iota((ROWS, COLS), 1)
    row = iota((ROWS, COLS), 0)
    from_left = unpack_edge(recv_ref[grp * GX + left])
    from_right = unpack_edge(recv_ref[grp * GX + right])
    top_right = unpack_edge(recv_ref[jnp.maximum(grp - 1, 0) * GX + right])[ROWS - 1 : ROWS]
    low_left = unpack_edge(recv_ref[jnp.minimum(grp + 1, 3) * GX + left])[0:1]
    top_right = jnp.where(grp == 0, from_right[0:1], top_right)
    low_left = jnp.where(grp == 2, from_left[ROWS - 1 : ROWS], low_left)
    top_right = jnp.where(nest, 0.0, top_right)
    low_left = jnp.where(nest, 0.0, low_left)
    left_sum = from_left + jnp.where(row == ROWS - 1, low_left, pltpu.roll(from_left, ROWS - 1, 0))
    right_sum = from_right + jnp.where(row == 0, top_right, pltpu.roll(from_right, 1, 0))
    left_sum = jnp.where(jnp.logical_and(nest, gx == 0), 0.0, left_sum)
    right_sum = jnp.where(jnp.logical_and(nest, gx == GX - 1), 0.0, right_sum)
    diff = diff_ref[...]
    left_sum = left_sum * diff[:, 0:1]
    right_sum = right_sum * diff[:, COLS - 1 : COLS]
    source = jnp.bitwise_and(EDGE + jnp.right_shift(lane + 1, 1), 127)
    spread = jnp.concatenate(
        [
            jnp.where(
                jnp.bitwise_and(lane[0:8], 1) == 0,
                take(left_sum[h : h + 8], source[0:8]),
                take(right_sum[h : h + 8], jnp.where(lane[0:8] == 127, EDGE, source[0:8])),
            )
            for h in (0, 8)
        ],
        axis=0,
    )
    outer = jnp.logical_or(lane == 0, lane == COLS - 1)
    for f in range(LANES):
        moved = spread if f == 0 else pltpu.roll(spread, 128 - 2 * f, 1)
        out_ref[f] = from_ref[f] + jnp.where(outer, moved, 0.0)


def add_rows(x_ref, out_ref, above_ref, below_ref, diff_ref, grp):
    lane = iota((LANES, COLS), 1)
    above = jnp.where(grp == 0, x_ref[:, 0, :], above_ref[...])
    below = jnp.where(grp == 2, x_ref[:, ROWS - 1, :], below_ref[...])
    above = above + jnp.where(lane == COLS - 1, 0.0, pltpu.roll(above, COLS - 1, 1))
    below = below + jnp.where(lane == 0, 0.0, pltpu.roll(below, 1, 1))
    out_ref[:, 0, :] = out_ref[:, 0, :] + diff_ref[0:1, :] * above
    out_ref[:, ROWS - 1, :] = out_ref[:, ROWS - 1, :] + diff_ref[ROWS - 1 : ROWS, :] * below


def regroup(recv_ref, base, groups, per, width, group_s, first):
    lane = iota((8, 128), 1)
    member_of = lane // width

    def body(g):
        tiles = [jnp.zeros((8, 128), F32) for _ in range(FG)]
        for i in range(per):
            block = recv_ref[jnp.minimum(base + g * per + i, DEVICES - 1)]
            for k in range(FG):
                shift = (width * (i - k)) % 128
                moved = block if shift == 0 else pltpu.roll(block, shift, 1)
                tiles[k] = jnp.where(member_of == i, moved, tiles[k])
        for k in range(FG):
            group_s[first + g, 8 * k : 8 * k + 8, :] = tiles[k]

    chunks(groups, 2 if groups % 2 == 0 else 1, body)


def interpolate(tabs_ref, first_row, weight_s, group_s, groups, cycle_s):
    cycle_s[...] = jnp.zeros((3, LANES, 128), F32)

    def body(t):
        code = jnp.broadcast_to(tabs_ref[pl.ds(first_row + t, 1), :], (8, 128))
        index = jnp.bitwise_and(code, 127)
        group = jnp.right_shift(code, 7)
        cells = [jnp.zeros((8, 128), F32) for _ in range(FG)]
        for g in range(groups):
            here = group == g
            for k in range(FG):
                cells[k] = jnp.where(here, take(group_s[g, 8 * k : 8 * k + 8, :], index), cells[k])
        weight = weight_s[pl.ds(t, 1), :]
        span = lax.rem(t, 3)
        for k in range(FG):
            cycle_s[span, 8 * k : 8 * k + 8, :] += weight * cells[k]

    chunks(TILES, 1, body)


def load_weights(weight_ref, weight_s, gx):
    weight_s[...] = jnp.zeros((16, 128), F32)
    for k in range(3):
        own = weight_ref[k, pl.ds(gx, 1), :]
        weight_s[3 * k : 3 * k + 1, :] = own[:, 0:128]
        weight_s[3 * k + 1 : 3 * k + 2, :] = own[:, 128:256]
        weight_s[3 * k + 2 : 3 * k + 3, 0:32] = own[:, 256:288]


def prescribe(out_ref, cycle_s, gx):
    lane = iota((ROWS, COLS), 1)

    @pl.when(jnp.logical_or(gx == 0, gx == GX - 1))
    def _():
        turned = jnp.concatenate([cycle_s[2], jnp.zeros((88, 128), F32)], axis=0).T
        column = jnp.where(gx == 0, turned[0:ROWS, :], turned[ROWS : 2 * ROWS, :])
        at = jnp.where(gx == 0, 0, COLS - 1)
        for f in range(LANES):
            out_ref[f] = jnp.where(lane == at, column[:, f : f + 1], out_ref[f])

    out_ref[:, 0, :] = cycle_s[0]
    out_ref[:, ROWS - 1, :] = cycle_s[1]


def coarsen(out_ref):
    coarse = jnp.zeros((LANES, 128), F32)
    for i in range(4):
        total = (out_ref[:, 4 * i, :] + out_ref[:, 4 * i + 1, :]) + (
            out_ref[:, 4 * i + 2, :] + out_ref[:, 4 * i + 3, :]
        )
        mean = jnp.where(iota((128, 128), 1) == 32 * i + iota((128, 128), 0) // 4, 1.0 / 16.0, 0.0)
        coarse = coarse + jnp.dot(
            total, mean, precision=lax.Precision.HIGHEST, preferred_element_type=F32
        )
    return coarse


def send_coarse(coarse, tabs_ref, send_ref, base):
    lane = iota((8, 128), 1)
    group_of = lane // SLOTS

    def body(o):
        index = jnp.broadcast_to(tabs_ref[pl.ds(o, 1), :], (8, 128))
        block = base
        for k in range(FG):
            block = jnp.where(group_of == k, take(coarse[8 * k : 8 * k + 8], index), block)
        send_ref[o] = block

    chunks(PARENTS, 8, body)


def send_hits(coarse, tabs_ref, send_ref, base):
    group_of = iota((8, 128), 1) // HITS

    def body(q):
        index = jnp.broadcast_to(tabs_ref[pl.ds(PARENTS + q, 1), :], (8, 128))
        block = base
        for k in range(FG):
            block = jnp.where(group_of == k, take(coarse[8 * k : 8 * k + 8], index), block)
        send_ref[PARENTS + q] = block

    chunks(GX, 8, body)


def feed_back(src_ref, out_ref, recv_ref, map_ref, group_s):
    regroup(recv_ref, PARENTS, 7, 5, SLOTS, group_s, 0)
    for r in range(ROWS):
        code = jnp.broadcast_to(map_ref[r : r + 1, :], (8, 128))
        index = jnp.bitwise_and(code, 127)
        group = jnp.right_shift(code, 7)
        cells = [src_ref[8 * k : 8 * k + 8, r, :] for k in range(FG)]
        for g in range(7):
            here = group == g
            for k in range(FG):
                cells[k] = jnp.where(here, take(group_s[g, 8 * k : 8 * k + 8, :], index), cells[k])
        for k in range(FG):
            out_ref[8 * k : 8 * k + 8, r, :] = cells[k]


def feedback_map(owner_ref, cell_ref, map_ref, me):
    owner = owner_ref[...]
    cell = cell_ref[...]
    own = owner == me
    found, _ = ranks([own])
    slot = jnp.minimum(found[0], float(SLOTS - 1))
    row = jnp.where(own, jnp.right_shift(cell, 7), -1)
    col = jnp.bitwise_and(cell, 127)
    planes = jnp.zeros((2 * ROWS, 128), F32)
    for q in range(GX):
        here = iota((ROWS, 128), 0) == row[q : q + 1, :]
        codes = jnp.concatenate(
            [jnp.where(here, float(q + 1), 0.0), jnp.where(here, slot[q : q + 1, :], 0.0)], axis=0
        )
        hot = jnp.where(iota((128, 128), 0) == col[q : q + 1, :], 1.0, 0.0)
        planes = planes + lax.dot_general(
            codes.astype(jnp.bfloat16),
            hot.astype(jnp.bfloat16),
            (((1,), (1,)), ((), ())),
            preferred_element_type=F32,
        )
    block = planes[0:ROWS].astype(jnp.int32) - 1
    slots = planes[ROWS : 2 * ROWS].astype(jnp.int32)
    group = jnp.right_shift(block * 205, 10)
    code = group * 128 + (block - 5 * group) * SLOTS + slots
    map_ref[...] = jnp.where(block < 0, -1, code)


def load_terms(owner_ref, cell_ref, gid_s):
    for k in range(3):
        gid = owner_ref[k] * 2048 + cell_ref[k]
        gid_s[3 * k] = gid[:, 0:128]
        gid_s[3 * k + 1] = gid[:, 128:256]
        gid_s[3 * k + 2] = jnp.full((GX, 128), -1, jnp.int32)
        gid_s[3 * k + 2, :, 0:32] = gid[:, 256:288]


def flag_block(over):
    worst = jnp.max(over, axis=0, keepdims=True)
    flag = jnp.where(worst > 0.5, 1.0, 0.0)
    return jnp.where(iota((8, 128), 1) == 127, jnp.broadcast_to(flag, (8, 128)), 0.0)


def first_kernel(
    x_ref, owner_ref, cell_ref, send_ref, table_ref, flag_ref, last_row_ref, first_row_ref,
    gid_s, mark_s, value_s, rows_s,
):
    grp = lax.axis_index("grp")
    gx = lax.axis_index("gx")
    blank = jnp.zeros((8, 128), F32)
    last_row_ref[...] = x_ref[:, ROWS - 1, :]
    first_row_ref[...] = x_ref[:, 0, :]

    @pl.when(grp < 3)
    def _():
        load_terms(owner_ref, cell_ref, gid_s)
        gids = [gid_s[t] for t in range(TILES)]
        masks = [jnp.right_shift(g, 11) == grp * GX + gx for g in gids]
        values = [jnp.bitwise_and(g, 2047).astype(F32) for g in gids]
        table, total = slot_table(masks, values, SLOTS, mark_s, value_s)
        table_ref[...] = table.astype(jnp.int32)
        flag_ref[...] = flag_block(jnp.where(total > float(SLOTS), 1.0, 0.0))
        for r in range(ROWS):
            rows_s[r] = x_ref[:, r, :]
        send_cells(rows_s, table_ref, send_ref, None)
        send_parent_edges(x_ref, send_ref, grp, gx, blank)

    @pl.when(grp == 3)
    def _():
        send_ref[PARENTS + lax.rem(gx + 1, GX)] = edge_block(x_ref, COLS - 1, blank)
        send_ref[PARENTS + lax.rem(gx + GX - 1, GX)] = edge_block(x_ref, 0, blank)


def tables_kernel(
    x_ref, diff_ref, cor_ref, mix_ref, owner_ref, cell_ref, fb_owner_ref, fb_cell_ref,
    fb_owner_sm, fb_cell_sm, flag_in_ref, fresh_ref, tabs_ref, flag_ref, map_ref,
    gid_s, mark_s, value_s,
):
    grp = lax.axis_index("grp")
    gx = lax.axis_index("gx")
    update(x_ref, fresh_ref, diff_ref, cor_ref, mix_ref)

    @pl.when(grp < 3)
    def _():
        flag_ref[...] = flag_in_ref[...]
        feedback_map(fb_owner_ref, fb_cell_ref, map_ref, grp * GX + gx)

    @pl.when(grp == 3)
    def _():
        load_terms(owner_ref, cell_ref, gid_s)
        own = fb_owner_ref[pl.ds(gx, 1), :]
        hot = iota((PARENTS, 128), 0) == own
        found, total = ranks([hot])
        over = jnp.max(jnp.where(total > float(SLOTS), 1.0, 0.0), axis=0, keepdims=True)
        rank = jnp.sum(jnp.where(hot, found[0], 0.0), axis=0, keepdims=True)
        slot_of = lax.rem(iota((128, 128), 0), SLOTS).astype(F32)
        chosen = jnp.where(slot_of == rank, iota((128, 128), 1).astype(F32), 0.0)
        table = lax.dot_general(
            jnp.where(hot, 1.0, 0.0).astype(jnp.bfloat16),
            chosen.astype(jnp.bfloat16),
            (((1,), (1,)), ((), ())),
            preferred_element_type=F32,
        )
        tabs_ref[0:PARENTS, :] = table.astype(jnp.int32)

        owners = [jnp.right_shift(gid_s[t, pl.ds(gx, 1), :], 11) for t in range(TILES)]
        hots = [iota((PARENTS, 128), 0) == o for o in owners]
        found, _ = ranks(hots)
        for t in range(TILES):
            slot = jnp.sum(jnp.where(hots[t], found[t], 0.0), axis=0, keepdims=True)
            slot = jnp.minimum(slot.astype(jnp.int32), SLOTS - 1)
            group = jnp.right_shift(owners[t] * 205, 10)
            code = group * 128 + (owners[t] - 5 * group) * SLOTS + slot
            tabs_ref[T1_ROW + t : T1_ROW + t + 1, :] = code

        def seek(c, found_at):
            for s in range(4):
                b = 4 * c + s
                wanted = fb_owner_sm[gx, b] * 2048 + fb_cell_sm[gx, b]
                found_at = [jnp.where(gid_s[t] == wanted, b, found_at[t]) for t in range(TILES)]
            return found_at

        none = [jnp.full((GX, 128), -1, jnp.int32) for _ in range(TILES)]
        found_at = lax.fori_loop(0, 32, seek, none)
        table, total = slot_table(
            [f >= 0 for f in found_at], [f.astype(F32) for f in found_at], HITS, mark_s, value_s
        )
        tabs_ref[PARENTS : PARENTS + GX, :] = table.astype(jnp.int32)
        over = jnp.maximum(
            over, jnp.max(jnp.where(total > float(HITS), 1.0, 0.0), axis=0, keepdims=True)
        )
        flag_ref[...] = flag_block(over)


def second_kernel(
    recv_ref, x_ref, fresh_ref, diff_ref, above_ref, below_ref, weight_ref, table_ref, tabs_ref,
    flag_ref, out_ref, send_ref, rows_s, group_s, cycle_s, weight_s,
):
    grp = lax.axis_index("grp")
    gx = lax.axis_index("gx")
    add_columns(fresh_ref, out_ref, recv_ref, diff_ref, grp, gx)
    base = flag_ref[...]

    @pl.when(grp < 3)
    def _():
        add_rows(x_ref, out_ref, above_ref, below_ref, diff_ref, grp)
        for r in range(ROWS):
            rows_s[r] = out_ref[:, r, :]
        for d in range(PARENTS):
            send_ref[d] = base
        send_cells(rows_s, table_ref, send_ref, base)

    @pl.when(grp == 3)
    def _():
        load_weights(weight_ref, weight_s, gx)
        regroup(recv_ref, 0, PGROUPS, 5, SLOTS, group_s, 0)
        interpolate(tabs_ref, T1_ROW, weight_s, group_s, PGROUPS, cycle_s)
        prescribe(out_ref, cycle_s, gx)
        coarse = coarsen(out_ref)
        send_coarse(coarse, tabs_ref, send_ref, base)
        first = edge_block(out_ref, 0, base)
        last = edge_block(out_ref, COLS - 1, base)
        send_hits(coarse, tabs_ref, send_ref, base)
        lane = iota((8, 128), 1)
        right = PARENTS + lax.rem(gx + 1, GX)
        left = PARENTS + lax.rem(gx + GX - 1, GX)
        send_ref[right] = jnp.where(lane < EDGE, send_ref[right], last)
        send_ref[left] = jnp.where(lane < EDGE, send_ref[left], first)


def hits_kernel(
    x_ref, diff_ref, cor_ref, mix_ref, owner_ref, cell_ref, fb_owner_ref, fb_cell_ref, tabs_ref,
    fresh_ref, codes_ref, gid_s, turned_s,
):
    gx = lax.axis_index("gx")

    @pl.when(lax.axis_index("grp") == 3)
    def _():
        update(x_ref, fresh_ref, diff_ref, cor_ref, mix_ref)
        load_terms(owner_ref, cell_ref, gid_s)
        terms = [gid_s[t, pl.ds(gx, 1), :] for t in range(TILES)]
        fed = (fb_owner_ref[...] * 2048 + fb_cell_ref[...]).astype(F32)
        turned_s[...] = jnp.concatenate([fed, jnp.full((96, 128), -2.0, F32)], axis=0).T
        wide = [jnp.broadcast_to(t.astype(F32), (8, 128)) for t in terms]

        def match(q, from_block):
            column = pltpu.roll(turned_s[...], lax.rem(128 - q, 128), 1)[:, 0:1]
            for s in range(16):
                part = jnp.broadcast_to(column[8 * s : 8 * s + 8, :], (8, 128))
                from_block = [jnp.where(part == w, q, f) for w, f in zip(wide, from_block)]
            return from_block

        none = [jnp.full((8, 128), -1, jnp.int32) for _ in range(TILES)]
        from_block = lax.fori_loop(0, GX, match, none)
        sources = [jnp.max(f, axis=0, keepdims=True) for f in from_block]
        hots = [iota((GX, 128), 0) == s for s in sources]
        found, _ = ranks(hots)
        for t in range(TILES):
            slot = jnp.sum(jnp.where(hots[t], found[t], 0.0), axis=0, keepdims=True)
            slot = jnp.minimum(slot.astype(jnp.int32), HITS - 1)
            code = (PGROUPS + jnp.right_shift(sources[t], 4)) * 128
            code = code + jnp.bitwise_and(sources[t], 15) * HITS + slot
            plain = tabs_ref[T1_ROW + t : T1_ROW + t + 1, :]
            codes_ref[t : t + 1, :] = jnp.where(sources[t] >= 0, code, plain)


def third_kernel(
    recv_ref, x_ref, fresh_ref, diff_ref, weight_ref, tabs_ref, codes_ref, map_ref,
    out_ref, send_ref, flag_ref, last_row_ref, first_row_ref, group_s, cycle_s, weight_s,
):
    grp = lax.axis_index("grp")
    gx = lax.axis_index("gx")
    blank = jnp.zeros((8, 128), F32)
    flag = recv_ref[0]
    for d in range(1, DEVICES):
        flag = jnp.maximum(flag, recv_ref[d])
    flag_ref[...] = flag

    @pl.when(grp < 3)
    def _():
        feed_back(x_ref, out_ref, recv_ref, map_ref, group_s)
        send_parent_edges(out_ref, send_ref, grp, gx, blank)
        last_row_ref[...] = out_ref[:, ROWS - 1, :]
        first_row_ref[...] = out_ref[:, 0, :]

    @pl.when(grp == 3)
    def _():
        add_columns(fresh_ref, out_ref, recv_ref, diff_ref, grp, gx)
        load_weights(weight_ref, weight_s, gx)
        regroup(recv_ref, 0, PGROUPS, 5, SLOTS, group_s, 0)
        regroup(recv_ref, PARENTS, 2, 16, HITS, group_s, PGROUPS)
        interpolate(codes_ref, 0, weight_s, group_s, GROUPS, cycle_s)
        prescribe(out_ref, cycle_s, gx)
        send_coarse(coarsen(out_ref), tabs_ref, send_ref, blank)


def parents_kernel(x_ref, diff_ref, cor_ref, mix_ref, fresh_ref):
    @pl.when(lax.axis_index("grp") < 3)
    def _():
        update(x_ref, fresh_ref, diff_ref, cor_ref, mix_ref)


def fourth_kernel(
    recv_ref, x_ref, fresh_ref, diff_ref, above_ref, below_ref, map_ref, out_ref, group_s
):
    grp = lax.axis_index("grp")
    gx = lax.axis_index("gx")

    @pl.when(grp < 3)
    def _():
        add_columns(fresh_ref, out_ref, recv_ref, diff_ref, grp, gx)
        add_rows(x_ref, out_ref, above_ref, below_ref, diff_ref, grp)
        feed_back(out_ref, out_ref, recv_ref, map_ref, group_s)

    @pl.when(grp == 3)
    def _():
        out_ref[...] = x_ref[...]


def call(kernel, name, ins, spaces, outs, scratch, flops=1000000):
    return pl.pallas_call(
        kernel,
        name=name,
        in_specs=[
            pl.BlockSpec(memory_space=pltpu.SMEM if s == "s" else pltpu.VMEM) for s in spaces
        ],
        out_specs=[pl.BlockSpec(memory_space=pltpu.VMEM) for _ in outs],
        out_shape=[jax.ShapeDtypeStruct(s, d) for s, d in outs],
        scratch_shapes=[pltpu.VMEM(s, d) for s, d in scratch],
        compiler_params=pltpu.CompilerParams(vmem_limit_bytes=VMEM_LIMIT),
        cost_estimate=pl.CostEstimate(flops=flops, bytes_accessed=4000000, transcendentals=0),
    )(*ins)


STATE = ((LANES, ROWS, COLS), F32)
BLOCKS = ((DEVICES, 8, 128), F32)
RIM = ((LANES, COLS), F32)
ROWMAJOR = ((ROWS, LANES, COLS), F32)
GROUPED = ((GROUPS, LANES, 128), F32)
CYCLE = ((3, LANES, 128), F32)
WEIGHTS = ((16, 128), F32)
TABS = ((TAB_ROWS, 128), jnp.int32)
TABLE = ((GX, 128), jnp.int32)
CODES = ((16, 128), jnp.int32)
BLOCK = ((8, 128), F32)
GIDS = ((TILES, GX, 128), jnp.int32)
MAP = ((ROWS, 128), jnp.int32)
TERMS = ((TILES, GX, 128), F32)


def exchange(blocks):
    return lax.all_to_all(blocks, ("grp", "gx"), 0, 0, tiled=True)


def rims(last_row, first_row):
    above = lax.ppermute(last_row, "grp", [(0, 1), (1, 2)])
    below = lax.ppermute(first_row, "grp", [(1, 0), (2, 1)])
    return above, below


def shards(atmosphere, diffusion, coriolis, mixing, owner, cell, weight, fb_owner, fb_cell):
    inputs = (atmosphere, diffusion, coriolis, mixing, owner, cell, weight, fb_owner, fb_cell)
    owner, cell, weight = (jnp.transpose(a, (1, 0, 2)) for a in (owner, cell, weight))
    physics = (diffusion, coriolis, mixing)
    send, table, flag, last_row, first_row = call(
        first_kernel,
        "first_cells",
        (atmosphere, owner, cell),
        "vvv",
        (BLOCKS, TABLE, BLOCK, RIM, RIM),
        (GIDS, TERMS, TERMS, ROWMAJOR),
    )
    recv = exchange(send)
    above, below = rims(last_row, first_row)
    fresh, tabs, flag, place = call(
        tables_kernel,
        "tables",
        (atmosphere,) + physics + (owner, cell, fb_owner, fb_cell, fb_owner, fb_cell, flag),
        "vvssvvvvssv",
        (STATE, TABS, BLOCK, MAP),
        (GIDS, TERMS, TERMS),
    )
    state, send = call(
        second_kernel,
        "substep_one",
        (recv, atmosphere, fresh, diffusion, above, below, weight, table, tabs, flag),
        "vvvvvvvvvv",
        (STATE, BLOCKS),
        (ROWMAJOR, GROUPED, CYCLE, WEIGHTS),
    )
    recv = exchange(send)
    fresh, codes = call(
        hits_kernel,
        "hits",
        (state,) + physics + (owner, cell, fb_owner, fb_cell, tabs),
        "vvssvvvvv",
        (STATE, CODES),
        (GIDS, ((128, 128), F32)),
    )
    state, send, flag, last_row, first_row = call(
        third_kernel,
        "substep_two",
        (recv, state, fresh, diffusion, weight, tabs, codes, place),
        "vvvvvvvv",
        (STATE, BLOCKS, BLOCK, RIM, RIM),
        (GROUPED, CYCLE, WEIGHTS),
    )
    recv = exchange(send)
    above, below = rims(last_row, first_row)
    (fresh,) = call(parents_kernel, "parents", (state,) + physics, "vvss", (STATE,), ())
    (state,) = call(
        fourth_kernel,
        "finish",
        (recv, state, fresh, diffusion, above, below, place),
        "vvvvvvv",
        (STATE,),
        (GROUPED,),
    )
    return lax.cond(flag[0, 127] > 0.5, lambda s, *a: dense_plan(*a), lambda s, *a: s, state, *inputs)


def solution(mesh):
    placed = (P(None, "grp", "gx"), P("grp", "gx"), P("grp"), P(), P(), P(), P(), P(), P())
    return jax.shard_map(
        shards, mesh=mesh, in_specs=placed, out_specs=P(None, "grp", "gx"), check_vma=False
    )
```

```python
import jax
import jax.numpy as jnp
from jax import lax
from jax.experimental import pallas as pl
from jax.experimental.pallas import tpu as pltpu
from jax.sharding import PartitionSpec as P

SUBSTEPS = 2
F32 = jnp.float32
LANES = 40
ROWS = 16
COLS = 128
LEVELS = 10
GX = 32
PARENTS = 96
DEVICES = 128
PERIM = 288
TILES = 9
SLOTS = 25
HITS = 8
EDGE = 40
FG = 5
PGROUPS = 20
GROUPS = 22
ENTRIES = 128
PLANES = 2
MEANS = 8 * PLANES
SENT = PARENTS * 8
TAKEN = GX * 8
VMEM_LIMIT = 24 * 1024 * 1024


def padded(cells, sides, width):
    for axis, dim in sides:
        count = lax.axis_size(axis)
        head = lax.slice_in_dim(cells, 0, width, axis=dim)
        tail = lax.slice_in_dim(cells, cells.shape[dim] - width, cells.shape[dim], axis=dim)
        cells = jnp.concatenate(
            [
                lax.ppermute(tail, axis, [(i, (i + 1) % count) for i in range(count)]),
                cells,
                lax.ppermute(head, axis, [((i + 1) % count, i) for i in range(count)]),
            ],
            axis=dim,
        )
    return cells


def broadcast(value, axis, source):
    kept = jnp.where(lax.axis_index(axis) == source, value, 0).astype(value.dtype)
    for other in range(lax.axis_size(axis)):
        if other != source:
            kept = kept + lax.ppermute(jnp.where(lax.axis_index(axis) == source, value, 0), axis, [(source, other)])
    return kept


def gather_columns(value, axis):
    count = lax.axis_size(axis)
    copies = jnp.broadcast_to(value[None], (count,) + value.shape)
    blocks = lax.all_to_all(copies, axis, 0, 0, tiled=True)
    return blocks.transpose(1, 0, 2).reshape(value.shape[0], -1)


def reduce_cycle(terms, column_count, group_count):
    blocks = terms.reshape(terms.shape[0], column_count, -1).transpose(1, 0, 2)
    partial = lax.all_to_all(blocks, "gx", 0, 0, tiled=True).sum(axis=0)
    total = partial
    for group in range(group_count - 1):
        total = total + lax.ppermute(partial, "grp", [(group, group_count - 1)])
    return total


def advance(extended, center, diffusion, coriolis, mixing):
    neighbours = (
        extended[:, 1:-1, :-2]
        + extended[:, 1:-1, 2:]
        + extended[:, :-2, 1:-1]
        + extended[:, 2:, 1:-1]
        + extended[:, :-2, 2:]
        + extended[:, 2:, :-2]
    )
    laplace = neighbours - 6.0 * center
    lane_count, row_count, col_count = center.shape
    level_count = mixing.shape[0]
    stacked = center.reshape(lane_count // level_count, level_count, row_count, col_count)
    upper = jnp.concatenate([stacked[:, 1:], stacked[:, -1:]], axis=1)
    lower = jnp.concatenate([stacked[:, :1], stacked[:, :-1]], axis=1)
    vertical = mixing[None, :, None, None] * (upper - 2.0 * stacked + lower)
    rotation = jnp.concatenate(
        [
            (coriolis[:, None] * stacked[1])[None],
            (-coriolis[:, None] * stacked[0])[None],
            jnp.zeros_like(stacked[2:]),
        ],
        axis=0,
    )
    return center + diffusion * laplace + (vertical + rotation).reshape(center.shape)


def dense_plan(
    atmosphere,
    diffusion,
    coriolis,
    mixing,
    stencil_owner,
    stencil_cell,
    stencil_weight,
    feedback_owner,
    feedback_cell,
):
    lane_count, row_count, col_count = atmosphere.shape
    cell_count = row_count * col_count
    column_count = lax.axis_size("gx")
    group_count = lax.axis_size("grp")
    group_index = lax.axis_index("grp")
    column_index = lax.axis_index("gx")
    own_rank = group_index * column_count + column_index
    is_nested = group_index == group_count - 1
    perimeter = stencil_owner.shape[2]
    owner_flat = feedback_owner.reshape(-1)
    target_flat = feedback_cell.reshape(-1)
    current = atmosphere
    for substep in range(SUBSTEPS):
        flat_now = current.reshape(lane_count, cell_count)
        cycle_terms = jnp.zeros((lane_count, column_count * perimeter), jnp.float32)
        for member in range(stencil_owner.shape[1]):
            mine = stencil_owner[:, member, :].reshape(-1) == own_rank
            positions = jnp.where(mine, stencil_cell[:, member, :].reshape(-1), 0)
            weights = jnp.where(mine, stencil_weight[:, member, :].reshape(-1), 0.0)
            cycle_terms = cycle_terms + jnp.take(flat_now, positions, axis=1) * weights
        cycle = reduce_cycle(cycle_terms, column_count, group_count)
        extended = padded(current, (("grp", 1), ("gx", 2)), 1)
        upper_rim = jnp.where(group_index == 0, extended[:, 1:2, :], extended[:, 0:1, :])
        lower_rim = jnp.where(
            group_index == group_count - 2, extended[:, -2:-1, :], extended[:, -1:, :]
        )
        extended = jnp.concatenate([upper_rim, extended[:, 1:-1, :], lower_rim], axis=1)
        fresh = advance(extended, current, diffusion, coriolis, mixing)
        left_edge = jnp.where(
            column_index == 0, cycle[:, 2 * col_count : 2 * col_count + row_count], fresh[:, :, 0]
        )
        right_edge = jnp.where(
            column_index == column_count - 1, cycle[:, 2 * col_count + row_count :], fresh[:, :, -1]
        )
        framed = fresh.at[:, :, 0].set(left_edge).at[:, :, -1].set(right_edge)
        framed = (
            framed.at[:, 0, :]
            .set(cycle[:, :col_count])
            .at[:, -1, :]
            .set(cycle[:, col_count : 2 * col_count])
        )
        fresh = jnp.where(is_nested, framed, fresh)
        coarse = fresh.reshape(lane_count, row_count // 4, 4, col_count // 4, 4).mean(axis=(2, 4))
        coarse = coarse.reshape(lane_count, -1)
        fresh_flat = fresh.reshape(lane_count, cell_count)
        shared = broadcast(coarse, "grp", group_count - 1)
        place_positions = jnp.where(owner_flat == own_rank, target_flat, cell_count)
        result_flat = fresh_flat.at[:, place_positions].set(
            gather_columns(shared, "gx"), mode="drop"
        )
        current = result_flat.reshape(lane_count, row_count, col_count)
    return current


def iota(shape, dim):
    return lax.broadcasted_iota(jnp.int32, shape, dim)


def rows_of(device):
    return pl.ds(pl.multiple_of(8 * device, 8), 8)


def take(tile, index):
    return jnp.take_along_axis(tile, index, axis=1, mode="promise_in_bounds")


def halves(values):
    high = values.astype(jnp.bfloat16)
    return high, (values - high.astype(F32)).astype(jnp.bfloat16)


def product(left, right, contract=(1, 0)):
    dims = (((contract[0],), (contract[1],)), ((), ()))
    return lax.dot_general(left, right, dims, preferred_element_type=F32)


def ranks(masks):
    rows = masks[0].shape[0]
    stacked = jnp.concatenate([jnp.where(m, 1.0, 0.0) for m in masks], axis=0)
    stacked = stacked.astype(jnp.bfloat16)
    before = jnp.where(iota((128, 128), 0) < iota((128, 128), 1), 1.0, 0.0).astype(jnp.bfloat16)
    ones = jnp.ones((128, 128), jnp.bfloat16)
    within = product(stacked, before)
    totals = product(stacked, ones)
    carry = jnp.zeros((rows, 128), F32)
    found = []
    for t in range(len(masks)):
        found.append(within[t * rows : (t + 1) * rows] + carry)
        carry = carry + totals[t * rows : (t + 1) * rows]
    return found, carry


def slot_table(masks, values, slots, mark_s, value_s):
    found, total = ranks(masks)
    for t in range(TILES):
        mark_s[t] = jnp.where(masks[t], found[t], -1.0)
        value_s[t] = values[t]
    slot_of = lax.rem(iota((8, 128), 1), slots)
    parts = []
    for part in range(GX // 8):
        span = slice(8 * part, 8 * part + 8)
        marks = [mark_s[t, span, :] for t in range(TILES)]
        vals = [value_s[t, span, :] for t in range(TILES)]
        table = jnp.zeros((8, 128), F32)
        for j in range(slots):
            picked = [jnp.where(m == float(j), v, 0.0) for m, v in zip(marks, vals)]
            while len(picked) > 1:
                picked = [sum(picked[k : k + 2]) for k in range(0, len(picked), 2)]
            table = jnp.where(slot_of == j, jnp.sum(picked[0], axis=1, keepdims=True), table)
        parts.append(table)
    return jnp.concatenate(parts, axis=0), total


def send_cells(rows_s, table_ref, send_ref, flag):
    lane = iota((8, 128), 1)
    group_of = lane // SLOTS
    table = table_ref[0:GX, :]
    for g in range(7):
        index = jnp.zeros((1, 128), jnp.int32)
        members = [q for q in range(5 * g, 5 * g + 5) if q < GX]
        for q in members:
            index = jnp.where(group_of[0:1] == q - 5 * g, table[q : q + 1, :], index)
        index = jnp.broadcast_to(index, (8, 128))
        col = jnp.bitwise_and(index, 127)
        row = jnp.right_shift(index, 7)
        cells = [jnp.zeros((8, 128), F32) for _ in range(FG)]
        for r in range(ROWS):
            here = row == r
            for k in range(FG):
                cells[k] = jnp.where(here, take(rows_s[r, 8 * k : 8 * k + 8, :], col), cells[k])
        for q in members:
            block = jnp.zeros((8, 128), F32) if flag is None else flag
            for k in range(FG):
                shift = (SLOTS * (k - (q - 5 * g))) % 128
                moved = cells[k] if shift == 0 else pltpu.roll(cells[k], shift, 1)
                block = jnp.where(group_of == k, moved, block)
            send_ref[8 * (PARENTS + q) : 8 * (PARENTS + q) + 8, :] = block


def edge_block(x_ref, col):
    lane = iota((8, 128), 1)
    block = jnp.zeros((8, 128), F32)
    for h in range(2):
        for f in range(LANES):
            edge = x_ref[f, 8 * h : 8 * h + 8, col : col + 1]
            block = jnp.where(lane == EDGE + h * LANES + f, edge, block)
    return block


def send_parent_edges(x_ref, send_ref, grp, gx):
    first = edge_block(x_ref, 0)
    last = edge_block(x_ref, COLS - 1)
    right = lax.rem(gx + 1, GX)
    left = lax.rem(gx + GX - 1, GX)
    send_ref[rows_of(grp * GX + right), :] = last
    send_ref[rows_of(grp * GX + left), :] = first

    @pl.when(grp > 0)
    def _():
        send_ref[rows_of((grp - 1) * GX + right), :] = last

    @pl.when(grp < 2)
    def _():
        send_ref[rows_of((grp + 1) * GX + left), :] = first


def unpack_edge(block):
    return jnp.concatenate([block, pltpu.roll(block, 128 - LANES, 1)], axis=0)


def update(x_ref, out_ref, diff_ref, cor_ref, mix_ref):
    lane = iota((ROWS, COLS), 1)
    row = iota((ROWS, COLS), 0)
    diff = diff_ref[...]
    cor = jnp.zeros((ROWS, COLS), F32)
    for r in range(ROWS):
        cor = jnp.where(row == r, cor_ref[r], cor)
    for f in range(LANES):
        level = f % LEVELS
        x = x_ref[f]
        up = jnp.where(row == 0, 0.0, pltpu.roll(x, 1, 0))
        down = jnp.where(row == ROWS - 1, 0.0, pltpu.roll(x, ROWS - 1, 0))
        westward = jnp.where(lane == 0, 0.0, pltpu.roll(x + down, 1, 1))
        eastward = jnp.where(lane == COLS - 1, 0.0, pltpu.roll(x + up, COLS - 1, 1))
        laplace = (westward + eastward) + (up + down) - 6.0 * x
        upper = x if level == LEVELS - 1 else x_ref[f + 1]
        lower = x if level == 0 else x_ref[f - 1]
        extra = mix_ref[level] * (upper - 2.0 * x + lower)
        if f < LEVELS:
            extra = extra + cor * x_ref[f + LEVELS]
        elif f < 2 * LEVELS:
            extra = extra - cor * x_ref[f - LEVELS]
        out_ref[f] = x + diff * laplace + extra


def add_columns(from_ref, out_ref, recv_ref, diff_ref, grp, gx):
    nest = grp == 3
    right = lax.rem(gx + 1, GX)
    left = lax.rem(gx + GX - 1, GX)
    lane = iota((ROWS, COLS), 1)
    row = iota((ROWS, COLS), 0)
    from_left = unpack_edge(recv_ref[rows_of(grp * GX + left), :])
    from_right = unpack_edge(recv_ref[rows_of(grp * GX + right), :])
    top_right = unpack_edge(recv_ref[rows_of(jnp.maximum(grp - 1, 0) * GX + right), :])[ROWS - 1 : ROWS]
    low_left = unpack_edge(recv_ref[rows_of(jnp.minimum(grp + 1, 3) * GX + left), :])[0:1]
    top_right = jnp.where(grp == 0, from_right[0:1], top_right)
    low_left = jnp.where(grp == 2, from_left[ROWS - 1 : ROWS], low_left)
    top_right = jnp.where(nest, 0.0, top_right)
    low_left = jnp.where(nest, 0.0, low_left)
    left_sum = from_left + jnp.where(row == ROWS - 1, low_left, pltpu.roll(from_left, ROWS - 1, 0))
    right_sum = from_right + jnp.where(row == 0, top_right, pltpu.roll(from_right, 1, 0))
    left_sum = jnp.where(jnp.logical_and(nest, gx == 0), 0.0, left_sum)
    right_sum = jnp.where(jnp.logical_and(nest, gx == GX - 1), 0.0, right_sum)
    diff = diff_ref[...]
    left_sum = left_sum * diff[:, 0:1]
    right_sum = right_sum * diff[:, COLS - 1 : COLS]
    source = jnp.bitwise_and(EDGE + jnp.right_shift(lane + 1, 1), 127)
    spread = jnp.concatenate(
        [
            jnp.where(
                jnp.bitwise_and(lane[0:8], 1) == 0,
                take(left_sum[h : h + 8], source[0:8]),
                take(right_sum[h : h + 8], jnp.where(lane[0:8] == 127, EDGE, source[0:8])),
            )
            for h in (0, 8)
        ],
        axis=0,
    )
    outer = jnp.logical_or(lane == 0, lane == COLS - 1)
    for f in range(LANES):
        moved = spread if f == 0 else pltpu.roll(spread, 128 - 2 * f, 1)
        out_ref[f] = from_ref[f] + jnp.where(outer, moved, 0.0)


def add_rows(x_ref, out_ref, above_ref, below_ref, diff_ref, grp):
    lane = iota((LANES, COLS), 1)
    above = jnp.where(grp == 0, x_ref[:, 0, :], above_ref[...])
    below = jnp.where(grp == 2, x_ref[:, ROWS - 1, :], below_ref[...])
    above = above + jnp.where(lane == COLS - 1, 0.0, pltpu.roll(above, COLS - 1, 1))
    below = below + jnp.where(lane == 0, 0.0, pltpu.roll(below, 1, 1))
    out_ref[:, 0, :] = out_ref[:, 0, :] + diff_ref[0:1, :] * above
    out_ref[:, ROWS - 1, :] = out_ref[:, ROWS - 1, :] + diff_ref[ROWS - 1 : ROWS, :] * below


def chunks(count, step, body):
    def run(c, carry):
        for s in range(step):
            body(c * step + s)
        return carry

    lax.fori_loop(0, count // step, run, 0)


def regroup(recv_ref, group_s):
    member_of = iota((8, 128), 1) // SLOTS

    def body(g):
        tiles = [jnp.zeros((8, 128), F32) for _ in range(FG)]
        for i in range(5):
            block = recv_ref[rows_of(g * 5 + i), :]
            for k in range(FG):
                shift = (SLOTS * (i - k)) % 128
                moved = block if shift == 0 else pltpu.roll(block, shift, 1)
                tiles[k] = jnp.where(member_of == i, moved, tiles[k])
        for k in range(FG):
            group_s[g, 8 * k : 8 * k + 8, :] = tiles[k]

    chunks(PGROUPS, 2, body)


def regroup_hits(recv_ref, group_s):
    for h in range(2):
        first = SENT + 128 * h
        group_s[PGROUPS + h] = recv_ref[first : first + 128, :].T[0:LANES]


def interpolate(codes_ref, weight_s, group_s, groups, cycle_s, column_s):
    def cells_of(t):
        code = jnp.broadcast_to(codes_ref[pl.ds(t, 1), :], (8, 128))
        index = jnp.bitwise_and(code, 127)
        group = jnp.right_shift(code, 7)
        weight = weight_s[pl.ds(t, 1), :]
        cells = [jnp.zeros((8, 128), F32) for _ in range(FG)]
        for g in range(groups):
            here = group == g
            for k in range(FG):
                cells[k] = jnp.where(here, take(group_s[g, 8 * k : 8 * k + 8, :], index), cells[k])
        return [weight * c for c in cells]

    cycle_s[...] = jnp.zeros((2, LANES, 128), F32)

    def body(t):
        span = jnp.bitwise_and(t, 1)
        for k, cells in enumerate(cells_of(t)):
            cycle_s[span, 8 * k : 8 * k + 8, :] += cells

    chunks(6, 1, body)
    for k, cells in enumerate(cells_of(6)):
        total = cells + pltpu.roll(cells, 96, 1) + pltpu.roll(cells, 64, 1)
        column_s[8 * k : 8 * k + 8, :] = total


def load_weights(weight_ref, weight_s, gx):
    weight_s[...] = jnp.zeros((8, 128), F32)
    for k in range(3):
        own = weight_ref[k, pl.ds(gx, 1), :]
        weight_s[2 * k : 2 * k + 1, :] = own[:, 0:128]
        weight_s[2 * k + 1 : 2 * k + 2, :] = own[:, 128:256]
        weight_s[6:7, 32 * k : 32 * k + 32] = own[:, 256:288]


def pack_tiles(rows):
    lane = iota((1, 128), 1)
    last = rows[2]
    for k in (1, 2):
        moved = pltpu.roll(jnp.broadcast_to(rows[3 * k + 2], (8, 128)), 32 * k, 1)[0:1]
        last = jnp.where(lane >= 32 * k, moved, last)
    return [rows[3 * k + span] for k in range(3) for span in range(2)] + [last]


def prescribe(out_ref, cycle_s, column_s, gx):
    lane = iota((ROWS, COLS), 1)

    @pl.when(jnp.logical_or(gx == 0, gx == GX - 1))
    def _():
        turned = jnp.concatenate([column_s[...], jnp.zeros((88, 128), F32)], axis=0).T
        column = jnp.where(gx == 0, turned[0:ROWS, :], turned[ROWS : 2 * ROWS, :])
        at = jnp.where(gx == 0, 0, COLS - 1)
        for f in range(LANES):
            out_ref[f] = jnp.where(lane == at, column[:, f : f + 1], out_ref[f])

    out_ref[:, 0, :] = cycle_s[0]
    out_ref[:, ROWS - 1, :] = cycle_s[1]


def send_coarse(out_ref, pick_ref, send_ref, base, count):
    mean = jnp.where(iota((32, 128), 1) // 4 == iota((32, 128), 0), 1.0 / 16.0, 0.0)
    parts = []
    for i in range(4):
        total = (out_ref[:, 4 * i, :] + out_ref[:, 4 * i + 1, :]) + (
            out_ref[:, 4 * i + 2, :] + out_ref[:, 4 * i + 3, :]
        )
        wide = jnp.concatenate([total, total, jnp.zeros((48, 128), F32)], axis=0)
        parts.append(
            lax.dot_general(
                mean,
                wide,
                (((1,), (1,)), ((), ())),
                precision=lax.Precision.HIGHEST,
                preferred_element_type=F32,
            )
        )
    coarse = jnp.concatenate(parts, axis=0)
    plane_of = iota((128, 128), 1) // LANES
    placed = [jnp.where(plane_of == plane, coarse, 0.0) for plane in range(PLANES)]
    high, low = halves(jnp.concatenate(placed, axis=0))
    both = product(pick_ref[0:count, :], jnp.concatenate([high, low], axis=1))
    sent = both[:, 0:128] + both[:, 128:256]
    if base is not None:
        sent = sent + base[0:1, :]
    send_ref[0:count, :] = sent


def feed_back(src_ref, out_ref, recv_ref, pick_ref, map_ref):
    high, low = halves(recv_ref[SENT : SENT + TAKEN, :])
    both = product(pick_ref[...], jnp.concatenate([high, low], axis=1))
    total = both[:, 0:128] + both[:, 128:256]
    entries = total[0:ENTRIES]
    for plane in range(1, PLANES):
        part = total[plane * ENTRIES : (plane + 1) * ENTRIES]
        entries = entries + pltpu.roll(part, 128 - LANES * plane, 1)
    turned = entries.T
    for r in range(ROWS):
        code = jnp.broadcast_to(map_ref[r : r + 1, :], (8, 128))
        fed = code >= 0
        index = jnp.bitwise_and(code, 127)
        for k in range(FG):
            span = slice(8 * k, 8 * k + 8)
            out_ref[span, r, :] = jnp.where(fed, take(turned[span], index), src_ref[span, r, :])


def feedback_routes(owner_ref, cell_ref, pick_ref, map_ref, me):
    cell = cell_ref[...]
    own = owner_ref[...] == me
    found, total = ranks([own])
    slot = jnp.minimum(found[0], float(MEANS - 1))
    below = jnp.where(iota((GX, GX), 1) < iota((GX, GX), 0), 1.0, 0.0).astype(jnp.bfloat16)
    entry = found[0] + product(below, total.astype(jnp.bfloat16))
    entry = jnp.where(own, entry, -1.0)
    plane = jnp.floor(slot * 0.125)
    place = iota((GX, 128), 0).astype(F32) * 8.0 + (slot - 8.0 * plane)
    row = jnp.right_shift(cell, 7)
    col = jnp.bitwise_and(cell, 127)
    cells = jnp.zeros((ROWS, 128), F32)
    codes = jnp.zeros((ENTRIES, 128), F32)
    for q in range(GX):
        line = slice(q, q + 1)
        here = jnp.where(iota((ROWS, 128), 0) == row[line], entry[line] + 1.0, 0.0)
        hot = jnp.where(iota((128, 128), 0) == col[line], 1.0, 0.0)
        cells = cells + product(here.astype(jnp.bfloat16), hot.astype(jnp.bfloat16), (1, 1))
        hot = jnp.where(iota((ENTRIES, 128), 0).astype(F32) == entry[line], 1.0, 0.0)
        both = jnp.where(
            iota((128, 128), 0) == 0,
            place[line],
            jnp.where(iota((128, 128), 0) == 1, plane[line] + 1.0, 0.0),
        )
        codes = codes + product(hot.astype(jnp.bfloat16), both.astype(jnp.bfloat16), (1, 1))
    map_ref[...] = cells.astype(jnp.int32) - 1
    at = codes[:, 0:1]
    level = codes[:, 1:2] - 1.0
    lane = iota((ENTRIES, TAKEN), 1).astype(F32)
    for p in range(PLANES):
        hot = jnp.where(jnp.where(level == float(p), at, -1.0) == lane, 1.0, 0.0)
        pick_ref[p * ENTRIES : (p + 1) * ENTRIES, :] = hot.astype(jnp.bfloat16)
    count = jnp.sum(jnp.where(own, 1.0, 0.0), axis=0, keepdims=True)
    return jnp.where(jnp.sum(count, axis=1, keepdims=True) > float(ENTRIES), 1.0, 0.0)


def load_terms(owner_ref, cell_ref, gid_s):
    for k in range(3):
        gid = owner_ref[k] * 2048 + cell_ref[k]
        gid_s[3 * k] = gid[:, 0:128]
        gid_s[3 * k + 1] = gid[:, 128:256]
        gid_s[3 * k + 2] = jnp.full((GX, 128), -1, jnp.int32)
        gid_s[3 * k + 2, :, 0:32] = gid[:, 256:288]


def flag_block(over):
    worst = jnp.max(over, axis=0, keepdims=True)
    flag = jnp.where(worst > 0.5, 1.0, 0.0)
    return jnp.where(iota((8, 128), 1) == 127, jnp.broadcast_to(flag, (8, 128)), 0.0)


def first_kernel(
    x_ref, owner_ref, cell_ref, send_ref, table_ref, flag_ref, last_row_ref, first_row_ref,
    gid_s, mark_s, value_s, rows_s,
):
    grp = lax.axis_index("grp")
    gx = lax.axis_index("gx")
    last_row_ref[...] = x_ref[:, ROWS - 1, :]
    first_row_ref[...] = x_ref[:, 0, :]

    @pl.when(grp < 3)
    def _():
        load_terms(owner_ref, cell_ref, gid_s)
        gids = [gid_s[t] for t in range(TILES)]
        masks = [jnp.right_shift(g, 11) == grp * GX + gx for g in gids]
        values = [jnp.bitwise_and(g, 2047).astype(F32) for g in gids]
        table, total = slot_table(masks, values, SLOTS, mark_s, value_s)
        table_ref[...] = table.astype(jnp.int32)
        flag_ref[...] = flag_block(jnp.where(total > float(SLOTS), 1.0, 0.0))
        for r in range(ROWS):
            rows_s[r] = x_ref[:, r, :]
        send_cells(rows_s, table_ref, send_ref, None)
        send_parent_edges(x_ref, send_ref, grp, gx)

    @pl.when(grp == 3)
    def _():
        right = PARENTS + lax.rem(gx + 1, GX)
        left = PARENTS + lax.rem(gx + GX - 1, GX)
        send_ref[rows_of(right), :] = edge_block(x_ref, COLS - 1)
        send_ref[rows_of(left), :] = edge_block(x_ref, 0)


def tables_kernel(
    x_ref, diff_ref, cor_ref, mix_ref, owner_ref, cell_ref, fb_owner_ref, fb_cell_ref,
    flag_in_ref, fresh_ref, codes_ref, pick_ref, flag_ref, map_ref, entry_ref,
    gid_s, mark_s, value_s, found_s, seek_s,
):
    grp = lax.axis_index("grp")
    gx = lax.axis_index("gx")
    update(x_ref, fresh_ref, diff_ref, cor_ref, mix_ref)

    @pl.when(grp < 3)
    def _():
        over = feedback_routes(fb_owner_ref, fb_cell_ref, entry_ref, map_ref, grp * GX + gx)
        lane = iota((8, 128), 1)
        flag_ref[...] = jnp.where(lane == 127, jnp.maximum(flag_in_ref[...], over), 0.0)

    @pl.when(grp == 3)
    def _():
        load_terms(owner_ref, cell_ref, gid_s)
        own_owner = fb_owner_ref[pl.ds(gx, 1), :]
        own_cell = fb_cell_ref[pl.ds(gx, 1), :]
        hot = iota((128, 128), 0) == own_owner
        found, total = ranks([hot])
        over = jnp.max(jnp.where(total > float(MEANS), 1.0, 0.0), axis=0, keepdims=True)
        rank = jnp.sum(jnp.where(hot, found[0], 0.0), axis=0, keepdims=True).astype(jnp.int32)
        level = jnp.right_shift(rank, 3)
        place = own_owner * 8 + jnp.bitwise_and(rank, 7)
        for p in range(PLANES):
            wanted = jnp.where(level == p, place, -1)
            for part in range(6):
                line = iota((128, 128), 0) + 128 * part
                pick_ref[128 * part : 128 * part + 128, 128 * p : 128 * p + 128] = jnp.where(
                    line == wanted, 1.0, 0.0
                ).astype(jnp.bfloat16)

        owners = [jnp.right_shift(gid_s[t, pl.ds(gx, 1), :], 11) for t in range(TILES)]
        hots = [iota((PARENTS, 128), 0) == o for o in owners]
        found, _ = ranks(hots)
        codes = []
        for t in range(TILES):
            slot = jnp.sum(jnp.where(hots[t], found[t], 0.0), axis=0, keepdims=True)
            slot = jnp.minimum(slot.astype(jnp.int32), SLOTS - 1)
            group = jnp.right_shift(owners[t] * 205, 10)
            codes.append(group * 128 + (owners[t] - 5 * group) * SLOTS + slot)
        for t, code in enumerate(pack_tiles(codes)):
            codes_ref[t : t + 1, :] = code

        hot = jnp.where(hot, 1.0, 0.0).astype(jnp.bfloat16)
        chosen = iota((32, 128), 0) == rank

        def by_owner(values):
            picked = jnp.where(chosen, values.astype(F32), 0.0).astype(jnp.bfloat16)
            return product(picked, hot, (1, 1)).astype(jnp.int32)

        number = by_owner(iota((1, 128), 1) + 1)
        cells = by_owner(jnp.right_shift(own_cell, 4)) * 16 + by_owner(jnp.bitwise_and(own_cell, 15))
        seek_s[...] = jnp.where(number > 0, cells * 256 + number - 1, -1)
        found_s[...] = jnp.full((TILES, GX, 128), -1, jnp.int32)

        def seek(j, carry):
            line = jnp.broadcast_to(seek_s[pl.ds(j, 1), :], (8, 128))
            for t in range(TILES):
                for part in range(GX // 8):
                    span = slice(8 * part, 8 * part + 8)
                    gid = gid_s[t, span, :]
                    entry = take(line, jnp.bitwise_and(jnp.right_shift(gid, 11), 127))
                    same = jnp.right_shift(entry, 8) == jnp.bitwise_and(gid, 2047)
                    found_s[t, span, :] = jnp.where(
                        same, jnp.bitwise_and(entry, 255), found_s[t, span, :]
                    )
            return carry

        most = jnp.minimum(jnp.max(total).astype(jnp.int32), 32)
        lax.fori_loop(0, most, seek, 0)
        found_at = [found_s[t] for t in range(TILES)]
        table, total = slot_table(
            [f >= 0 for f in found_at], [f.astype(F32) for f in found_at], HITS, mark_s, value_s
        )
        over = jnp.maximum(
            over, jnp.max(jnp.where(total > float(HITS), 1.0, 0.0), axis=0, keepdims=True)
        )
        turned = jnp.concatenate([table, jnp.zeros((96, 128), F32)], axis=0).T
        lane = iota((8, 128), 1).astype(F32)
        blank = jnp.zeros((16, 128 * (PLANES - 1)), jnp.bfloat16)
        for pair in range(GX // 2):
            line = slice(SENT + 16 * pair, SENT + 16 * pair + 16)
            hits = [
                jnp.where(turned[0:HITS, q : q + 1] == lane, 1.0, 0.0)
                for q in (2 * pair, 2 * pair + 1)
            ]
            pick_ref[line, 0:128] = jnp.concatenate(hits, axis=0).astype(jnp.bfloat16)
            pick_ref[line, 128 : 128 * PLANES] = blank
        flag_ref[...] = flag_block(over)


def second_kernel(
    recv_ref, x_ref, fresh_ref, diff_ref, above_ref, below_ref, weight_ref, table_ref, codes_ref,
    pick_ref, flag_ref, out_ref, send_ref, rows_s, group_s, cycle_s, column_s, weight_s,
):
    grp = lax.axis_index("grp")
    gx = lax.axis_index("gx")
    add_columns(fresh_ref, out_ref, recv_ref, diff_ref, grp, gx)
    base = flag_ref[...]

    @pl.when(grp < 3)
    def _():
        add_rows(x_ref, out_ref, above_ref, below_ref, diff_ref, grp)
        for r in range(ROWS):
            rows_s[r] = out_ref[:, r, :]
        for d in range(PARENTS):
            send_ref[8 * d : 8 * d + 8, :] = base
        send_cells(rows_s, table_ref, send_ref, base)

    @pl.when(grp == 3)
    def _():
        load_weights(weight_ref, weight_s, gx)
        regroup(recv_ref, group_s)
        interpolate(codes_ref, weight_s, group_s, PGROUPS, cycle_s, column_s)
        prescribe(out_ref, cycle_s, column_s, gx)
        send_coarse(out_ref, pick_ref, send_ref, base, SENT + TAKEN)
        right = rows_of(PARENTS + lax.rem(gx + 1, GX))
        left = rows_of(PARENTS + lax.rem(gx + GX - 1, GX))
        send_ref[right, :] = send_ref[right, :] + edge_block(out_ref, COLS - 1)
        send_ref[left, :] = send_ref[left, :] + edge_block(out_ref, 0)


def hits_kernel(
    x_ref, diff_ref, cor_ref, mix_ref, owner_ref, cell_ref, fb_owner_ref, fb_cell_ref, plain_ref,
    fresh_ref, codes_ref, gid_s, turned_s,
):
    gx = lax.axis_index("gx")

    @pl.when(lax.axis_index("grp") == 3)
    def _():
        update(x_ref, fresh_ref, diff_ref, cor_ref, mix_ref)
        load_terms(owner_ref, cell_ref, gid_s)
        terms = [gid_s[t, pl.ds(gx, 1), :] for t in range(TILES)]
        fed = (fb_owner_ref[...] * 2048 + fb_cell_ref[...]).astype(F32)
        turned_s[...] = jnp.concatenate([fed, jnp.full((96, 128), -2.0, F32)], axis=0).T
        wide = [jnp.broadcast_to(t.astype(F32), (8, 128)) for t in terms]

        def match(q, from_block):
            column = pltpu.roll(turned_s[...], lax.rem(128 - q, 128), 1)[:, 0:1]
            for s in range(16):
                part = jnp.broadcast_to(column[8 * s : 8 * s + 8, :], (8, 128))
                from_block = [jnp.where(part == w, q, f) for w, f in zip(wide, from_block)]
            return from_block

        none = [jnp.full((8, 128), -1, jnp.int32) for _ in range(TILES)]
        from_block = lax.fori_loop(0, GX, match, none)
        sources = [jnp.max(f, axis=0, keepdims=True) for f in from_block]
        hots = [iota((GX, 128), 0) == s for s in sources]
        found, _ = ranks(hots)
        codes = []
        for t in range(TILES):
            slot = jnp.sum(jnp.where(hots[t], found[t], 0.0), axis=0, keepdims=True)
            slot = jnp.minimum(slot.astype(jnp.int32), HITS - 1)
            code = (PGROUPS + jnp.right_shift(sources[t], 4)) * 128
            code = code + jnp.bitwise_and(sources[t], 15) * HITS + slot
            codes.append(jnp.where(sources[t] >= 0, code, -1))
        for t, code in enumerate(pack_tiles(codes)):
            plain = plain_ref[t : t + 1, :]
            codes_ref[t : t + 1, :] = jnp.where(code >= 0, code, plain)


def third_kernel(
    recv_ref, x_ref, fresh_ref, diff_ref, weight_ref, codes_ref, pick_ref, map_ref, entry_ref,
    out_ref, send_ref, flag_ref, last_row_ref, first_row_ref,
    group_s, cycle_s, column_s, weight_s,
):
    grp = lax.axis_index("grp")
    gx = lax.axis_index("gx")
    flag = recv_ref[0:8, :]
    for d in range(1, DEVICES):
        flag = jnp.maximum(flag, recv_ref[8 * d : 8 * d + 8, :])
    flag_ref[...] = flag

    @pl.when(grp < 3)
    def _():
        feed_back(x_ref, out_ref, recv_ref, entry_ref, map_ref)
        send_parent_edges(out_ref, send_ref, grp, gx)
        last_row_ref[...] = out_ref[:, ROWS - 1, :]
        first_row_ref[...] = out_ref[:, 0, :]

    @pl.when(grp == 3)
    def _():
        add_columns(fresh_ref, out_ref, recv_ref, diff_ref, grp, gx)
        load_weights(weight_ref, weight_s, gx)
        regroup(recv_ref, group_s)
        regroup_hits(recv_ref, group_s)
        interpolate(codes_ref, weight_s, group_s, GROUPS, cycle_s, column_s)
        prescribe(out_ref, cycle_s, column_s, gx)
        send_coarse(out_ref, pick_ref, send_ref, None, SENT)


def parents_kernel(x_ref, diff_ref, cor_ref, mix_ref, fresh_ref):
    @pl.when(lax.axis_index("grp") < 3)
    def _():
        update(x_ref, fresh_ref, diff_ref, cor_ref, mix_ref)


def fourth_kernel(
    recv_ref, x_ref, fresh_ref, diff_ref, above_ref, below_ref, map_ref, entry_ref, out_ref
):
    grp = lax.axis_index("grp")
    gx = lax.axis_index("gx")

    @pl.when(grp < 3)
    def _():
        add_columns(fresh_ref, out_ref, recv_ref, diff_ref, grp, gx)
        add_rows(x_ref, out_ref, above_ref, below_ref, diff_ref, grp)
        feed_back(out_ref, out_ref, recv_ref, entry_ref, map_ref)

    @pl.when(grp == 3)
    def _():
        out_ref[...] = x_ref[...]


def call(kernel, name, ins, spaces, outs, scratch):
    space = {"s": pltpu.SMEM, "v": pltpu.VMEM}
    return pl.pallas_call(
        kernel,
        name=name,
        in_specs=[pl.BlockSpec(memory_space=space[s]) for s in spaces],
        out_specs=[pl.BlockSpec(memory_space=pltpu.VMEM) for _ in outs],
        out_shape=[jax.ShapeDtypeStruct(s, d) for s, d in outs],
        scratch_shapes=[pltpu.VMEM(s, d) for s, d in scratch],
        compiler_params=pltpu.CompilerParams(vmem_limit_bytes=VMEM_LIMIT),
        cost_estimate=pl.CostEstimate(flops=1000000, bytes_accessed=4000000, transcendentals=0),
    )(*ins)


STATE = ((LANES, ROWS, COLS), F32)
BLOCKS = ((DEVICES * 8, 128), F32)
BLOCK = ((8, 128), F32)
RIM = ((LANES, COLS), F32)
ROWMAJOR = ((ROWS, LANES, COLS), F32)
MAP = ((ROWS, 128), jnp.int32)
GIDS = ((TILES, GX, 128), jnp.int32)
TERMS = ((TILES, GX, 128), F32)
PICK = ((SENT + TAKEN, PLANES * 128), jnp.bfloat16)
ENTRY = ((PLANES * ENTRIES, TAKEN), jnp.bfloat16)
GROUPED = ((GROUPS, LANES, 128), F32)
CYCLE = ((2, LANES, 128), F32)
TABLE = ((GX, 128), jnp.int32)
CODES = ((8, 128), jnp.int32)


def exchange(blocks):
    return lax.all_to_all(blocks, ("grp", "gx"), 0, 0, tiled=True)


def rims(last_row, first_row):
    above = lax.ppermute(last_row, "grp", [(0, 1), (1, 2)])
    below = lax.ppermute(first_row, "grp", [(1, 0), (2, 1)])
    return above, below


def shards(atmosphere, diffusion, coriolis, mixing, owner, cell, weight, fb_owner, fb_cell):
    inputs = (atmosphere, diffusion, coriolis, mixing, owner, cell, weight, fb_owner, fb_cell)
    owner, cell, weight = (jnp.transpose(a, (1, 0, 2)) for a in (owner, cell, weight))
    physics = (diffusion, coriolis, mixing)
    send, table, flag, last_row, first_row = call(
        first_kernel,
        "first_cells",
        (atmosphere, owner, cell),
        "vvv",
        (BLOCKS, TABLE, BLOCK, RIM, RIM),
        (GIDS, TERMS, TERMS, ROWMAJOR),
    )
    recv = exchange(send)
    above, below = rims(last_row, first_row)
    fresh, codes, pick, flag, place, entry = call(
        tables_kernel,
        "tables",
        (atmosphere,) + physics + (owner, cell, fb_owner, fb_cell, flag),
        "vvssvvvvv",
        (STATE, CODES, PICK, BLOCK, MAP, ENTRY),
        (GIDS, TERMS, TERMS, GIDS, ((32, 128), jnp.int32)),
    )
    state, send = call(
        second_kernel,
        "substep_one",
        (recv, atmosphere, fresh, diffusion, above, below, weight, table, codes, pick, flag),
        "v" * 11,
        (STATE, BLOCKS),
        (ROWMAJOR, GROUPED, CYCLE, RIM, BLOCK),
    )
    recv = exchange(send)
    fresh, codes = call(
        hits_kernel,
        "hits",
        (state,) + physics + (owner, cell, fb_owner, fb_cell, codes),
        "vvssvvvvv",
        (STATE, CODES),
        (GIDS, ((128, 128), F32)),
    )
    state, send, flag, last_row, first_row = call(
        third_kernel,
        "substep_two",
        (recv, state, fresh, diffusion, weight, codes, pick, place, entry),
        "v" * 9,
        (STATE, BLOCKS, BLOCK, RIM, RIM),
        (GROUPED, CYCLE, RIM, BLOCK),
    )
    recv = exchange(send)
    above, below = rims(last_row, first_row)
    (fresh,) = call(parents_kernel, "parents", (state,) + physics, "vvss", (STATE,), ())
    (state,) = call(
        fourth_kernel,
        "finish",
        (recv, state, fresh, diffusion, above, below, place, entry),
        "v" * 8,
        (STATE,),
        (),
    )
    return lax.cond(flag[0, 127] > 0.5, lambda s, *a: dense_plan(*a), lambda s, *a: s, state, *inputs)


def solution(mesh):
    placed = (P(None, "grp", "gx"), P("grp", "gx"), P("grp"), P(), P(), P(), P(), P(), P())
    return jax.shard_map(
        shards, mesh=mesh, in_specs=placed, out_specs=P(None, "grp", "gx"), check_vma=False
    )
```

```python
import jax
import jax.numpy as jnp
from jax import lax
from jax.experimental import pallas as pl
from jax.experimental.pallas import tpu as pltpu
from jax.sharding import PartitionSpec as P

SUBSTEPS = 2
F32 = jnp.float32
LANES = 40
ROWS = 16
COLS = 128
LEVELS = 10
GX = 32
PARENTS = 96
DEVICES = 128
PERIM = 288
TILES = 9
SLOTS = 25
HITS = 8
EDGE = 40
FG = 5
PGROUPS = 20
GROUPS = 22
ENTRIES = 128
PLANES = 3
DEPTH = 4
MEANS = DEPTH * PLANES
MEAN_ROWS = PARENTS * DEPTH
SENT = PARENTS * 8
TAKEN = GX * 8
VMEM_LIMIT = 24 * 1024 * 1024


def padded(cells, sides, width):
    for axis, dim in sides:
        count = lax.axis_size(axis)
        head = lax.slice_in_dim(cells, 0, width, axis=dim)
        tail = lax.slice_in_dim(cells, cells.shape[dim] - width, cells.shape[dim], axis=dim)
        cells = jnp.concatenate(
            [
                lax.ppermute(tail, axis, [(i, (i + 1) % count) for i in range(count)]),
                cells,
                lax.ppermute(head, axis, [((i + 1) % count, i) for i in range(count)]),
            ],
            axis=dim,
        )
    return cells


def broadcast(value, axis, source):
    kept = jnp.where(lax.axis_index(axis) == source, value, 0).astype(value.dtype)
    for other in range(lax.axis_size(axis)):
        if other != source:
            kept = kept + lax.ppermute(jnp.where(lax.axis_index(axis) == source, value, 0), axis, [(source, other)])
    return kept


def gather_columns(value, axis):
    count = lax.axis_size(axis)
    copies = jnp.broadcast_to(value[None], (count,) + value.shape)
    blocks = lax.all_to_all(copies, axis, 0, 0, tiled=True)
    return blocks.transpose(1, 0, 2).reshape(value.shape[0], -1)


def reduce_cycle(terms, column_count, group_count):
    blocks = terms.reshape(terms.shape[0], column_count, -1).transpose(1, 0, 2)
    partial = lax.all_to_all(blocks, "gx", 0, 0, tiled=True).sum(axis=0)
    total = partial
    for group in range(group_count - 1):
        total = total + lax.ppermute(partial, "grp", [(group, group_count - 1)])
    return total


def advance(extended, center, diffusion, coriolis, mixing):
    neighbours = (
        extended[:, 1:-1, :-2]
        + extended[:, 1:-1, 2:]
        + extended[:, :-2, 1:-1]
        + extended[:, 2:, 1:-1]
        + extended[:, :-2, 2:]
        + extended[:, 2:, :-2]
    )
    laplace = neighbours - 6.0 * center
    lane_count, row_count, col_count = center.shape
    level_count = mixing.shape[0]
    stacked = center.reshape(lane_count // level_count, level_count, row_count, col_count)
    upper = jnp.concatenate([stacked[:, 1:], stacked[:, -1:]], axis=1)
    lower = jnp.concatenate([stacked[:, :1], stacked[:, :-1]], axis=1)
    vertical = mixing[None, :, None, None] * (upper - 2.0 * stacked + lower)
    rotation = jnp.concatenate(
        [
            (coriolis[:, None] * stacked[1])[None],
            (-coriolis[:, None] * stacked[0])[None],
            jnp.zeros_like(stacked[2:]),
        ],
        axis=0,
    )
    return center + diffusion * laplace + (vertical + rotation).reshape(center.shape)


def dense_plan(
    atmosphere,
    diffusion,
    coriolis,
    mixing,
    stencil_owner,
    stencil_cell,
    stencil_weight,
    feedback_owner,
    feedback_cell,
):
    lane_count, row_count, col_count = atmosphere.shape
    cell_count = row_count * col_count
    column_count = lax.axis_size("gx")
    group_count = lax.axis_size("grp")
    group_index = lax.axis_index("grp")
    column_index = lax.axis_index("gx")
    own_rank = group_index * column_count + column_index
    is_nested = group_index == group_count - 1
    perimeter = stencil_owner.shape[2]
    owner_flat = feedback_owner.reshape(-1)
    target_flat = feedback_cell.reshape(-1)
    current = atmosphere
    for substep in range(SUBSTEPS):
        flat_now = current.reshape(lane_count, cell_count)
        cycle_terms = jnp.zeros((lane_count, column_count * perimeter), jnp.float32)
        for member in range(stencil_owner.shape[1]):
            mine = stencil_owner[:, member, :].reshape(-1) == own_rank
            positions = jnp.where(mine, stencil_cell[:, member, :].reshape(-1), 0)
            weights = jnp.where(mine, stencil_weight[:, member, :].reshape(-1), 0.0)
            cycle_terms = cycle_terms + jnp.take(flat_now, positions, axis=1) * weights
        cycle = reduce_cycle(cycle_terms, column_count, group_count)
        extended = padded(current, (("grp", 1), ("gx", 2)), 1)
        upper_rim = jnp.where(group_index == 0, extended[:, 1:2, :], extended[:, 0:1, :])
        lower_rim = jnp.where(
            group_index == group_count - 2, extended[:, -2:-1, :], extended[:, -1:, :]
        )
        extended = jnp.concatenate([upper_rim, extended[:, 1:-1, :], lower_rim], axis=1)
        fresh = advance(extended, current, diffusion, coriolis, mixing)
        left_edge = jnp.where(
            column_index == 0, cycle[:, 2 * col_count : 2 * col_count + row_count], fresh[:, :, 0]
        )
        right_edge = jnp.where(
            column_index == column_count - 1, cycle[:, 2 * col_count + row_count :], fresh[:, :, -1]
        )
        framed = fresh.at[:, :, 0].set(left_edge).at[:, :, -1].set(right_edge)
        framed = (
            framed.at[:, 0, :]
            .set(cycle[:, :col_count])
            .at[:, -1, :]
            .set(cycle[:, col_count : 2 * col_count])
        )
        fresh = jnp.where(is_nested, framed, fresh)
        coarse = fresh.reshape(lane_count, row_count // 4, 4, col_count // 4, 4).mean(axis=(2, 4))
        coarse = coarse.reshape(lane_count, -1)
        fresh_flat = fresh.reshape(lane_count, cell_count)
        shared = broadcast(coarse, "grp", group_count - 1)
        place_positions = jnp.where(owner_flat == own_rank, target_flat, cell_count)
        result_flat = fresh_flat.at[:, place_positions].set(
            gather_columns(shared, "gx"), mode="drop"
        )
        current = result_flat.reshape(lane_count, row_count, col_count)
    return current


def iota(shape, dim):
    return lax.broadcasted_iota(jnp.int32, shape, dim)


def rows_of(device):
    return pl.ds(pl.multiple_of(8 * device, 8), 8)


def take(tile, index):
    return jnp.take_along_axis(tile, index, axis=1, mode="promise_in_bounds")


def halves(values):
    high = values.astype(jnp.bfloat16)
    return high, (values - high.astype(F32)).astype(jnp.bfloat16)


def product(left, right, contract=(1, 0)):
    dims = (((contract[0],), (contract[1],)), ((), ()))
    return lax.dot_general(left, right, dims, preferred_element_type=F32)


def ranks(masks):
    rows = masks[0].shape[0]
    stacked = jnp.concatenate([jnp.where(m, 1.0, 0.0) for m in masks], axis=0)
    stacked = stacked.astype(jnp.bfloat16)
    before = jnp.where(iota((128, 128), 0) < iota((128, 128), 1), 1.0, 0.0).astype(jnp.bfloat16)
    ones = jnp.ones((128, 128), jnp.bfloat16)
    within = product(stacked, before)
    totals = product(stacked, ones)
    carry = jnp.zeros((rows, 128), F32)
    found = []
    for t in range(len(masks)):
        found.append(within[t * rows : (t + 1) * rows] + carry)
        carry = carry + totals[t * rows : (t + 1) * rows]
    return found, carry


def slot_table(masks, values, slots, mark_s, value_s):
    found, total = ranks(masks)
    for t in range(TILES):
        mark_s[t] = jnp.where(masks[t], found[t], -1.0)
        value_s[t] = values[t]
    slot_of = lax.rem(iota((8, 128), 1), slots)
    parts = []
    for part in range(GX // 8):
        span = slice(8 * part, 8 * part + 8)
        marks = [mark_s[t, span, :] for t in range(TILES)]
        vals = [value_s[t, span, :] for t in range(TILES)]
        table = jnp.zeros((8, 128), F32)
        for j in range(slots):
            picked = [jnp.where(m == float(j), v, 0.0) for m, v in zip(marks, vals)]
            while len(picked) > 1:
                picked = [sum(picked[k : k + 2]) for k in range(0, len(picked), 2)]
            table = jnp.where(slot_of == j, jnp.sum(picked[0], axis=1, keepdims=True), table)
        parts.append(table)
    return jnp.concatenate(parts, axis=0), total


def send_cells(rows_s, table_ref, blocks_s, send_ref, sems):
    copies = []
    lane = iota((8, 128), 1)
    group_of = lane // SLOTS
    table = table_ref[0:GX, :]
    for g in range(7):
        index = jnp.zeros((1, 128), jnp.int32)
        members = [q for q in range(5 * g, 5 * g + 5) if q < GX]
        for q in members:
            index = jnp.where(group_of[0:1] == q - 5 * g, table[q : q + 1, :], index)
        index = jnp.broadcast_to(index, (8, 128))
        col = jnp.bitwise_and(index, 127)
        row = jnp.right_shift(index, 7)
        cells = [jnp.zeros((8, 128), F32) for _ in range(FG)]
        for r in range(ROWS):
            here = row == r
            for k in range(FG):
                cells[k] = jnp.where(here, take(rows_s[r, 8 * k : 8 * k + 8, :], col), cells[k])
        for q in members:
            block = jnp.zeros((8, 128), F32)
            for k in range(FG):
                shift = (SLOTS * (k - (q - 5 * g))) % 128
                moved = cells[k] if shift == 0 else pltpu.roll(cells[k], shift, 1)
                block = jnp.where(group_of == k, moved, block)
            blocks_s[8 * q : 8 * q + 8, :] = block
        span = pl.ds(8 * members[0], 8 * len(members))
        rows = pl.ds(SENT + 8 * members[0], 8 * len(members))
        copies.append(pltpu.make_async_copy(blocks_s.at[span, :], send_ref.at[rows, :], sems.at[g]))
        copies[-1].start()
    return copies


def edge_block(x_ref, col):
    lane = iota((8, 128), 1)
    block = jnp.zeros((8, 128), F32)
    for h in range(2):
        for f in range(LANES):
            edge = x_ref[f, 8 * h : 8 * h + 8, col : col + 1]
            block = jnp.where(lane == EDGE + h * LANES + f, edge, block)
    return block


def edge_copies(edges_s, send_ref, sems, grp, gx):
    right = lax.rem(gx + 1, GX)
    left = lax.rem(gx + GX - 1, GX)
    above = jnp.where(grp == 3, 3, jnp.maximum(grp - 1, 0))
    below = jnp.where(grp == 3, 3, jnp.minimum(grp + 1, 2))
    first, last = edges_s.at[0:8, :], edges_s.at[8:16, :]
    plan = [
        (last, grp * GX + right),
        (first, grp * GX + left),
        (last, above * GX + right),
        (first, below * GX + left),
    ]
    return [
        pltpu.make_async_copy(source, send_ref.at[rows_of(to), :], sems.at[i])
        for i, (source, to) in enumerate(plan)
    ]


def send_edges(x_ref, edges_s, send_ref, sems, grp, gx):
    edges_s[0:8, :] = edge_block(x_ref, 0)
    edges_s[8:16, :] = edge_block(x_ref, COLS - 1)
    near = edge_copies(edges_s, send_ref, sems, grp, gx)
    for copy in near[:2]:
        copy.start()

    @pl.when(jnp.logical_or(grp == 1, grp == 2))
    def _():
        near[2].start()

    @pl.when(grp < 2)
    def _():
        near[3].start()


def wait_edges(edges_s, send_ref, sems, grp, gx):
    near = edge_copies(edges_s, send_ref, sems, grp, gx)
    for copy in near[:2]:
        copy.wait()

    @pl.when(jnp.logical_or(grp == 1, grp == 2))
    def _():
        near[2].wait()

    @pl.when(grp < 2)
    def _():
        near[3].wait()


def unpack_edge(block):
    return jnp.concatenate([block, pltpu.roll(block, 128 - LANES, 1)], axis=0)


def update(x_ref, out_ref, diff_ref, cor_ref, mix_ref):
    lane = iota((ROWS, COLS), 1)
    row = iota((ROWS, COLS), 0)
    diff = diff_ref[...]
    cor = jnp.zeros((ROWS, COLS), F32)
    for r in range(ROWS):
        cor = jnp.where(row == r, cor_ref[r], cor)
    for f in range(LANES):
        level = f % LEVELS
        x = x_ref[f]
        up = jnp.where(row == 0, 0.0, pltpu.roll(x, 1, 0))
        down = jnp.where(row == ROWS - 1, 0.0, pltpu.roll(x, ROWS - 1, 0))
        westward = jnp.where(lane == 0, 0.0, pltpu.roll(x + down, 1, 1))
        eastward = jnp.where(lane == COLS - 1, 0.0, pltpu.roll(x + up, COLS - 1, 1))
        laplace = (westward + eastward) + (up + down) - 6.0 * x
        upper = x if level == LEVELS - 1 else x_ref[f + 1]
        lower = x if level == 0 else x_ref[f - 1]
        extra = mix_ref[level] * (upper - 2.0 * x + lower)
        if f < LEVELS:
            extra = extra + cor * x_ref[f + LEVELS]
        elif f < 2 * LEVELS:
            extra = extra - cor * x_ref[f - LEVELS]
        out_ref[f] = x + diff * laplace + extra


def gather_halo(recv_ref, grp, gx):
    right = lax.rem(gx + 1, GX)
    left = lax.rem(gx + GX - 1, GX)
    from_left = unpack_edge(recv_ref[rows_of(grp * GX + left), :])
    from_right = unpack_edge(recv_ref[rows_of(grp * GX + right), :])
    top_right = unpack_edge(recv_ref[rows_of(jnp.maximum(grp - 1, 0) * GX + right), :])
    low_left = unpack_edge(recv_ref[rows_of(jnp.minimum(grp + 1, 3) * GX + left), :])
    row = iota((ROWS, COLS), 0)
    corners = jnp.where(row == 0, top_right[ROWS - 1 : ROWS], low_left[0:1])
    return from_left, from_right, corners


def add_columns(from_ref, out_ref, halo, diff_ref, grp, gx):
    from_left, from_right, corners = halo
    nest = grp == 3
    lane = iota((ROWS, COLS), 1)
    row = iota((ROWS, COLS), 0)
    top_right = jnp.where(grp == 0, from_right[0:1], corners[0:1])
    low_left = jnp.where(grp == 2, from_left[ROWS - 1 : ROWS], corners[1:2])
    top_right = jnp.where(nest, 0.0, top_right)
    low_left = jnp.where(nest, 0.0, low_left)
    left_sum = from_left + jnp.where(row == ROWS - 1, low_left, pltpu.roll(from_left, ROWS - 1, 0))
    right_sum = from_right + jnp.where(row == 0, top_right, pltpu.roll(from_right, 1, 0))
    left_sum = jnp.where(jnp.logical_and(nest, gx == 0), 0.0, left_sum)
    right_sum = jnp.where(jnp.logical_and(nest, gx == GX - 1), 0.0, right_sum)
    diff = diff_ref[...]
    left_sum = left_sum * diff[:, 0:1]
    right_sum = right_sum * diff[:, COLS - 1 : COLS]
    source = jnp.bitwise_and(EDGE + jnp.right_shift(lane + 1, 1), 127)
    spread = jnp.concatenate(
        [
            jnp.where(
                jnp.bitwise_and(lane[0:8], 1) == 0,
                take(left_sum[h : h + 8], source[0:8]),
                take(right_sum[h : h + 8], jnp.where(lane[0:8] == 127, EDGE, source[0:8])),
            )
            for h in (0, 8)
        ],
        axis=0,
    )
    outer = jnp.logical_or(lane == 0, lane == COLS - 1)
    for f in range(LANES):
        moved = spread if f == 0 else pltpu.roll(spread, 128 - 2 * f, 1)
        out_ref[f] = from_ref[f] + jnp.where(outer, moved, 0.0)


def add_rows(first_ref, last_ref, out_ref, above_ref, below_ref, diff_ref, grp):
    lane = iota((LANES, COLS), 1)
    above = jnp.where(grp == 0, first_ref[...], above_ref[...])
    below = jnp.where(grp == 2, last_ref[...], below_ref[...])
    above = above + jnp.where(lane == COLS - 1, 0.0, pltpu.roll(above, COLS - 1, 1))
    below = below + jnp.where(lane == 0, 0.0, pltpu.roll(below, 1, 1))
    out_ref[:, 0, :] = out_ref[:, 0, :] + diff_ref[0:1, :] * above
    out_ref[:, ROWS - 1, :] = out_ref[:, ROWS - 1, :] + diff_ref[ROWS - 1 : ROWS, :] * below


def chunks(count, step, body):
    def run(c, carry):
        for s in range(step):
            body(c * step + s)
        return carry

    lax.fori_loop(0, count // step, run, 0)


def regroup(recv_ref, group_s):
    member_of = iota((8, 128), 1) // SLOTS

    def body(g):
        tiles = [jnp.zeros((8, 128), F32) for _ in range(FG)]
        for i in range(5):
            block = recv_ref[rows_of(g * 5 + i), :]
            for k in range(FG):
                shift = (SLOTS * (i - k)) % 128
                moved = block if shift == 0 else pltpu.roll(block, shift, 1)
                tiles[k] = jnp.where(member_of == i, moved, tiles[k])
        for k in range(FG):
            group_s[g, 8 * k : 8 * k + 8, :] = tiles[k]

    chunks(PGROUPS, 2, body)


def regroup_hits(recv_ref, group_s):
    for h in range(2):
        first = SENT + 128 * h
        group_s[PGROUPS + h] = recv_ref[first : first + 128, :].T[0:LANES]


def interpolate(codes_ref, weight_s, group_s, groups, cycle_s, column_s):
    def cells_of(t):
        code = jnp.broadcast_to(codes_ref[pl.ds(t, 1), :], (8, 128))
        index = jnp.bitwise_and(code, 127)
        group = jnp.right_shift(code, 7)
        weight = weight_s[pl.ds(t, 1), :]
        cells = [jnp.zeros((8, 128), F32) for _ in range(FG)]
        for g in range(groups):
            here = group == g
            for k in range(FG):
                cells[k] = jnp.where(here, take(group_s[g, 8 * k : 8 * k + 8, :], index), cells[k])
        return [weight * c for c in cells]

    cycle_s[...] = jnp.zeros((2, LANES, 128), F32)

    def body(t):
        span = jnp.bitwise_and(t, 1)
        for k, cells in enumerate(cells_of(t)):
            cycle_s[span, 8 * k : 8 * k + 8, :] += cells

    chunks(6, 1, body)
    for k, cells in enumerate(cells_of(6)):
        total = cells + pltpu.roll(cells, 96, 1) + pltpu.roll(cells, 64, 1)
        column_s[8 * k : 8 * k + 8, :] = total


def load_weights(weight_ref, weight_s, gx):
    weight_s[...] = jnp.zeros((8, 128), F32)
    for k in range(3):
        own = weight_ref[k, pl.ds(gx, 1), :]
        weight_s[2 * k : 2 * k + 1, :] = own[:, 0:128]
        weight_s[2 * k + 1 : 2 * k + 2, :] = own[:, 128:256]
        weight_s[6:7, 32 * k : 32 * k + 32] = own[:, 256:288]


def pack_tiles(rows):
    lane = iota((1, 128), 1)
    last = rows[2]
    for k in (1, 2):
        moved = pltpu.roll(jnp.broadcast_to(rows[3 * k + 2], (8, 128)), 32 * k, 1)[0:1]
        last = jnp.where(lane >= 32 * k, moved, last)
    return [rows[3 * k + span] for k in range(3) for span in range(2)] + [last]


def prescribe(out_ref, cycle_s, column_s, gx):
    lane = iota((ROWS, COLS), 1)

    @pl.when(jnp.logical_or(gx == 0, gx == GX - 1))
    def _():
        turned = jnp.concatenate([column_s[...], jnp.zeros((88, 128), F32)], axis=0).T
        column = jnp.where(gx == 0, turned[0:ROWS, :], turned[ROWS : 2 * ROWS, :])
        at = jnp.where(gx == 0, 0, COLS - 1)
        for f in range(LANES):
            out_ref[f] = jnp.where(lane == at, column[:, f : f + 1], out_ref[f])

    out_ref[:, 0, :] = cycle_s[0]
    out_ref[:, ROWS - 1, :] = cycle_s[1]


def coarse_values(out_ref):
    mean = jnp.where(iota((32, 128), 1) // 4 == iota((32, 128), 0), 1.0 / 16.0, 0.0)
    parts = []
    for i in range(4):
        total = (out_ref[:, 4 * i, :] + out_ref[:, 4 * i + 1, :]) + (
            out_ref[:, 4 * i + 2, :] + out_ref[:, 4 * i + 3, :]
        )
        wide = jnp.concatenate([total, total, total, jnp.zeros((8, 128), F32)], axis=0)
        parts.append(
            lax.dot_general(
                mean,
                wide,
                (((1,), (1,)), ((), ())),
                precision=lax.Precision.HIGHEST,
                preferred_element_type=F32,
            )
        )
    coarse = jnp.concatenate(parts, axis=0)
    plane_of = iota((128, 128), 1) // LANES
    placed = [jnp.where(plane_of == plane, coarse, 0.0) for plane in range(PLANES)]
    return jnp.concatenate(halves(jnp.concatenate(placed, axis=0)), axis=1)


def picked(pick, values):
    both = product(pick, values)
    return both[:, 0:128] + both[:, 128:256]


def unpack_entries(pick_ref, values):
    total = picked(pick_ref[...], jnp.concatenate(halves(values), axis=1))
    entries = total[0:ENTRIES]
    for plane in range(1, PLANES):
        part = total[plane * ENTRIES : (plane + 1) * ENTRIES]
        entries = entries + pltpu.roll(part, 128 - LANES * plane, 1)
    return entries


def place_rows(codes, turned, own):
    code = jnp.broadcast_to(codes, (8, 128))
    index = jnp.bitwise_and(code, 127)
    return [
        jnp.where(code >= 0, take(turned[8 * k : 8 * k + 8], index), own(slice(8 * k, 8 * k + 8)))
        for k in range(FG)
    ]


def feed_back(src_ref, out_ref, turned, map_ref):
    for r in range(ROWS):
        cells = place_rows(map_ref[r : r + 1, :], turned, lambda span: src_ref[span, r, :])
        for k in range(FG):
            out_ref[8 * k : 8 * k + 8, r, :] = cells[k]


def neighbours_of(owner, cell):
    row = jnp.right_shift(cell, 7)
    col = jnp.bitwise_and(cell, 127)
    at = jnp.bitwise_and(owner, GX - 1)
    left = owner - at + jnp.bitwise_and(at + GX - 1, GX - 1)
    right = owner - at + jnp.bitwise_and(at + 1, GX - 1)
    top = jnp.logical_and(row == 0, owner >= GX)
    low = jnp.logical_and(row == ROWS - 1, owner < 2 * GX)
    beside = jnp.where(col == 0, left, jnp.where(col == COLS - 1, right, -1))
    across = jnp.where(top, owner - GX, jnp.where(low, owner + GX, -1))
    diagonal = jnp.where(
        jnp.logical_and(low, col == 0),
        left + GX,
        jnp.where(jnp.logical_and(top, col == COLS - 1), right - GX, -1),
    )
    return owner, beside, across, diagonal


def feedback_routes(owner_ref, cell_ref, pick_ref, map_ref, halo_ref, me):
    cell = cell_ref[...]
    owner = owner_ref[...]
    row = jnp.right_shift(cell, 7)
    col = jnp.bitwise_and(cell, 127)
    own = owner == me
    left = me - lax.rem(me, GX) + lax.rem(me + GX - 1, GX)
    right = me - lax.rem(me, GX) + lax.rem(me + 1, GX)
    above = jnp.logical_and(owner == me - GX, row == ROWS - 1)
    below = jnp.logical_and(owner == me + GX, row == 0)
    target = jnp.where(jnp.logical_and(owner == left, col == COLS - 1), row, -1)
    target = jnp.where(jnp.logical_and(owner == right, col == 0), ROWS + row, target)
    corner = jnp.logical_and(row == ROWS - 1, col == 0)
    target = jnp.where(jnp.logical_and(owner == right - GX, corner), 2 * ROWS, target)
    corner = jnp.logical_and(row == 0, col == COLS - 1)
    target = jnp.where(jnp.logical_and(owner == left + GX, corner), 2 * ROWS + 1, target)
    taken = jnp.logical_or(jnp.logical_or(own, target >= 0), jnp.logical_or(above, below))
    found, total = ranks([taken])
    slot = jnp.minimum(found[0], float(MEANS - 1))
    before = jnp.where(iota((GX, GX), 1) < iota((GX, GX), 0), 1.0, 0.0).astype(jnp.bfloat16)
    entry = found[0] + product(before, total.astype(jnp.bfloat16))
    plane = jnp.floor(slot * (1.0 / DEPTH))
    place = iota((GX, 128), 0).astype(F32) * float(DEPTH) + (slot - float(DEPTH) * plane)
    line = jnp.where(own, row, jnp.where(above, ROWS, jnp.where(below, ROWS + 1, -1)))
    entry = jnp.where(taken, entry, -1.0)
    target = target.astype(F32)
    cells = jnp.zeros((2 * ROWS, 128), F32)
    codes = jnp.zeros((ENTRIES, 128), F32)
    for q in range(GX):
        one = slice(q, q + 1)
        here = jnp.where(iota((2 * ROWS, 128), 0) == line[one], entry[one] + 1.0, 0.0)
        hot = jnp.where(iota((128, 128), 0) == col[one], 1.0, 0.0)
        cells = cells + product(here.astype(jnp.bfloat16), hot.astype(jnp.bfloat16), (1, 1))
        hot = jnp.where(iota((ENTRIES, 128), 0).astype(F32) == entry[one], 1.0, 0.0)
        number = iota((128, 128), 0)
        facts = jnp.where(number == 1, plane[one] + 1.0, 0.0)
        facts = jnp.where(number == 0, place[one], jnp.where(number == 2, target[one] + 1.0, facts))
        codes = codes + product(hot.astype(jnp.bfloat16), facts.astype(jnp.bfloat16), (1, 1))
    map_ref[...] = cells.astype(jnp.int32) - 1
    at = codes[:, 0:1]
    level = codes[:, 1:2] - 1.0
    lane = iota((ENTRIES, 128), 1).astype(F32)
    for p in range(PLANES):
        hot = jnp.where(jnp.where(level == float(p), at, -1.0) == lane, 1.0, 0.0)
        pick_ref[p * ENTRIES : (p + 1) * ENTRIES, :] = hot.astype(jnp.bfloat16)
    goal = codes.T[2:3, :] - 1.0
    halo_ref[...] = jnp.where(iota((3 * ROWS, 128), 0).astype(F32) == goal, 1.0, 0.0).astype(
        jnp.bfloat16
    )


def load_terms(owner_ref, cell_ref, gid_s):
    for k in range(3):
        gid = owner_ref[k] * 2048 + cell_ref[k]
        gid_s[3 * k] = gid[:, 0:128]
        gid_s[3 * k + 1] = gid[:, 128:256]
        gid_s[3 * k + 2] = jnp.full((GX, 128), -1, jnp.int32)
        gid_s[3 * k + 2, :, 0:32] = gid[:, 256:288]


def flag_block(over):
    worst = jnp.max(over, axis=0, keepdims=True)
    flag = jnp.where(worst > 0.5, 1.0, 0.0)
    return jnp.where(iota((8, 128), 1) == 127, jnp.broadcast_to(flag, (8, 128)), 0.0)


def first_kernel(
    x_ref, owner_ref, cell_ref, send_ref, table_ref, last_row_ref, first_row_ref,
    x_s, owner_s, cell_s, gid_s, mark_s, value_s, rows_s, blocks_s, edges_s, in_sems, out_sems, edge_sems,
):
    grp = lax.axis_index("grp")
    gx = lax.axis_index("gx")
    fetch_x = pltpu.make_async_copy(x_ref, x_s, in_sems.at[0])
    fetch_index = [
        pltpu.make_async_copy(owner_ref, owner_s, in_sems.at[1]),
        pltpu.make_async_copy(cell_ref, cell_s, in_sems.at[2]),
    ]

    @pl.when(grp < 3)
    def _():
        for copy in fetch_index:
            copy.start()
        fetch_x.start()
        for copy in fetch_index:
            copy.wait()
        load_terms(owner_s, cell_s, gid_s)
        gids = [gid_s[t] for t in range(TILES)]
        masks = [jnp.right_shift(g, 11) == grp * GX + gx for g in gids]
        values = [jnp.bitwise_and(g, 2047).astype(F32) for g in gids]
        table, _ = slot_table(masks, values, SLOTS, mark_s, value_s)
        table_ref[...] = table.astype(jnp.int32)
        fetch_x.wait()
        send_edges(x_s, edges_s, send_ref, edge_sems, grp, gx)
        last_row_ref[...] = x_s[:, ROWS - 1, :]
        first_row_ref[...] = x_s[:, 0, :]
        for r in range(ROWS):
            rows_s[r] = x_s[:, r, :]
        for copy in send_cells(rows_s, table_ref, blocks_s, send_ref, out_sems):
            copy.wait()

    @pl.when(grp == 3)
    def _():
        fetch_x.start()
        fetch_x.wait()
        send_edges(x_s, edges_s, send_ref, edge_sems, grp, gx)

    wait_edges(edges_s, send_ref, edge_sems, grp, gx)


def tables_kernel(
    x_ref, diff_ref, cor_ref, mix_ref, owner_ref, cell_ref, weight_ref, fb_owner_ref, fb_cell_ref,
    fresh_ref, codes_ref, weights_ref, pick_ref, hits_ref, flag_ref, map_ref, entry_ref, halo_ref,
    gid_s, mark_s, value_s, found_s, seek_s,
):
    grp = lax.axis_index("grp")
    gx = lax.axis_index("gx")
    update(x_ref, fresh_ref, diff_ref, cor_ref, mix_ref)

    @pl.when(grp < 3)
    def _():
        feedback_routes(
            fb_owner_ref, fb_cell_ref, entry_ref, map_ref, halo_ref, grp * GX + gx
        )

    @pl.when(grp == 3)
    def _():
        load_terms(owner_ref, cell_ref, gid_s)
        load_weights(weight_ref, weights_ref, gx)

        number = iota((PARENTS, 128), 0)
        everyone = neighbours_of(fb_owner_ref[...], fb_cell_ref[...])
        back = jnp.zeros((PARENTS, 128), F32)
        for q in range(GX):
            hit = number == everyone[0][q : q + 1, :]
            for other in everyone[1:]:
                hit = jnp.logical_or(hit, number == other[q : q + 1, :])
            back = back + jnp.where(hit, 1.0, 0.0)
        back = jnp.sum(back, axis=1, keepdims=True)

        own_cell = fb_cell_ref[pl.ds(gx, 1), :]
        goals = neighbours_of(fb_owner_ref[pl.ds(gx, 1), :], own_cell)
        number = iota((128, 128), 0)
        hots = [number == goal for goal in goals]
        anyone = jnp.logical_or(jnp.logical_or(hots[0], hots[1]), jnp.logical_or(hots[2], hots[3]))
        found, total = ranks([anyone])
        over = jnp.max(jnp.where(total > float(MEANS), 1.0, 0.0), axis=0, keepdims=True)
        over = jnp.maximum(
            over, jnp.max(jnp.where(back > float(ENTRIES), 1.0, 0.0), axis=0, keepdims=True)
        )
        most = jnp.minimum(jnp.max(total).astype(jnp.int32), 32)
        slots = [
            jnp.sum(jnp.where(h, found[0], 0.0), axis=0, keepdims=True).astype(jnp.int32)
            for h in hots
        ]
        for p in range(PLANES):
            wanted = [
                jnp.where(
                    jnp.logical_and(goal >= 0, slot // DEPTH == p), goal * DEPTH + slot % DEPTH, -1
                )
                for goal, slot in zip(goals, slots)
            ]
            for part in range(MEAN_ROWS // 128):
                line = number + 128 * part
                hit = line == wanted[0]
                for other in wanted[1:]:
                    hit = jnp.logical_or(hit, line == other)
                pick_ref[128 * part : 128 * part + 128, 128 * p : 128 * p + 128] = jnp.where(
                    hit, 1.0, 0.0
                ).astype(jnp.bfloat16)
        hot, rank = hots[0], slots[0]

        owners = [jnp.right_shift(gid_s[t, pl.ds(gx, 1), :], 11) for t in range(TILES)]
        hots = [iota((PARENTS, 128), 0) == o for o in owners]
        found, total = ranks(hots)
        over = jnp.maximum(
            over, jnp.max(jnp.where(total > float(SLOTS), 1.0, 0.0), axis=0, keepdims=True)
        )
        codes = []
        for t in range(TILES):
            slot = jnp.sum(jnp.where(hots[t], found[t], 0.0), axis=0, keepdims=True)
            slot = jnp.minimum(slot.astype(jnp.int32), SLOTS - 1)
            group = jnp.right_shift(owners[t] * 205, 10)
            codes.append(group * 128 + (owners[t] - 5 * group) * SLOTS + slot)
        for t, code in enumerate(pack_tiles(codes)):
            codes_ref[t : t + 1, :] = code

        hot = jnp.where(hot, 1.0, 0.0).astype(jnp.bfloat16)
        chosen = iota((32, 128), 0) == rank

        def by_owner(values):
            picked = jnp.where(chosen, values.astype(F32), 0.0).astype(jnp.bfloat16)
            return product(picked, hot, (1, 1)).astype(jnp.int32)

        number = by_owner(iota((1, 128), 1) + 1)
        cells = by_owner(jnp.right_shift(own_cell, 4)) * 16 + by_owner(jnp.bitwise_and(own_cell, 15))
        seek_s[...] = jnp.where(number > 0, cells * 256 + number - 1, -1)
        found_s[...] = jnp.full((TILES, GX, 128), -1, jnp.int32)

        def seek(j, carry):
            line = jnp.broadcast_to(seek_s[pl.ds(j, 1), :], (8, 128))
            for t in range(TILES):
                for part in range(GX // 8):
                    span = slice(8 * part, 8 * part + 8)
                    gid = gid_s[t, span, :]
                    entry = take(line, jnp.bitwise_and(jnp.right_shift(gid, 11), 127))
                    same = jnp.right_shift(entry, 8) == jnp.bitwise_and(gid, 2047)
                    found_s[t, span, :] = jnp.where(
                        same, jnp.bitwise_and(entry, 255), found_s[t, span, :]
                    )
            return carry

        lax.fori_loop(0, most, seek, 0)
        found_at = [found_s[t] for t in range(TILES)]
        table, total = slot_table(
            [f >= 0 for f in found_at], [f.astype(F32) for f in found_at], HITS, mark_s, value_s
        )
        over = jnp.maximum(
            over, jnp.max(jnp.where(total > float(HITS), 1.0, 0.0), axis=0, keepdims=True)
        )
        turned = jnp.concatenate([table, jnp.zeros((96, 128), F32)], axis=0).T
        lane = iota((8, 128), 1).astype(F32)
        for pair in range(GX // 2):
            hits = [
                jnp.where(turned[0:HITS, q : q + 1] == lane, 1.0, 0.0)
                for q in (2 * pair, 2 * pair + 1)
            ]
            line = slice(16 * pair, 16 * pair + 16)
            hits_ref[line, :] = jnp.concatenate(hits, axis=0).astype(jnp.bfloat16)
        flag_ref[...] = flag_block(over)


def second_kernel(
    recv_ref, fresh_ref, diff_ref, above_ref, below_ref, first_ref, last_ref, weights_ref, table_ref,
    codes_ref, pick_ref, hits_ref, flag_ref, out_ref, send_ref, last_row_ref, first_row_ref,
    rows_s, group_s, cycle_s, column_s, blocks_s, edges_s, out_sems, edge_sems,
):
    grp = lax.axis_index("grp")
    gx = lax.axis_index("gx")
    add_columns(fresh_ref, out_ref, gather_halo(recv_ref, grp, gx), diff_ref, grp, gx)

    @pl.when(grp < 3)
    def _():
        add_rows(first_ref, last_ref, out_ref, above_ref, below_ref, diff_ref, grp)
        send_edges(out_ref, edges_s, send_ref, edge_sems, grp, gx)
        last_row_ref[...] = out_ref[:, ROWS - 1, :]
        first_row_ref[...] = out_ref[:, 0, :]
        for r in range(ROWS):
            rows_s[r] = out_ref[:, r, :]
        for copy in send_cells(rows_s, table_ref, blocks_s, send_ref, out_sems):
            copy.wait()
        wait_edges(edges_s, send_ref, edge_sems, grp, gx)

    @pl.when(grp == 3)
    def _():
        regroup(recv_ref, group_s)
        interpolate(codes_ref, weights_ref, group_s, PGROUPS, cycle_s, column_s)
        prescribe(out_ref, cycle_s, column_s, gx)
        values = coarse_values(out_ref)
        base = flag_ref[0:1, :]
        sent = picked(pick_ref[...], values) + base
        for j in range(PARENTS // 2):
            tile = sent[8 * j : 8 * j + 8]
            blocks_s[16 * j : 16 * j + 8, :] = tile
            blocks_s[16 * j + 8 : 16 * j + 16, :] = pltpu.roll(tile, DEPTH, 0)
        copies = [
            pltpu.make_async_copy(blocks_s.at[rows, :], send_ref.at[rows, :], out_sems.at[i])
            for i, rows in enumerate((pl.ds(0, SENT), pl.ds(SENT, TAKEN)))
        ]
        copies[0].start()
        blocks_s[SENT : SENT + TAKEN, :] = picked(hits_ref[...], values[0:128]) + base
        right = rows_of(PARENTS + lax.rem(gx + 1, GX))
        left = rows_of(PARENTS + lax.rem(gx + GX - 1, GX))
        blocks_s[right, :] = blocks_s[right, :] + edge_block(out_ref, COLS - 1)
        blocks_s[left, :] = blocks_s[left, :] + edge_block(out_ref, 0)
        copies[1].start()
        for copy in copies:
            copy.wait()


def hits_kernel(
    x_ref, diff_ref, cor_ref, mix_ref, owner_ref, cell_ref, fb_owner_ref, fb_cell_ref, plain_ref,
    fresh_ref, codes_ref, gid_s, turned_s,
):
    gx = lax.axis_index("gx")

    @pl.when(lax.axis_index("grp") == 3)
    def _():
        update(x_ref, fresh_ref, diff_ref, cor_ref, mix_ref)
        load_terms(owner_ref, cell_ref, gid_s)
        terms = [gid_s[t, pl.ds(gx, 1), :] for t in range(TILES)]
        fed = (fb_owner_ref[...] * 2048 + fb_cell_ref[...]).astype(F32)
        turned_s[...] = jnp.concatenate([fed, jnp.full((96, 128), -2.0, F32)], axis=0).T
        wide = [jnp.broadcast_to(t.astype(F32), (8, 128)) for t in terms]

        def match(q, from_block):
            column = pltpu.roll(turned_s[...], lax.rem(128 - q, 128), 1)[:, 0:1]
            for s in range(16):
                part = jnp.broadcast_to(column[8 * s : 8 * s + 8, :], (8, 128))
                from_block = [jnp.where(part == w, q, f) for w, f in zip(wide, from_block)]
            return from_block

        none = [jnp.full((8, 128), -1, jnp.int32) for _ in range(TILES)]
        from_block = lax.fori_loop(0, GX, match, none)
        sources = [jnp.max(f, axis=0, keepdims=True) for f in from_block]
        hots = [iota((GX, 128), 0) == s for s in sources]
        found, _ = ranks(hots)
        codes = []
        for t in range(TILES):
            slot = jnp.sum(jnp.where(hots[t], found[t], 0.0), axis=0, keepdims=True)
            slot = jnp.minimum(slot.astype(jnp.int32), HITS - 1)
            code = (PGROUPS + jnp.right_shift(sources[t], 4)) * 128
            code = code + jnp.bitwise_and(sources[t], 15) * HITS + slot
            codes.append(jnp.where(sources[t] >= 0, code, -1))
        for t, code in enumerate(pack_tiles(codes)):
            plain = plain_ref[t : t + 1, :]
            codes_ref[t : t + 1, :] = jnp.where(code >= 0, code, plain)


def third_kernel(
    recv_ref, x_ref, fresh_ref, diff_ref, weights_ref, codes_ref, pick_ref, map_ref, entry_ref,
    halo_ref, above_ref, below_ref, out_ref, send_ref, flag_ref, rims_ref, halos_ref,
    group_s, cycle_s, column_s, blocks_s, out_sem,
):
    grp = lax.axis_index("grp")
    gx = lax.axis_index("gx")
    flag = recv_ref[SENT : SENT + 8, :]
    for q in range(1, GX):
        flag = jnp.maximum(flag, recv_ref[SENT + 8 * q : SENT + 8 * q + 8, :])
    flag_ref[...] = flag

    @pl.when(grp < 3)
    def _():
        upper = iota((8, 128), 0) < DEPTH
        tiles = []
        for j in range(GX // 2):
            even = recv_ref[SENT + 16 * j : SENT + 16 * j + 8, :]
            odd = recv_ref[SENT + 16 * j + 8 : SENT + 16 * j + 16, :]
            tiles.append(jnp.where(upper, even, pltpu.roll(odd, DEPTH, 0)))
        entries = unpack_entries(entry_ref, jnp.concatenate(tiles, axis=0))
        turned = entries.T
        feed_back(x_ref, out_ref, turned, map_ref)
        for k, cells in enumerate(
            place_rows(map_ref[ROWS : ROWS + 1, :], turned, lambda span: above_ref[span, :])
        ):
            rims_ref[0, 8 * k : 8 * k + 8, :] = cells
        for k, cells in enumerate(
            place_rows(map_ref[ROWS + 1 : ROWS + 2, :], turned, lambda span: below_ref[span, :])
        ):
            rims_ref[1, 8 * k : 8 * k + 8, :] = cells
        hot = halo_ref[...]
        moved = jnp.concatenate(halves(pltpu.roll(entries, EDGE, 1)), axis=1)
        fed = jnp.sum(hot.astype(F32), axis=1, keepdims=True) > 0.5
        before = jnp.concatenate(gather_halo(recv_ref, grp, gx), axis=0)
        halos_ref[...] = jnp.where(fed, picked(hot, moved), before)

    @pl.when(grp == 3)
    def _():
        add_columns(fresh_ref, out_ref, gather_halo(recv_ref, grp, gx), diff_ref, grp, gx)
        regroup(recv_ref, group_s)
        regroup_hits(recv_ref, group_s)
        interpolate(codes_ref, weights_ref, group_s, GROUPS, cycle_s, column_s)
        prescribe(out_ref, cycle_s, column_s, gx)
        blocks_s[...] = picked(pick_ref[...], coarse_values(out_ref))
        copy = pltpu.make_async_copy(blocks_s, send_ref.at[pl.ds(0, MEAN_ROWS), :], out_sem.at[0])
        copy.start()
        copy.wait()


def parents_kernel(x_ref, diff_ref, cor_ref, mix_ref, rims_ref, halos_ref, fresh_ref):
    grp = lax.axis_index("grp")

    @pl.when(grp < 3)
    def _():
        update(x_ref, fresh_ref, diff_ref, cor_ref, mix_ref)
        halo = (halos_ref[0:ROWS, :], halos_ref[ROWS : 2 * ROWS, :], halos_ref[2 * ROWS : 3 * ROWS, :])
        add_columns(fresh_ref, fresh_ref, halo, diff_ref, grp, lax.axis_index("gx"))
        first = x_ref[:, 0, :]
        last = x_ref[:, ROWS - 1, :]
        add_rows(first, last, fresh_ref, rims_ref[0], rims_ref[1], diff_ref, grp)


def fourth_kernel(recv_ref, x_ref, fresh_ref, map_ref, entry_ref, out_ref):
    grp = lax.axis_index("grp")

    @pl.when(grp < 3)
    def _():
        entries = unpack_entries(entry_ref, recv_ref[MEAN_ROWS : MEAN_ROWS + 128, :])
        feed_back(fresh_ref, out_ref, entries.T, map_ref)

    @pl.when(grp == 3)
    def _():
        out_ref[...] = x_ref[...]


def call(kernel, name, ins, spaces, outs, out_spaces, scratch, sems=()):
    space = {"s": pltpu.SMEM, "v": pltpu.VMEM, "a": pl.ANY}
    return pl.pallas_call(
        kernel,
        name=name,
        in_specs=[pl.BlockSpec(memory_space=space[s]) for s in spaces],
        out_specs=[pl.BlockSpec(memory_space=space[s]) for s in out_spaces],
        out_shape=[jax.ShapeDtypeStruct(s, d) for s, d in outs],
        scratch_shapes=[pltpu.VMEM(s, d) for s, d in scratch]
        + [pltpu.SemaphoreType.DMA((n,)) for n in sems],
        compiler_params=pltpu.CompilerParams(vmem_limit_bytes=VMEM_LIMIT),
        cost_estimate=pl.CostEstimate(flops=1000000, bytes_accessed=4000000, transcendentals=0),
    )(*ins)


STATE = ((LANES, ROWS, COLS), F32)
BLOCKS = ((DEVICES * 8, 128), F32)
BLOCK = ((8, 128), F32)
RIM = ((LANES, COLS), F32)
ROWMAJOR = ((ROWS, LANES, COLS), F32)
MAP = ((2 * ROWS, 128), jnp.int32)
GIDS = ((TILES, GX, 128), jnp.int32)
TERMS = ((TILES, GX, 128), F32)
PICK = ((MEAN_ROWS, PLANES * 128), jnp.bfloat16)
HIT = ((TAKEN, 128), jnp.bfloat16)
ENTRY = ((PLANES * ENTRIES, 128), jnp.bfloat16)
HALO = ((3 * ROWS, 128), jnp.bfloat16)
HALOS = ((3 * ROWS, 128), F32)
RIMS = ((2, LANES, COLS), F32)
THIN = ((DEVICES * DEPTH, 128), F32)
GROUPED = ((GROUPS, LANES, 128), F32)
CYCLE = ((2, LANES, 128), F32)
TABLE = ((GX, 128), jnp.int32)
CODES = ((8, 128), jnp.int32)
INDEX = ((3, GX, PERIM), jnp.int32)
EDGES = ((16, 128), F32)
TO_NEST = ((TAKEN, 128), F32)


def exchange(blocks):
    return lax.all_to_all(blocks, ("grp", "gx"), 0, 0, tiled=True)


def rims(last_row, first_row):
    above = lax.ppermute(last_row, "grp", [(0, 1), (1, 2)])
    below = lax.ppermute(first_row, "grp", [(1, 0), (2, 1)])
    return above, below


def shards(atmosphere, diffusion, coriolis, mixing, owner, cell, weight, fb_owner, fb_cell):
    inputs = (atmosphere, diffusion, coriolis, mixing, owner, cell, weight, fb_owner, fb_cell)
    owner, cell, weight = (jnp.transpose(a, (1, 0, 2)) for a in (owner, cell, weight))
    physics = (diffusion, coriolis, mixing)
    send, table, last_row, first_row = call(
        first_kernel,
        "first_cells",
        (atmosphere, owner, cell),
        "aaa",
        (BLOCKS, TABLE, RIM, RIM),
        "avvv",
        (STATE, INDEX, INDEX, GIDS, TERMS, TERMS, ROWMAJOR, TO_NEST, EDGES),
        (3, 7, 4),
    )
    recv = exchange(send)
    above, below = rims(last_row, first_row)
    fresh, codes, weights, pick, hits, flag, place, entry, halo = call(
        tables_kernel,
        "tables",
        (atmosphere,) + physics + (owner, cell, weight, fb_owner, fb_cell),
        "vvssvvvvv",
        (STATE, CODES, BLOCK, PICK, HIT, BLOCK, MAP, ENTRY, HALO),
        "vvvvvvvvv",
        (GIDS, TERMS, TERMS, GIDS, ((32, 128), jnp.int32)),
    )
    state, send, next_last, next_first = call(
        second_kernel,
        "substep_one",
        (recv, fresh, diffusion, above, below, first_row, last_row, weights, table, codes, pick, hits, flag),
        "v" * 13,
        (STATE, BLOCKS, RIM, RIM),
        "vavv",
        (ROWMAJOR, GROUPED, CYCLE, RIM, BLOCKS, EDGES),
        (7, 4),
    )
    recv = exchange(send)
    above, below = rims(next_last, next_first)
    fresh, codes = call(
        hits_kernel,
        "hits",
        (state,) + physics + (owner, cell, fb_owner, fb_cell, codes),
        "vvssvvvvv",
        (STATE, CODES),
        "vv",
        (GIDS, ((128, 128), F32)),
    )
    state, send, flag, edge_rows, halos = call(
        third_kernel,
        "substep_two",
        (recv, state, fresh, diffusion, weights, codes, pick, place, entry, halo, above, below),
        "v" * 12,
        (STATE, THIN, BLOCK, RIMS, HALOS),
        "vavvv",
        (GROUPED, CYCLE, RIM, ((MEAN_ROWS, 128), F32)),
        (1,),
    )
    recv = exchange(send)
    (fresh,) = call(
        parents_kernel,
        "parents",
        (state,) + physics + (edge_rows, halos),
        "vvssvv",
        (STATE,),
        "v",
        (),
    )
    (state,) = call(
        fourth_kernel,
        "finish",
        (recv, state, fresh, place, entry),
        "v" * 5,
        (STATE,),
        "v",
        (),
    )
    return lax.cond(flag[0, 127] > 0.5, lambda s, *a: dense_plan(*a), lambda s, *a: s, state, *inputs)


def solution(mesh):
    placed = (P(None, "grp", "gx"), P("grp", "gx"), P("grp"), P(), P(), P(), P(), P(), P())
    return jax.shard_map(
        shards, mesh=mesh, in_specs=placed, out_specs=P(None, "grp", "gx"), check_vma=False
    )
```

```python
import jax
import jax.numpy as jnp
from jax import lax
from jax.experimental import pallas as pl
from jax.experimental.pallas import tpu as pltpu
from jax.sharding import PartitionSpec as P

SUBSTEPS = 2
F32 = jnp.float32
LANES = 40
ROWS = 16
COLS = 128
LEVELS = 10
GX = 32
PARENTS = 96
DEVICES = 128
PERIM = 288
TILES = 7
SLOTS = 25
HITS = 8
EDGE = 40
FG = 5
PGROUPS = 20
GROUPS = 22
ENTRIES = 128
PLANES = 3
DEPTH = 4
MEANS = DEPTH * PLANES
MEAN_ROWS = PARENTS * DEPTH
SENT = PARENTS * 8
TAKEN = GX * 8
VMEM_LIMIT = 24 * 1024 * 1024


def padded(cells, sides, width):
    for axis, dim in sides:
        count = lax.axis_size(axis)
        head = lax.slice_in_dim(cells, 0, width, axis=dim)
        tail = lax.slice_in_dim(cells, cells.shape[dim] - width, cells.shape[dim], axis=dim)
        cells = jnp.concatenate(
            [
                lax.ppermute(tail, axis, [(i, (i + 1) % count) for i in range(count)]),
                cells,
                lax.ppermute(head, axis, [((i + 1) % count, i) for i in range(count)]),
            ],
            axis=dim,
        )
    return cells


def broadcast(value, axis, source):
    kept = jnp.where(lax.axis_index(axis) == source, value, 0).astype(value.dtype)
    for other in range(lax.axis_size(axis)):
        if other != source:
            kept = kept + lax.ppermute(jnp.where(lax.axis_index(axis) == source, value, 0), axis, [(source, other)])
    return kept


def gather_columns(value, axis):
    count = lax.axis_size(axis)
    copies = jnp.broadcast_to(value[None], (count,) + value.shape)
    blocks = lax.all_to_all(copies, axis, 0, 0, tiled=True)
    return blocks.transpose(1, 0, 2).reshape(value.shape[0], -1)


def reduce_cycle(terms, column_count, group_count):
    blocks = terms.reshape(terms.shape[0], column_count, -1).transpose(1, 0, 2)
    partial = lax.all_to_all(blocks, "gx", 0, 0, tiled=True).sum(axis=0)
    total = partial
    for group in range(group_count - 1):
        total = total + lax.ppermute(partial, "grp", [(group, group_count - 1)])
    return total


def advance(extended, center, diffusion, coriolis, mixing):
    neighbours = (
        extended[:, 1:-1, :-2]
        + extended[:, 1:-1, 2:]
        + extended[:, :-2, 1:-1]
        + extended[:, 2:, 1:-1]
        + extended[:, :-2, 2:]
        + extended[:, 2:, :-2]
    )
    laplace = neighbours - 6.0 * center
    lane_count, row_count, col_count = center.shape
    level_count = mixing.shape[0]
    stacked = center.reshape(lane_count // level_count, level_count, row_count, col_count)
    upper = jnp.concatenate([stacked[:, 1:], stacked[:, -1:]], axis=1)
    lower = jnp.concatenate([stacked[:, :1], stacked[:, :-1]], axis=1)
    vertical = mixing[None, :, None, None] * (upper - 2.0 * stacked + lower)
    rotation = jnp.concatenate(
        [
            (coriolis[:, None] * stacked[1])[None],
            (-coriolis[:, None] * stacked[0])[None],
            jnp.zeros_like(stacked[2:]),
        ],
        axis=0,
    )
    return center + diffusion * laplace + (vertical + rotation).reshape(center.shape)


def dense_plan(
    atmosphere,
    diffusion,
    coriolis,
    mixing,
    stencil_owner,
    stencil_cell,
    stencil_weight,
    feedback_owner,
    feedback_cell,
):
    lane_count, row_count, col_count = atmosphere.shape
    cell_count = row_count * col_count
    column_count = lax.axis_size("gx")
    group_count = lax.axis_size("grp")
    group_index = lax.axis_index("grp")
    column_index = lax.axis_index("gx")
    own_rank = group_index * column_count + column_index
    is_nested = group_index == group_count - 1
    perimeter = stencil_owner.shape[2]
    owner_flat = feedback_owner.reshape(-1)
    target_flat = feedback_cell.reshape(-1)
    current = atmosphere
    for substep in range(SUBSTEPS):
        flat_now = current.reshape(lane_count, cell_count)
        cycle_terms = jnp.zeros((lane_count, column_count * perimeter), jnp.float32)
        for member in range(stencil_owner.shape[1]):
            mine = stencil_owner[:, member, :].reshape(-1) == own_rank
            positions = jnp.where(mine, stencil_cell[:, member, :].reshape(-1), 0)
            weights = jnp.where(mine, stencil_weight[:, member, :].reshape(-1), 0.0)
            cycle_terms = cycle_terms + jnp.take(flat_now, positions, axis=1) * weights
        cycle = reduce_cycle(cycle_terms, column_count, group_count)
        extended = padded(current, (("grp", 1), ("gx", 2)), 1)
        upper_rim = jnp.where(group_index == 0, extended[:, 1:2, :], extended[:, 0:1, :])
        lower_rim = jnp.where(
            group_index == group_count - 2, extended[:, -2:-1, :], extended[:, -1:, :]
        )
        extended = jnp.concatenate([upper_rim, extended[:, 1:-1, :], lower_rim], axis=1)
        fresh = advance(extended, current, diffusion, coriolis, mixing)
        left_edge = jnp.where(
            column_index == 0, cycle[:, 2 * col_count : 2 * col_count + row_count], fresh[:, :, 0]
        )
        right_edge = jnp.where(
            column_index == column_count - 1, cycle[:, 2 * col_count + row_count :], fresh[:, :, -1]
        )
        framed = fresh.at[:, :, 0].set(left_edge).at[:, :, -1].set(right_edge)
        framed = (
            framed.at[:, 0, :]
            .set(cycle[:, :col_count])
            .at[:, -1, :]
            .set(cycle[:, col_count : 2 * col_count])
        )
        fresh = jnp.where(is_nested, framed, fresh)
        coarse = fresh.reshape(lane_count, row_count // 4, 4, col_count // 4, 4).mean(axis=(2, 4))
        coarse = coarse.reshape(lane_count, -1)
        fresh_flat = fresh.reshape(lane_count, cell_count)
        shared = broadcast(coarse, "grp", group_count - 1)
        place_positions = jnp.where(owner_flat == own_rank, target_flat, cell_count)
        result_flat = fresh_flat.at[:, place_positions].set(
            gather_columns(shared, "gx"), mode="drop"
        )
        current = result_flat.reshape(lane_count, row_count, col_count)
    return current


def iota(shape, dim):
    return lax.broadcasted_iota(jnp.int32, shape, dim)


def rows_of(device):
    return pl.ds(pl.multiple_of(8 * device, 8), 8)


def take(tile, index):
    return jnp.take_along_axis(tile, index, axis=1, mode="promise_in_bounds")


def halves(values):
    high = values.astype(jnp.bfloat16)
    return high, (values - high.astype(F32)).astype(jnp.bfloat16)


def product(left, right, contract=(1, 0)):
    dims = (((contract[0],), (contract[1],)), ((), ()))
    return lax.dot_general(left, right, dims, preferred_element_type=F32)


def ranks(masks):
    rows = masks[0].shape[0]
    stacked = jnp.concatenate([jnp.where(m, 1.0, 0.0) for m in masks], axis=0)
    stacked = stacked.astype(jnp.bfloat16)
    before = jnp.where(iota((128, 128), 0) < iota((128, 128), 1), 1.0, 0.0).astype(jnp.bfloat16)
    ones = jnp.ones((128, 128), jnp.bfloat16)
    within = product(stacked, before)
    totals = product(stacked, ones)
    carry = jnp.zeros((rows, 128), F32)
    found = []
    for t in range(len(masks)):
        found.append(within[t * rows : (t + 1) * rows] + carry)
        carry = carry + totals[t * rows : (t + 1) * rows]
    return found, carry


def slot_table(masks, values, slots, mark_s, value_s):
    found, total = ranks(masks)
    for t in range(TILES):
        mark_s[t] = jnp.where(masks[t], found[t], -1.0)
        value_s[t] = values[t]
    slot_of = lax.rem(iota((8, 128), 1), slots)
    parts = []
    for part in range(GX // 8):
        span = slice(8 * part, 8 * part + 8)
        marks = [mark_s[t, span, :] for t in range(TILES)]
        vals = [value_s[t, span, :] for t in range(TILES)]
        table = jnp.zeros((8, 128), F32)
        for j in range(slots):
            picked = [jnp.where(m == float(j), v, 0.0) for m, v in zip(marks, vals)]
            while len(picked) > 1:
                picked = [sum(picked[k + 1 : k + 2], picked[k]) for k in range(0, len(picked), 2)]
            table = jnp.where(slot_of == j, jnp.sum(picked[0], axis=1, keepdims=True), table)
        parts.append(table)
    return jnp.concatenate(parts, axis=0), total


def swap_segments(tiles):
    segment = iota((8, 128), 1) // SLOTS
    moved = {}
    for shift in range(1 - FG, FG):
        diagonal = None
        for s in range(FG):
            if 0 <= s + shift < FG:
                tile = tiles[s + shift]
                diagonal = tile if diagonal is None else jnp.where(segment == s, tile, diagonal)
        by = (SLOTS * shift) % 128
        moved[shift] = diagonal if by == 0 else pltpu.roll(diagonal, by, 1)
    results = []
    for s in range(FG):
        result = moved[-s]
        for a in range(1, FG):
            result = jnp.where(segment == a, moved[a - s], result)
        results.append(result)
    return results


def send_cells(rows_s, table_ref, blocks_s, send_ref, sems):
    copies = []
    lane = iota((8, 128), 1)
    group_of = lane // SLOTS
    table = table_ref[0:GX, :]
    for g in range(7):
        index = jnp.zeros((1, 128), jnp.int32)
        members = [q for q in range(5 * g, 5 * g + 5) if q < GX]
        for q in members:
            index = jnp.where(group_of[0:1] == q - 5 * g, table[q : q + 1, :], index)
        index = jnp.broadcast_to(index, (8, 128))
        col = jnp.bitwise_and(index, 127)
        row = jnp.right_shift(index, 7)
        cells = [jnp.zeros((8, 128), F32) for _ in range(FG)]
        for r in range(ROWS):
            here = row == r
            for k in range(FG):
                cells[k] = jnp.where(here, take(rows_s[r, 8 * k : 8 * k + 8, :], col), cells[k])
        blocks = swap_segments(cells)
        for q in members:
            blocks_s[8 * q : 8 * q + 8, :] = blocks[q - 5 * g]
        span = pl.ds(8 * members[0], 8 * len(members))
        rows = pl.ds(SENT + 8 * members[0], 8 * len(members))
        copies.append(pltpu.make_async_copy(blocks_s.at[span, :], send_ref.at[rows, :], sems.at[g]))
        copies[-1].start()
    return copies


def edge_block(x_ref, col):
    lane = iota((8, 128), 1)
    block = jnp.zeros((8, 128), F32)
    for h in range(2):
        for f in range(LANES):
            edge = x_ref[f, 8 * h : 8 * h + 8, col : col + 1]
            block = jnp.where(lane == EDGE + h * LANES + f, edge, block)
    return block


def edge_copies(edges_s, send_ref, sems, grp, gx):
    right = lax.rem(gx + 1, GX)
    left = lax.rem(gx + GX - 1, GX)
    above = jnp.where(grp == 3, 3, jnp.maximum(grp - 1, 0))
    below = jnp.where(grp == 3, 3, jnp.minimum(grp + 1, 2))
    first, last = edges_s.at[0:8, :], edges_s.at[8:16, :]
    plan = [
        (last, grp * GX + right),
        (first, grp * GX + left),
        (last, above * GX + right),
        (first, below * GX + left),
    ]
    return [
        pltpu.make_async_copy(source, send_ref.at[rows_of(to), :], sems.at[i])
        for i, (source, to) in enumerate(plan)
    ]


def send_edges(x_ref, edges_s, send_ref, sems, grp, gx):
    edges_s[0:8, :] = edge_block(x_ref, 0)
    edges_s[8:16, :] = edge_block(x_ref, COLS - 1)
    near = edge_copies(edges_s, send_ref, sems, grp, gx)
    for copy in near[:2]:
        copy.start()

    @pl.when(jnp.logical_or(grp == 1, grp == 2))
    def _():
        near[2].start()

    @pl.when(grp < 2)
    def _():
        near[3].start()


def wait_edges(edges_s, send_ref, sems, grp, gx):
    near = edge_copies(edges_s, send_ref, sems, grp, gx)
    for copy in near[:2]:
        copy.wait()

    @pl.when(jnp.logical_or(grp == 1, grp == 2))
    def _():
        near[2].wait()

    @pl.when(grp < 2)
    def _():
        near[3].wait()


def unpack_edge(block):
    return jnp.concatenate([block, pltpu.roll(block, 128 - LANES, 1)], axis=0)


def update(x_ref, out_ref, diff_ref, cor_ref, mix_ref):
    lane = iota((ROWS, COLS), 1)
    row = iota((ROWS, COLS), 0)
    diff = diff_ref[...]
    cor = jnp.zeros((ROWS, COLS), F32)
    for r in range(ROWS):
        cor = jnp.where(row == r, cor_ref[r], cor)
    for f in range(LANES):
        level = f % LEVELS
        x = x_ref[f]
        up = jnp.where(row == 0, 0.0, pltpu.roll(x, 1, 0))
        down = jnp.where(row == ROWS - 1, 0.0, pltpu.roll(x, ROWS - 1, 0))
        westward = jnp.where(lane == 0, 0.0, pltpu.roll(x + down, 1, 1))
        eastward = jnp.where(lane == COLS - 1, 0.0, pltpu.roll(x + up, COLS - 1, 1))
        laplace = (westward + eastward) + (up + down) - 6.0 * x
        upper = x if level == LEVELS - 1 else x_ref[f + 1]
        lower = x if level == 0 else x_ref[f - 1]
        extra = mix_ref[level] * (upper - 2.0 * x + lower)
        if f < LEVELS:
            extra = extra + cor * x_ref[f + LEVELS]
        elif f < 2 * LEVELS:
            extra = extra - cor * x_ref[f - LEVELS]
        out_ref[f] = x + diff * laplace + extra


def gather_halo(recv_ref, grp, gx):
    right = lax.rem(gx + 1, GX)
    left = lax.rem(gx + GX - 1, GX)
    from_left = unpack_edge(recv_ref[rows_of(grp * GX + left), :])
    from_right = unpack_edge(recv_ref[rows_of(grp * GX + right), :])
    top_right = unpack_edge(recv_ref[rows_of(jnp.maximum(grp - 1, 0) * GX + right), :])
    low_left = unpack_edge(recv_ref[rows_of(jnp.minimum(grp + 1, 3) * GX + left), :])
    row = iota((ROWS, COLS), 0)
    corners = jnp.where(row == 0, top_right[ROWS - 1 : ROWS], low_left[0:1])
    return from_left, from_right, corners


def add_columns(from_ref, out_ref, halo, diff_ref, grp, gx):
    from_left, from_right, corners = halo
    nest = grp == 3
    lane = iota((ROWS, COLS), 1)
    row = iota((ROWS, COLS), 0)
    top_right = jnp.where(grp == 0, from_right[0:1], corners[0:1])
    low_left = jnp.where(grp == 2, from_left[ROWS - 1 : ROWS], corners[1:2])
    top_right = jnp.where(nest, 0.0, top_right)
    low_left = jnp.where(nest, 0.0, low_left)
    left_sum = from_left + jnp.where(row == ROWS - 1, low_left, pltpu.roll(from_left, ROWS - 1, 0))
    right_sum = from_right + jnp.where(row == 0, top_right, pltpu.roll(from_right, 1, 0))
    left_sum = jnp.where(jnp.logical_and(nest, gx == 0), 0.0, left_sum)
    right_sum = jnp.where(jnp.logical_and(nest, gx == GX - 1), 0.0, right_sum)
    diff = diff_ref[...]
    left_sum = left_sum * diff[:, 0:1]
    right_sum = right_sum * diff[:, COLS - 1 : COLS]
    source = jnp.bitwise_and(EDGE + jnp.right_shift(lane + 1, 1), 127)
    spread = jnp.concatenate(
        [
            jnp.where(
                jnp.bitwise_and(lane[0:8], 1) == 0,
                take(left_sum[h : h + 8], source[0:8]),
                take(right_sum[h : h + 8], jnp.where(lane[0:8] == 127, EDGE, source[0:8])),
            )
            for h in (0, 8)
        ],
        axis=0,
    )
    outer = jnp.logical_or(lane == 0, lane == COLS - 1)
    for f in range(LANES):
        moved = spread if f == 0 else pltpu.roll(spread, 128 - 2 * f, 1)
        out_ref[f] = from_ref[f] + jnp.where(outer, moved, 0.0)


def add_rows(first_ref, last_ref, out_ref, above_ref, below_ref, diff_ref, grp):
    lane = iota((LANES, COLS), 1)
    above = jnp.where(grp == 0, first_ref[...], above_ref[...])
    below = jnp.where(grp == 2, last_ref[...], below_ref[...])
    above = above + jnp.where(lane == COLS - 1, 0.0, pltpu.roll(above, COLS - 1, 1))
    below = below + jnp.where(lane == 0, 0.0, pltpu.roll(below, 1, 1))
    out_ref[:, 0, :] = out_ref[:, 0, :] + diff_ref[0:1, :] * above
    out_ref[:, ROWS - 1, :] = out_ref[:, ROWS - 1, :] + diff_ref[ROWS - 1 : ROWS, :] * below


def chunks(count, step, body):
    def run(c, carry):
        for s in range(step):
            body(c * step + s)
        return carry

    lax.fori_loop(0, count // step, run, 0)


def regroup(recv_ref, group_s):
    def body(g):
        tiles = swap_segments([recv_ref[rows_of(g * 5 + i), :] for i in range(5)])
        for k in range(FG):
            group_s[g, 8 * k : 8 * k + 8, :] = tiles[k]

    chunks(PGROUPS, 4, body)


def regroup_hits(recv_ref, group_s):
    for h in range(2):
        first = SENT + 128 * h
        group_s[PGROUPS + h] = recv_ref[first : first + 128, :].T[0:LANES]


def interpolate(codes_ref, weight_s, group_s, groups, cycle_s, column_s):
    def cells_of(t):
        code = jnp.broadcast_to(codes_ref[pl.ds(t, 1), :], (8, 128))
        index = jnp.bitwise_and(code, 127)
        group = jnp.right_shift(code, 7)
        weight = weight_s[pl.ds(t, 1), :]
        cells = [jnp.zeros((8, 128), F32) for _ in range(FG)]
        for g in range(groups):
            here = group == g
            for k in range(FG):
                cells[k] = jnp.where(here, take(group_s[g, 8 * k : 8 * k + 8, :], index), cells[k])
        return [weight * c for c in cells]

    cycle_s[...] = jnp.zeros((2, LANES, 128), F32)

    def body(t):
        span = jnp.bitwise_and(t, 1)
        for k, cells in enumerate(cells_of(t)):
            cycle_s[span, 8 * k : 8 * k + 8, :] += cells

    chunks(6, 1, body)
    for k, cells in enumerate(cells_of(6)):
        total = cells + pltpu.roll(cells, 96, 1) + pltpu.roll(cells, 64, 1)
        column_s[8 * k : 8 * k + 8, :] = total


def load_weights(weight_ref, weight_s, gx):
    weight_s[...] = jnp.zeros((8, 128), F32)
    for k in range(3):
        own = weight_ref[k, pl.ds(gx, 1), :]
        weight_s[2 * k : 2 * k + 1, :] = own[:, 0:128]
        weight_s[2 * k + 1 : 2 * k + 2, :] = own[:, 128:256]
        weight_s[6:7, 32 * k : 32 * k + 32] = own[:, 256:288]


def prescribe(out_ref, cycle_s, column_s, gx):
    lane = iota((ROWS, COLS), 1)

    @pl.when(jnp.logical_or(gx == 0, gx == GX - 1))
    def _():
        turned = jnp.concatenate([column_s[...], jnp.zeros((88, 128), F32)], axis=0).T
        column = jnp.where(gx == 0, turned[0:ROWS, :], turned[ROWS : 2 * ROWS, :])
        at = jnp.where(gx == 0, 0, COLS - 1)
        for f in range(LANES):
            out_ref[f] = jnp.where(lane == at, column[:, f : f + 1], out_ref[f])

    out_ref[:, 0, :] = cycle_s[0]
    out_ref[:, ROWS - 1, :] = cycle_s[1]


def coarse_values(out_ref):
    mean = jnp.where(iota((32, 128), 1) // 4 == iota((32, 128), 0), 1.0 / 16.0, 0.0)
    parts = []
    for i in range(4):
        total = (out_ref[:, 4 * i, :] + out_ref[:, 4 * i + 1, :]) + (
            out_ref[:, 4 * i + 2, :] + out_ref[:, 4 * i + 3, :]
        )
        wide = jnp.concatenate([total, total, total, jnp.zeros((8, 128), F32)], axis=0)
        parts.append(
            lax.dot_general(
                mean,
                wide,
                (((1,), (1,)), ((), ())),
                precision=lax.Precision.HIGHEST,
                preferred_element_type=F32,
            )
        )
    coarse = jnp.concatenate(parts, axis=0)
    plane_of = iota((128, 128), 1) // LANES
    placed = [jnp.where(plane_of == plane, coarse, 0.0) for plane in range(PLANES)]
    return jnp.concatenate(halves(jnp.concatenate(placed, axis=0)), axis=1)


def picked(pick, values):
    both = product(pick, values)
    return both[:, 0:128] + both[:, 128:256]


def unpack_entries(pick_ref, values):
    total = picked(pick_ref[...], jnp.concatenate(halves(values), axis=1))
    entries = total[0:ENTRIES]
    for plane in range(1, PLANES):
        part = total[plane * ENTRIES : (plane + 1) * ENTRIES]
        entries = entries + pltpu.roll(part, 128 - LANES * plane, 1)
    return entries


def place_rows(codes, turned, own):
    code = jnp.broadcast_to(codes, (8, 128))
    index = jnp.bitwise_and(code, 127)
    return [
        jnp.where(code >= 0, take(turned[8 * k : 8 * k + 8], index), own(slice(8 * k, 8 * k + 8)))
        for k in range(FG)
    ]


def feed_back(src_ref, out_ref, turned, map_ref):
    for r in range(ROWS):
        cells = place_rows(map_ref[r : r + 1, :], turned, lambda span: src_ref[span, r, :])
        for k in range(FG):
            out_ref[8 * k : 8 * k + 8, r, :] = cells[k]


def neighbours_of(owner, cell):
    row = jnp.right_shift(cell, 7)
    col = jnp.bitwise_and(cell, 127)
    at = jnp.bitwise_and(owner, GX - 1)
    left = owner - at + jnp.bitwise_and(at + GX - 1, GX - 1)
    right = owner - at + jnp.bitwise_and(at + 1, GX - 1)
    top = jnp.logical_and(row == 0, owner >= GX)
    low = jnp.logical_and(row == ROWS - 1, owner < 2 * GX)
    beside = jnp.where(col == 0, left, jnp.where(col == COLS - 1, right, -1))
    across = jnp.where(top, owner - GX, jnp.where(low, owner + GX, -1))
    diagonal = jnp.where(
        jnp.logical_and(low, col == 0),
        left + GX,
        jnp.where(jnp.logical_and(top, col == COLS - 1), right - GX, -1),
    )
    return owner, beside, across, diagonal


def feedback_routes(owner_ref, cell_ref, pick_ref, map_ref, halo_ref, me):
    cell = cell_ref[...]
    owner = owner_ref[...]
    row = jnp.right_shift(cell, 7)
    col = jnp.bitwise_and(cell, 127)
    own = owner == me
    left = me - lax.rem(me, GX) + lax.rem(me + GX - 1, GX)
    right = me - lax.rem(me, GX) + lax.rem(me + 1, GX)
    above = jnp.logical_and(owner == me - GX, row == ROWS - 1)
    below = jnp.logical_and(owner == me + GX, row == 0)
    target = jnp.where(jnp.logical_and(owner == left, col == COLS - 1), row, -1)
    target = jnp.where(jnp.logical_and(owner == right, col == 0), ROWS + row, target)
    corner = jnp.logical_and(row == ROWS - 1, col == 0)
    target = jnp.where(jnp.logical_and(owner == right - GX, corner), 2 * ROWS, target)
    corner = jnp.logical_and(row == 0, col == COLS - 1)
    target = jnp.where(jnp.logical_and(owner == left + GX, corner), 2 * ROWS + 1, target)
    taken = jnp.logical_or(jnp.logical_or(own, target >= 0), jnp.logical_or(above, below))
    found, total = ranks([taken])
    slot = jnp.minimum(found[0], float(MEANS - 1))
    before = jnp.where(iota((GX, GX), 1) < iota((GX, GX), 0), 1.0, 0.0).astype(jnp.bfloat16)
    entry = found[0] + product(before, total.astype(jnp.bfloat16))
    plane = jnp.floor(slot * (1.0 / DEPTH))
    place = iota((GX, 128), 0).astype(F32) * float(DEPTH) + (slot - float(DEPTH) * plane)
    line = jnp.where(own, row, jnp.where(above, ROWS, jnp.where(below, ROWS + 1, -1)))
    entry = jnp.where(taken, entry, -1.0)
    target = target.astype(F32)
    cells = jnp.zeros((2 * ROWS, 128), F32)
    codes = jnp.zeros((ENTRIES, 128), F32)
    for q in range(GX):
        one = slice(q, q + 1)
        here = jnp.where(iota((2 * ROWS, 128), 0) == line[one], entry[one] + 1.0, 0.0)
        hot = jnp.where(iota((128, 128), 0) == col[one], 1.0, 0.0)
        cells = cells + product(here.astype(jnp.bfloat16), hot.astype(jnp.bfloat16), (1, 1))
        hot = jnp.where(iota((ENTRIES, 128), 0).astype(F32) == entry[one], 1.0, 0.0)
        number = iota((128, 128), 0)
        facts = jnp.where(number == 1, plane[one] + 1.0, 0.0)
        facts = jnp.where(number == 0, place[one], jnp.where(number == 2, target[one] + 1.0, facts))
        codes = codes + product(hot.astype(jnp.bfloat16), facts.astype(jnp.bfloat16), (1, 1))
    map_ref[...] = cells.astype(jnp.int32) - 1
    at = codes[:, 0:1]
    level = codes[:, 1:2] - 1.0
    lane = iota((ENTRIES, 128), 1).astype(F32)
    for p in range(PLANES):
        hot = jnp.where(jnp.where(level == float(p), at, -1.0) == lane, 1.0, 0.0)
        pick_ref[p * ENTRIES : (p + 1) * ENTRIES, :] = hot.astype(jnp.bfloat16)
    goal = codes.T[2:3, :] - 1.0
    halo_ref[...] = jnp.where(iota((3 * ROWS, 128), 0).astype(F32) == goal, 1.0, 0.0).astype(
        jnp.bfloat16
    )


def load_terms(owner_ref, cell_ref, gid_s):
    gid_s[6] = jnp.full((GX, 128), -1, jnp.int32)
    for k in range(3):
        gid = owner_ref[k] * 2048 + cell_ref[k]
        gid_s[2 * k] = gid[:, 0:128]
        gid_s[2 * k + 1] = gid[:, 128:256]
        gid_s[6, :, 32 * k : 32 * k + 32] = gid[:, 256:288]


def flag_block(over):
    worst = jnp.max(over, axis=0, keepdims=True)
    flag = jnp.where(worst > 0.5, 1.0, 0.0)
    return jnp.where(iota((8, 128), 1) == 127, jnp.broadcast_to(flag, (8, 128)), 0.0)


def first_kernel(
    x_ref, owner_ref, cell_ref, send_ref, table_ref, last_row_ref, first_row_ref,
    x_s, owner_s, cell_s, gid_s, mark_s, value_s, rows_s, blocks_s, edges_s, in_sems, out_sems, edge_sems,
):
    grp = lax.axis_index("grp")
    gx = lax.axis_index("gx")
    fetch_x = pltpu.make_async_copy(x_ref, x_s, in_sems.at[0])
    fetch_index = [
        pltpu.make_async_copy(owner_ref, owner_s, in_sems.at[1]),
        pltpu.make_async_copy(cell_ref, cell_s, in_sems.at[2]),
    ]

    @pl.when(grp < 3)
    def _():
        for copy in fetch_index:
            copy.start()
        fetch_x.start()
        for copy in fetch_index:
            copy.wait()
        load_terms(owner_s, cell_s, gid_s)
        gids = [gid_s[t] for t in range(TILES)]
        masks = [jnp.right_shift(g, 11) == grp * GX + gx for g in gids]
        values = [jnp.bitwise_and(g, 2047).astype(F32) for g in gids]
        table, _ = slot_table(masks, values, SLOTS, mark_s, value_s)
        table_ref[...] = table.astype(jnp.int32)
        fetch_x.wait()
        send_edges(x_s, edges_s, send_ref, edge_sems, grp, gx)
        last_row_ref[...] = x_s[:, ROWS - 1, :]
        first_row_ref[...] = x_s[:, 0, :]
        for r in range(ROWS):
            rows_s[r] = x_s[:, r, :]
        for copy in send_cells(rows_s, table_ref, blocks_s, send_ref, out_sems):
            copy.wait()

    @pl.when(grp == 3)
    def _():
        fetch_x.start()
        fetch_x.wait()
        send_edges(x_s, edges_s, send_ref, edge_sems, grp, gx)

    wait_edges(edges_s, send_ref, edge_sems, grp, gx)


def tables_kernel(
    x_ref, diff_ref, cor_ref, mix_ref, owner_ref, cell_ref, weight_ref, fb_owner_ref, fb_cell_ref,
    fresh_ref, codes_ref, weights_ref, pick_ref, hits_ref, flag_ref, map_ref, entry_ref, halo_ref,
    gid_s, mark_s, value_s, found_s, seek_s,
):
    grp = lax.axis_index("grp")
    gx = lax.axis_index("gx")
    update(x_ref, fresh_ref, diff_ref, cor_ref, mix_ref)

    @pl.when(grp < 3)
    def _():
        feedback_routes(
            fb_owner_ref, fb_cell_ref, entry_ref, map_ref, halo_ref, grp * GX + gx
        )

    @pl.when(grp == 3)
    def _():
        load_terms(owner_ref, cell_ref, gid_s)
        load_weights(weight_ref, weights_ref, gx)

        number = iota((PARENTS, 128), 0)
        everyone = neighbours_of(fb_owner_ref[...], fb_cell_ref[...])
        back = jnp.zeros((PARENTS, 128), F32)
        for q in range(GX):
            hit = number == everyone[0][q : q + 1, :]
            for other in everyone[1:]:
                hit = jnp.logical_or(hit, number == other[q : q + 1, :])
            back = back + jnp.where(hit, 1.0, 0.0)
        back = jnp.sum(back, axis=1, keepdims=True)

        own_cell = fb_cell_ref[pl.ds(gx, 1), :]
        goals = neighbours_of(fb_owner_ref[pl.ds(gx, 1), :], own_cell)
        number = iota((128, 128), 0)
        hots = [number == goal for goal in goals]
        anyone = jnp.logical_or(jnp.logical_or(hots[0], hots[1]), jnp.logical_or(hots[2], hots[3]))
        found, total = ranks([anyone])
        over = jnp.max(jnp.where(total > float(MEANS), 1.0, 0.0), axis=0, keepdims=True)
        over = jnp.maximum(
            over, jnp.max(jnp.where(back > float(ENTRIES), 1.0, 0.0), axis=0, keepdims=True)
        )
        most = jnp.minimum(jnp.max(total).astype(jnp.int32), 32)
        slots = [
            jnp.sum(jnp.where(h, found[0], 0.0), axis=0, keepdims=True).astype(jnp.int32)
            for h in hots
        ]
        for p in range(PLANES):
            wanted = [
                jnp.where(
                    jnp.logical_and(goal >= 0, slot // DEPTH == p), goal * DEPTH + slot % DEPTH, -1
                )
                for goal, slot in zip(goals, slots)
            ]
            for part in range(MEAN_ROWS // 128):
                line = number + 128 * part
                hit = line == wanted[0]
                for other in wanted[1:]:
                    hit = jnp.logical_or(hit, line == other)
                pick_ref[128 * part : 128 * part + 128, 128 * p : 128 * p + 128] = jnp.where(
                    hit, 1.0, 0.0
                ).astype(jnp.bfloat16)
        hot, rank = hots[0], slots[0]

        owners = [jnp.right_shift(gid_s[t, pl.ds(gx, 1), :], 11) for t in range(TILES)]
        hots = [iota((PARENTS, 128), 0) == o for o in owners]
        found, total = ranks(hots)
        over = jnp.maximum(
            over, jnp.max(jnp.where(total > float(SLOTS), 1.0, 0.0), axis=0, keepdims=True)
        )
        codes = []
        for t in range(TILES):
            slot = jnp.sum(jnp.where(hots[t], found[t], 0.0), axis=0, keepdims=True)
            slot = jnp.minimum(slot.astype(jnp.int32), SLOTS - 1)
            group = jnp.right_shift(owners[t] * 205, 10)
            codes.append(group * 128 + (owners[t] - 5 * group) * SLOTS + slot)
        for t, code in enumerate(codes):
            codes_ref[t : t + 1, :] = code

        hot = jnp.where(hot, 1.0, 0.0).astype(jnp.bfloat16)
        chosen = iota((32, 128), 0) == rank

        def by_owner(values):
            picked = jnp.where(chosen, values.astype(F32), 0.0).astype(jnp.bfloat16)
            return product(picked, hot, (1, 1)).astype(jnp.int32)

        number = by_owner(iota((1, 128), 1) + 1)
        cells = by_owner(jnp.right_shift(own_cell, 4)) * 16 + by_owner(jnp.bitwise_and(own_cell, 15))
        seek_s[...] = jnp.where(number > 0, cells * 256 + number - 1, -1)
        found_s[...] = jnp.full((TILES, GX, 128), -1, jnp.int32)

        def seek(j, carry):
            line = jnp.broadcast_to(seek_s[pl.ds(j, 1), :], (8, 128))
            for t in range(TILES):
                for part in range(GX // 8):
                    span = slice(8 * part, 8 * part + 8)
                    gid = gid_s[t, span, :]
                    entry = take(line, jnp.bitwise_and(jnp.right_shift(gid, 11), 127))
                    same = jnp.right_shift(entry, 8) == jnp.bitwise_and(gid, 2047)
                    found_s[t, span, :] = jnp.where(
                        same, jnp.bitwise_and(entry, 255), found_s[t, span, :]
                    )
            return carry

        lax.fori_loop(0, most, seek, 0)
        found_at = [found_s[t] for t in range(TILES)]
        table, total = slot_table(
            [f >= 0 for f in found_at], [f.astype(F32) for f in found_at], HITS, mark_s, value_s
        )
        over = jnp.maximum(
            over, jnp.max(jnp.where(total > float(HITS), 1.0, 0.0), axis=0, keepdims=True)
        )
        turned = jnp.concatenate([table, jnp.zeros((96, 128), F32)], axis=0).T
        lane = iota((8, 128), 1).astype(F32)
        for pair in range(GX // 2):
            hits = [
                jnp.where(turned[0:HITS, q : q + 1] == lane, 1.0, 0.0)
                for q in (2 * pair, 2 * pair + 1)
            ]
            line = slice(16 * pair, 16 * pair + 16)
            hits_ref[line, :] = jnp.concatenate(hits, axis=0).astype(jnp.bfloat16)
        flag_ref[...] = flag_block(over)


def second_kernel(
    recv_ref, fresh_ref, diff_ref, above_ref, below_ref, first_ref, last_ref, weights_ref, table_ref,
    codes_ref, pick_ref, hits_ref, flag_ref, out_ref, send_ref, last_row_ref, first_row_ref,
    rows_s, group_s, cycle_s, column_s, blocks_s, edges_s, out_sems, edge_sems,
):
    grp = lax.axis_index("grp")
    gx = lax.axis_index("gx")
    add_columns(fresh_ref, out_ref, gather_halo(recv_ref, grp, gx), diff_ref, grp, gx)

    @pl.when(grp < 3)
    def _():
        add_rows(first_ref, last_ref, out_ref, above_ref, below_ref, diff_ref, grp)
        send_edges(out_ref, edges_s, send_ref, edge_sems, grp, gx)
        last_row_ref[...] = out_ref[:, ROWS - 1, :]
        first_row_ref[...] = out_ref[:, 0, :]
        for r in range(ROWS):
            rows_s[r] = out_ref[:, r, :]
        for copy in send_cells(rows_s, table_ref, blocks_s, send_ref, out_sems):
            copy.wait()
        wait_edges(edges_s, send_ref, edge_sems, grp, gx)

    @pl.when(grp == 3)
    def _():
        regroup(recv_ref, group_s)
        interpolate(codes_ref, weights_ref, group_s, PGROUPS, cycle_s, column_s)
        prescribe(out_ref, cycle_s, column_s, gx)
        values = coarse_values(out_ref)
        base = flag_ref[0:1, :]
        sent = picked(pick_ref[...], values) + base
        for j in range(PARENTS // 2):
            tile = sent[8 * j : 8 * j + 8]
            blocks_s[16 * j : 16 * j + 8, :] = tile
            blocks_s[16 * j + 8 : 16 * j + 16, :] = pltpu.roll(tile, DEPTH, 0)
        copies = [
            pltpu.make_async_copy(blocks_s.at[rows, :], send_ref.at[rows, :], out_sems.at[i])
            for i, rows in enumerate((pl.ds(0, SENT), pl.ds(SENT, TAKEN)))
        ]
        copies[0].start()
        blocks_s[SENT : SENT + TAKEN, :] = picked(hits_ref[...], values[0:128]) + base
        right = rows_of(PARENTS + lax.rem(gx + 1, GX))
        left = rows_of(PARENTS + lax.rem(gx + GX - 1, GX))
        blocks_s[right, :] = blocks_s[right, :] + edge_block(out_ref, COLS - 1)
        blocks_s[left, :] = blocks_s[left, :] + edge_block(out_ref, 0)
        copies[1].start()
        for copy in copies:
            copy.wait()


def hits_kernel(
    x_ref, diff_ref, cor_ref, mix_ref, owner_ref, cell_ref, fb_owner_ref, fb_cell_ref, plain_ref,
    fresh_ref, codes_ref, gid_s, turned_s,
):
    gx = lax.axis_index("gx")

    @pl.when(lax.axis_index("grp") == 3)
    def _():
        update(x_ref, fresh_ref, diff_ref, cor_ref, mix_ref)
        load_terms(owner_ref, cell_ref, gid_s)
        terms = [gid_s[t, pl.ds(gx, 1), :] for t in range(TILES)]
        fed = (fb_owner_ref[...] * 2048 + fb_cell_ref[...]).astype(F32)
        turned_s[...] = jnp.concatenate([fed, jnp.full((96, 128), -2.0, F32)], axis=0).T
        wide = [jnp.broadcast_to(t.astype(F32), (8, 128)) for t in terms]

        def match(q, from_block):
            index = jnp.full((8, 128), q, jnp.int32)
            for s in range(16):
                part = take(turned_s[8 * s : 8 * s + 8, :], index)
                from_block = [jnp.where(part == w, q, f) for w, f in zip(wide, from_block)]
            return from_block

        none = [jnp.full((8, 128), -1, jnp.int32) for _ in terms]
        from_block = lax.fori_loop(0, GX, match, none)
        sources = [jnp.max(f, axis=0, keepdims=True) for f in from_block]
        hots = [iota((GX, 128), 0) == s for s in sources]
        found, _ = ranks(hots)
        codes = []
        for t in range(TILES):
            slot = jnp.sum(jnp.where(hots[t], found[t], 0.0), axis=0, keepdims=True)
            slot = jnp.minimum(slot.astype(jnp.int32), HITS - 1)
            code = (PGROUPS + jnp.right_shift(sources[t], 4)) * 128
            code = code + jnp.bitwise_and(sources[t], 15) * HITS + slot
            codes.append(jnp.where(sources[t] >= 0, code, -1))
        for t, code in enumerate(codes):
            plain = plain_ref[t : t + 1, :]
            codes_ref[t : t + 1, :] = jnp.where(code >= 0, code, plain)


def third_kernel(
    recv_ref, x_ref, fresh_ref, diff_ref, weights_ref, codes_ref, pick_ref, map_ref, entry_ref,
    halo_ref, above_ref, below_ref, out_ref, send_ref, flag_ref, rims_ref, halos_ref,
    group_s, cycle_s, column_s, blocks_s, out_sem,
):
    grp = lax.axis_index("grp")
    gx = lax.axis_index("gx")
    flag = recv_ref[SENT : SENT + 8, :]
    for q in range(1, GX):
        flag = jnp.maximum(flag, recv_ref[SENT + 8 * q : SENT + 8 * q + 8, :])
    flag_ref[...] = flag

    @pl.when(grp < 3)
    def _():
        upper = iota((8, 128), 0) < DEPTH
        tiles = []
        for j in range(GX // 2):
            even = recv_ref[SENT + 16 * j : SENT + 16 * j + 8, :]
            odd = recv_ref[SENT + 16 * j + 8 : SENT + 16 * j + 16, :]
            tiles.append(jnp.where(upper, even, pltpu.roll(odd, DEPTH, 0)))
        entries = unpack_entries(entry_ref, jnp.concatenate(tiles, axis=0))
        turned = entries.T
        feed_back(x_ref, out_ref, turned, map_ref)
        for k, cells in enumerate(
            place_rows(map_ref[ROWS : ROWS + 1, :], turned, lambda span: above_ref[span, :])
        ):
            rims_ref[0, 8 * k : 8 * k + 8, :] = cells
        for k, cells in enumerate(
            place_rows(map_ref[ROWS + 1 : ROWS + 2, :], turned, lambda span: below_ref[span, :])
        ):
            rims_ref[1, 8 * k : 8 * k + 8, :] = cells
        hot = halo_ref[...]
        moved = jnp.concatenate(halves(pltpu.roll(entries, EDGE, 1)), axis=1)
        fed = jnp.sum(hot.astype(F32), axis=1, keepdims=True) > 0.5
        before = jnp.concatenate(gather_halo(recv_ref, grp, gx), axis=0)
        halos_ref[...] = jnp.where(fed, picked(hot, moved), before)

    @pl.when(grp == 3)
    def _():
        add_columns(fresh_ref, out_ref, gather_halo(recv_ref, grp, gx), diff_ref, grp, gx)
        regroup(recv_ref, group_s)
        regroup_hits(recv_ref, group_s)
        interpolate(codes_ref, weights_ref, group_s, GROUPS, cycle_s, column_s)
        prescribe(out_ref, cycle_s, column_s, gx)
        blocks_s[...] = picked(pick_ref[...], coarse_values(out_ref))
        copy = pltpu.make_async_copy(blocks_s, send_ref.at[pl.ds(0, MEAN_ROWS), :], out_sem.at[0])
        copy.start()
        copy.wait()


def parents_kernel(x_ref, diff_ref, cor_ref, mix_ref, rims_ref, halos_ref, fresh_ref):
    grp = lax.axis_index("grp")

    @pl.when(grp < 3)
    def _():
        update(x_ref, fresh_ref, diff_ref, cor_ref, mix_ref)
        halo = (halos_ref[0:ROWS, :], halos_ref[ROWS : 2 * ROWS, :], halos_ref[2 * ROWS : 3 * ROWS, :])
        add_columns(fresh_ref, fresh_ref, halo, diff_ref, grp, lax.axis_index("gx"))
        first = x_ref[:, 0, :]
        last = x_ref[:, ROWS - 1, :]
        add_rows(first, last, fresh_ref, rims_ref[0], rims_ref[1], diff_ref, grp)


def fourth_kernel(recv_ref, x_ref, fresh_ref, map_ref, entry_ref, out_ref):
    grp = lax.axis_index("grp")

    @pl.when(grp < 3)
    def _():
        entries = unpack_entries(entry_ref, recv_ref[MEAN_ROWS : MEAN_ROWS + 128, :])
        feed_back(fresh_ref, out_ref, entries.T, map_ref)

    @pl.when(grp == 3)
    def _():
        out_ref[...] = x_ref[...]


def call(kernel, name, ins, spaces, outs, out_spaces, scratch, sems=()):
    space = {"s": pltpu.SMEM, "v": pltpu.VMEM, "a": pl.ANY}
    return pl.pallas_call(
        kernel,
        name=name,
        in_specs=[pl.BlockSpec(memory_space=space[s]) for s in spaces],
        out_specs=[pl.BlockSpec(memory_space=space[s]) for s in out_spaces],
        out_shape=[jax.ShapeDtypeStruct(s, d) for s, d in outs],
        scratch_shapes=[pltpu.VMEM(s, d) for s, d in scratch]
        + [pltpu.SemaphoreType.DMA((n,)) for n in sems],
        compiler_params=pltpu.CompilerParams(vmem_limit_bytes=VMEM_LIMIT),
        cost_estimate=pl.CostEstimate(flops=1000000, bytes_accessed=4000000, transcendentals=0),
    )(*ins)


STATE = ((LANES, ROWS, COLS), F32)
BLOCKS = ((DEVICES * 8, 128), F32)
BLOCK = ((8, 128), F32)
RIM = ((LANES, COLS), F32)
ROWMAJOR = ((ROWS, LANES, COLS), F32)
MAP = ((2 * ROWS, 128), jnp.int32)
GIDS = ((TILES, GX, 128), jnp.int32)
TERMS = ((TILES, GX, 128), F32)
PICK = ((MEAN_ROWS, PLANES * 128), jnp.bfloat16)
HIT = ((TAKEN, 128), jnp.bfloat16)
ENTRY = ((PLANES * ENTRIES, 128), jnp.bfloat16)
HALO = ((3 * ROWS, 128), jnp.bfloat16)
HALOS = ((3 * ROWS, 128), F32)
RIMS = ((2, LANES, COLS), F32)
THIN = ((DEVICES * DEPTH, 128), F32)
GROUPED = ((GROUPS, LANES, 128), F32)
CYCLE = ((2, LANES, 128), F32)
TABLE = ((GX, 128), jnp.int32)
CODES = ((8, 128), jnp.int32)
INDEX = ((3, GX, PERIM), jnp.int32)
EDGES = ((16, 128), F32)
TO_NEST = ((TAKEN, 128), F32)


def exchange(blocks):
    return lax.all_to_all(blocks, ("grp", "gx"), 0, 0, tiled=True)


def rims(last_row, first_row):
    above = lax.ppermute(last_row, "grp", [(0, 1), (1, 2)])
    below = lax.ppermute(first_row, "grp", [(1, 0), (2, 1)])
    return above, below


def shards(atmosphere, diffusion, coriolis, mixing, owner, cell, weight, fb_owner, fb_cell):
    inputs = (atmosphere, diffusion, coriolis, mixing, owner, cell, weight, fb_owner, fb_cell)
    owner, cell, weight = (jnp.transpose(a, (1, 0, 2)) for a in (owner, cell, weight))
    physics = (diffusion, coriolis, mixing)
    send, table, last_row, first_row = call(
        first_kernel,
        "first_cells",
        (atmosphere, owner, cell),
        "aaa",
        (BLOCKS, TABLE, RIM, RIM),
        "avvv",
        (STATE, INDEX, INDEX, GIDS, TERMS, TERMS, ROWMAJOR, TO_NEST, EDGES),
        (3, 7, 4),
    )
    recv = exchange(send)
    above, below = rims(last_row, first_row)
    fresh, codes, weights, pick, hits, flag, place, entry, halo = call(
        tables_kernel,
        "tables",
        (atmosphere,) + physics + (owner, cell, weight, fb_owner, fb_cell),
        "vvssvvvvv",
        (STATE, CODES, BLOCK, PICK, HIT, BLOCK, MAP, ENTRY, HALO),
        "vvvvvvvvv",
        (GIDS, TERMS, TERMS, GIDS, ((32, 128), jnp.int32)),
    )
    state, send, next_last, next_first = call(
        second_kernel,
        "substep_one",
        (recv, fresh, diffusion, above, below, first_row, last_row, weights, table, codes, pick, hits, flag),
        "v" * 13,
        (STATE, BLOCKS, RIM, RIM),
        "vavv",
        (ROWMAJOR, GROUPED, CYCLE, RIM, BLOCKS, EDGES),
        (7, 4),
    )
    recv = exchange(send)
    above, below = rims(next_last, next_first)
    fresh, codes = call(
        hits_kernel,
        "hits",
        (state,) + physics + (owner, cell, fb_owner, fb_cell, codes),
        "vvssvvvvv",
        (STATE, CODES),
        "vv",
        (GIDS, ((128, 128), F32)),
    )
    state, send, flag, edge_rows, halos = call(
        third_kernel,
        "substep_two",
        (recv, state, fresh, diffusion, weights, codes, pick, place, entry, halo, above, below),
        "v" * 12,
        (STATE, THIN, BLOCK, RIMS, HALOS),
        "vavvv",
        (GROUPED, CYCLE, RIM, ((MEAN_ROWS, 128), F32)),
        (1,),
    )
    recv = exchange(send)
    (fresh,) = call(
        parents_kernel,
        "parents",
        (state,) + physics + (edge_rows, halos),
        "vvssvv",
        (STATE,),
        "v",
        (),
    )

    def finish(received, *_):
        return call(fourth_kernel, "finish", received, "v" * 5, (STATE,), "v", ())[0]

    received = (recv, state, fresh, place, entry)
    return lax.cond(flag[0, 127] > 0.5, lambda _, *a: dense_plan(*a), finish, received, *inputs)


def solution(mesh):
    placed = (P(None, "grp", "gx"), P("grp", "gx"), P("grp"), P(), P(), P(), P(), P(), P())
    return jax.shard_map(
        shards, mesh=mesh, in_specs=placed, out_specs=P(None, "grp", "gx"), check_vma=False
    )
```

```python
import jax
import jax.numpy as jnp
from jax import lax
from jax.experimental import pallas as pl
from jax.experimental.pallas import tpu as pltpu
from jax.sharding import PartitionSpec as P

SUBSTEPS = 2
F32 = jnp.float32
LANES = 40
ROWS = 16
COLS = 128
LEVELS = 10
GX = 32
PARENTS = 96
DEVICES = 128
PERIM = 288
TILES = 7
SLOTS = 25
HITS = 8
EDGE = 40
FG = 5
UNROLL = 6
GROUP_UNROLL = 20
PGROUPS = 20
GROUPS = 22
ENTRIES = 128
PLANES = 3
DEPTH = 4
MEANS = DEPTH * PLANES
MEAN_ROWS = PARENTS * DEPTH
SENT = PARENTS * 8
TAKEN = GX * 8
VMEM_LIMIT = 24 * 1024 * 1024


def padded(cells, sides, width):
    for axis, dim in sides:
        count = lax.axis_size(axis)
        head = lax.slice_in_dim(cells, 0, width, axis=dim)
        tail = lax.slice_in_dim(cells, cells.shape[dim] - width, cells.shape[dim], axis=dim)
        cells = jnp.concatenate(
            [
                lax.ppermute(tail, axis, [(i, (i + 1) % count) for i in range(count)]),
                cells,
                lax.ppermute(head, axis, [((i + 1) % count, i) for i in range(count)]),
            ],
            axis=dim,
        )
    return cells


def broadcast(value, axis, source):
    kept = jnp.where(lax.axis_index(axis) == source, value, 0).astype(value.dtype)
    for other in range(lax.axis_size(axis)):
        if other != source:
            kept = kept + lax.ppermute(jnp.where(lax.axis_index(axis) == source, value, 0), axis, [(source, other)])
    return kept


def gather_columns(value, axis):
    count = lax.axis_size(axis)
    copies = jnp.broadcast_to(value[None], (count,) + value.shape)
    blocks = lax.all_to_all(copies, axis, 0, 0, tiled=True)
    return blocks.transpose(1, 0, 2).reshape(value.shape[0], -1)


def reduce_cycle(terms, column_count, group_count):
    blocks = terms.reshape(terms.shape[0], column_count, -1).transpose(1, 0, 2)
    partial = lax.all_to_all(blocks, "gx", 0, 0, tiled=True).sum(axis=0)
    total = partial
    for group in range(group_count - 1):
        total = total + lax.ppermute(partial, "grp", [(group, group_count - 1)])
    return total


def advance(extended, center, diffusion, coriolis, mixing):
    neighbours = (
        extended[:, 1:-1, :-2]
        + extended[:, 1:-1, 2:]
        + extended[:, :-2, 1:-1]
        + extended[:, 2:, 1:-1]
        + extended[:, :-2, 2:]
        + extended[:, 2:, :-2]
    )
    laplace = neighbours - 6.0 * center
    lane_count, row_count, col_count = center.shape
    level_count = mixing.shape[0]
    stacked = center.reshape(lane_count // level_count, level_count, row_count, col_count)
    upper = jnp.concatenate([stacked[:, 1:], stacked[:, -1:]], axis=1)
    lower = jnp.concatenate([stacked[:, :1], stacked[:, :-1]], axis=1)
    vertical = mixing[None, :, None, None] * (upper - 2.0 * stacked + lower)
    rotation = jnp.concatenate(
        [
            (coriolis[:, None] * stacked[1])[None],
            (-coriolis[:, None] * stacked[0])[None],
            jnp.zeros_like(stacked[2:]),
        ],
        axis=0,
    )
    return center + diffusion * laplace + (vertical + rotation).reshape(center.shape)


def dense_plan(
    atmosphere,
    diffusion,
    coriolis,
    mixing,
    stencil_owner,
    stencil_cell,
    stencil_weight,
    feedback_owner,
    feedback_cell,
):
    lane_count, row_count, col_count = atmosphere.shape
    cell_count = row_count * col_count
    column_count = lax.axis_size("gx")
    group_count = lax.axis_size("grp")
    group_index = lax.axis_index("grp")
    column_index = lax.axis_index("gx")
    own_rank = group_index * column_count + column_index
    is_nested = group_index == group_count - 1
    perimeter = stencil_owner.shape[2]
    owner_flat = feedback_owner.reshape(-1)
    target_flat = feedback_cell.reshape(-1)
    current = atmosphere
    for substep in range(SUBSTEPS):
        flat_now = current.reshape(lane_count, cell_count)
        cycle_terms = jnp.zeros((lane_count, column_count * perimeter), jnp.float32)
        for member in range(stencil_owner.shape[1]):
            mine = stencil_owner[:, member, :].reshape(-1) == own_rank
            positions = jnp.where(mine, stencil_cell[:, member, :].reshape(-1), 0)
            weights = jnp.where(mine, stencil_weight[:, member, :].reshape(-1), 0.0)
            cycle_terms = cycle_terms + jnp.take(flat_now, positions, axis=1) * weights
        cycle = reduce_cycle(cycle_terms, column_count, group_count)
        extended = padded(current, (("grp", 1), ("gx", 2)), 1)
        upper_rim = jnp.where(group_index == 0, extended[:, 1:2, :], extended[:, 0:1, :])
        lower_rim = jnp.where(
            group_index == group_count - 2, extended[:, -2:-1, :], extended[:, -1:, :]
        )
        extended = jnp.concatenate([upper_rim, extended[:, 1:-1, :], lower_rim], axis=1)
        fresh = advance(extended, current, diffusion, coriolis, mixing)
        left_edge = jnp.where(
            column_index == 0, cycle[:, 2 * col_count : 2 * col_count + row_count], fresh[:, :, 0]
        )
        right_edge = jnp.where(
            column_index == column_count - 1, cycle[:, 2 * col_count + row_count :], fresh[:, :, -1]
        )
        framed = fresh.at[:, :, 0].set(left_edge).at[:, :, -1].set(right_edge)
        framed = (
            framed.at[:, 0, :]
            .set(cycle[:, :col_count])
            .at[:, -1, :]
            .set(cycle[:, col_count : 2 * col_count])
        )
        fresh = jnp.where(is_nested, framed, fresh)
        coarse = fresh.reshape(lane_count, row_count // 4, 4, col_count // 4, 4).mean(axis=(2, 4))
        coarse = coarse.reshape(lane_count, -1)
        fresh_flat = fresh.reshape(lane_count, cell_count)
        shared = broadcast(coarse, "grp", group_count - 1)
        place_positions = jnp.where(owner_flat == own_rank, target_flat, cell_count)
        result_flat = fresh_flat.at[:, place_positions].set(
            gather_columns(shared, "gx"), mode="drop"
        )
        current = result_flat.reshape(lane_count, row_count, col_count)
    return current


def iota(shape, dim):
    return lax.broadcasted_iota(jnp.int32, shape, dim)


def rows_of(device):
    return pl.ds(pl.multiple_of(8 * device, 8), 8)


def take(tile, index):
    return jnp.take_along_axis(tile, index, axis=1, mode="promise_in_bounds")


def halves(values):
    high = values.astype(jnp.bfloat16)
    return high, (values - high.astype(F32)).astype(jnp.bfloat16)


def product(left, right, contract=(1, 0)):
    dims = (((contract[0],), (contract[1],)), ((), ()))
    return lax.dot_general(left, right, dims, preferred_element_type=F32)


def ranks(masks):
    rows = masks[0].shape[0]
    stacked = jnp.concatenate([jnp.where(m, 1.0, 0.0) for m in masks], axis=0)
    stacked = stacked.astype(jnp.bfloat16)
    before = jnp.where(iota((128, 128), 0) < iota((128, 128), 1), 1.0, 0.0).astype(jnp.bfloat16)
    ones = jnp.ones((128, 128), jnp.bfloat16)
    within = product(stacked, before)
    totals = product(stacked, ones)
    carry = jnp.zeros((rows, 128), F32)
    found = []
    for t in range(len(masks)):
        found.append(within[t * rows : (t + 1) * rows] + carry)
        carry = carry + totals[t * rows : (t + 1) * rows]
    return found, carry


def slot_table(masks, values, slots, mark_s, value_s):
    found, total = ranks(masks)
    for t in range(TILES):
        mark_s[t] = jnp.where(masks[t], found[t], -1.0)
        value_s[t] = values[t]
    slot_of = lax.rem(iota((8, 128), 1), slots)
    parts = []
    for part in range(GX // 8):
        span = slice(8 * part, 8 * part + 8)
        marks = [mark_s[t, span, :] for t in range(TILES)]
        vals = [value_s[t, span, :] for t in range(TILES)]
        table = jnp.zeros((8, 128), F32)
        for j in range(slots):
            picked = [jnp.where(m == float(j), v, 0.0) for m, v in zip(marks, vals)]
            while len(picked) > 1:
                picked = [sum(picked[k + 1 : k + 2], picked[k]) for k in range(0, len(picked), 2)]
            table = jnp.where(slot_of == j, jnp.sum(picked[0], axis=1, keepdims=True), table)
        parts.append(table)
    return jnp.concatenate(parts, axis=0), total


def swap_segments(tiles):
    segment = iota((8, 128), 1) // SLOTS
    moved = {}
    for shift in range(1 - FG, FG):
        diagonal = None
        for s in range(FG):
            if 0 <= s + shift < FG:
                tile = tiles[s + shift]
                diagonal = tile if diagonal is None else jnp.where(segment == s, tile, diagonal)
        by = (SLOTS * shift) % 128
        moved[shift] = diagonal if by == 0 else pltpu.roll(diagonal, by, 1)
    results = []
    for s in range(FG):
        result = moved[-s]
        for a in range(1, FG):
            result = jnp.where(segment == a, moved[a - s], result)
        results.append(result)
    return results


def send_cells(rows_s, table_ref, blocks_s, send_ref, sems):
    copies = []
    lane = iota((8, 128), 1)
    group_of = lane // SLOTS
    table = table_ref[0:GX, :]
    for g in range(7):
        index = jnp.zeros((1, 128), jnp.int32)
        members = [q for q in range(5 * g, 5 * g + 5) if q < GX]
        for q in members:
            index = jnp.where(group_of[0:1] == q - 5 * g, table[q : q + 1, :], index)
        index = jnp.broadcast_to(index, (8, 128))
        col = jnp.bitwise_and(index, 127)
        row = jnp.right_shift(index, 7)
        cells = [jnp.zeros((8, 128), F32) for _ in range(FG)]
        for r in range(ROWS):
            here = row == r
            for k in range(FG):
                cells[k] = jnp.where(here, take(rows_s[r, 8 * k : 8 * k + 8, :], col), cells[k])
        blocks = swap_segments(cells)
        for q in members:
            blocks_s[8 * q : 8 * q + 8, :] = blocks[q - 5 * g]
        span = pl.ds(8 * members[0], 8 * len(members))
        rows = pl.ds(SENT + 8 * members[0], 8 * len(members))
        copies.append(pltpu.make_async_copy(blocks_s.at[span, :], send_ref.at[rows, :], sems.at[g]))
        copies[-1].start()
    return copies


def edge_block(x_ref, col):
    lane = iota((8, 128), 1)
    block = jnp.zeros((8, 128), F32)
    for h in range(2):
        for f in range(LANES):
            edge = x_ref[f, 8 * h : 8 * h + 8, col : col + 1]
            block = jnp.where(lane == EDGE + h * LANES + f, edge, block)
    return block


def edge_copies(edges_s, send_ref, sems, grp, gx):
    right = lax.rem(gx + 1, GX)
    left = lax.rem(gx + GX - 1, GX)
    above = jnp.where(grp == 3, 3, jnp.maximum(grp - 1, 0))
    below = jnp.where(grp == 3, 3, jnp.minimum(grp + 1, 2))
    first, last = edges_s.at[0:8, :], edges_s.at[8:16, :]
    plan = [
        (last, grp * GX + right),
        (first, grp * GX + left),
        (last, above * GX + right),
        (first, below * GX + left),
    ]
    return [
        pltpu.make_async_copy(source, send_ref.at[rows_of(to), :], sems.at[i])
        for i, (source, to) in enumerate(plan)
    ]


def send_edges(x_ref, edges_s, send_ref, sems, grp, gx):
    edges_s[0:8, :] = edge_block(x_ref, 0)
    edges_s[8:16, :] = edge_block(x_ref, COLS - 1)
    near = edge_copies(edges_s, send_ref, sems, grp, gx)
    for copy in near[:2]:
        copy.start()

    @pl.when(jnp.logical_or(grp == 1, grp == 2))
    def _():
        near[2].start()

    @pl.when(grp < 2)
    def _():
        near[3].start()


def wait_edges(edges_s, send_ref, sems, grp, gx):
    near = edge_copies(edges_s, send_ref, sems, grp, gx)
    for copy in near[:2]:
        copy.wait()

    @pl.when(jnp.logical_or(grp == 1, grp == 2))
    def _():
        near[2].wait()

    @pl.when(grp < 2)
    def _():
        near[3].wait()


def unpack_edge(block):
    return jnp.concatenate([block, pltpu.roll(block, 128 - LANES, 1)], axis=0)


def update(x_ref, out_ref, diff_ref, cor_ref, mix_ref):
    lane = iota((ROWS, COLS), 1)
    row = iota((ROWS, COLS), 0)
    diff = diff_ref[...]
    cor = jnp.zeros((ROWS, COLS), F32)
    for r in range(ROWS):
        cor = jnp.where(row == r, cor_ref[r], cor)
    for f in range(LANES):
        level = f % LEVELS
        x = x_ref[f]
        up = jnp.where(row == 0, 0.0, pltpu.roll(x, 1, 0))
        down = jnp.where(row == ROWS - 1, 0.0, pltpu.roll(x, ROWS - 1, 0))
        westward = jnp.where(lane == 0, 0.0, pltpu.roll(x + down, 1, 1))
        eastward = jnp.where(lane == COLS - 1, 0.0, pltpu.roll(x + up, COLS - 1, 1))
        laplace = (westward + eastward) + (up + down) - 6.0 * x
        upper = x if level == LEVELS - 1 else x_ref[f + 1]
        lower = x if level == 0 else x_ref[f - 1]
        extra = mix_ref[level] * (upper - 2.0 * x + lower)
        if f < LEVELS:
            extra = extra + cor * x_ref[f + LEVELS]
        elif f < 2 * LEVELS:
            extra = extra - cor * x_ref[f - LEVELS]
        out_ref[f] = x + diff * laplace + extra


def gather_halo(recv_ref, grp, gx):
    right = lax.rem(gx + 1, GX)
    left = lax.rem(gx + GX - 1, GX)
    from_left = unpack_edge(recv_ref[rows_of(grp * GX + left), :])
    from_right = unpack_edge(recv_ref[rows_of(grp * GX + right), :])
    top_right = unpack_edge(recv_ref[rows_of(jnp.maximum(grp - 1, 0) * GX + right), :])
    low_left = unpack_edge(recv_ref[rows_of(jnp.minimum(grp + 1, 3) * GX + left), :])
    row = iota((ROWS, COLS), 0)
    corners = jnp.where(row == 0, top_right[ROWS - 1 : ROWS], low_left[0:1])
    return from_left, from_right, corners


def add_columns(from_ref, out_ref, halo, diff_ref, grp, gx):
    from_left, from_right, corners = halo
    nest = grp == 3
    lane = iota((ROWS, COLS), 1)
    row = iota((ROWS, COLS), 0)
    top_right = jnp.where(grp == 0, from_right[0:1], corners[0:1])
    low_left = jnp.where(grp == 2, from_left[ROWS - 1 : ROWS], corners[1:2])
    top_right = jnp.where(nest, 0.0, top_right)
    low_left = jnp.where(nest, 0.0, low_left)
    left_sum = from_left + jnp.where(row == ROWS - 1, low_left, pltpu.roll(from_left, ROWS - 1, 0))
    right_sum = from_right + jnp.where(row == 0, top_right, pltpu.roll(from_right, 1, 0))
    left_sum = jnp.where(jnp.logical_and(nest, gx == 0), 0.0, left_sum)
    right_sum = jnp.where(jnp.logical_and(nest, gx == GX - 1), 0.0, right_sum)
    diff = diff_ref[...]
    left_sum = left_sum * diff[:, 0:1]
    right_sum = right_sum * diff[:, COLS - 1 : COLS]
    source = jnp.bitwise_and(EDGE + jnp.right_shift(lane + 1, 1), 127)
    spread = jnp.concatenate(
        [
            jnp.where(
                jnp.bitwise_and(lane[0:8], 1) == 0,
                take(left_sum[h : h + 8], source[0:8]),
                take(right_sum[h : h + 8], jnp.where(lane[0:8] == 127, EDGE, source[0:8])),
            )
            for h in (0, 8)
        ],
        axis=0,
    )
    outer = jnp.logical_or(lane == 0, lane == COLS - 1)
    for f in range(LANES):
        moved = spread if f == 0 else pltpu.roll(spread, 128 - 2 * f, 1)
        out_ref[f] = from_ref[f] + jnp.where(outer, moved, 0.0)


def add_rows(first_ref, last_ref, out_ref, above_ref, below_ref, diff_ref, grp):
    lane = iota((LANES, COLS), 1)
    above = jnp.where(grp == 0, first_ref[...], above_ref[...])
    below = jnp.where(grp == 2, last_ref[...], below_ref[...])
    above = above + jnp.where(lane == COLS - 1, 0.0, pltpu.roll(above, COLS - 1, 1))
    below = below + jnp.where(lane == 0, 0.0, pltpu.roll(below, 1, 1))
    out_ref[:, 0, :] = out_ref[:, 0, :] + diff_ref[0:1, :] * above
    out_ref[:, ROWS - 1, :] = out_ref[:, ROWS - 1, :] + diff_ref[ROWS - 1 : ROWS, :] * below


def chunks(count, step, body):
    def run(c, carry):
        for s in range(step):
            body(c * step + s)
        return carry

    lax.fori_loop(0, count // step, run, 0)


def regroup(recv_ref, group_s):
    def body(g):
        tiles = swap_segments([recv_ref[rows_of(g * 5 + i), :] for i in range(5)])
        for k in range(FG):
            group_s[g, 8 * k : 8 * k + 8, :] = tiles[k]

    chunks(PGROUPS, GROUP_UNROLL, body)


def regroup_hits(recv_ref, group_s):
    for h in range(2):
        first = SENT + 128 * h
        group_s[PGROUPS + h] = recv_ref[first : first + 128, :].T[0:LANES]


def interpolate(codes_ref, weight_s, group_s, groups, cycle_s, column_s):
    def cells_of(t):
        code = jnp.broadcast_to(codes_ref[pl.ds(t, 1), :], (8, 128))
        index = jnp.bitwise_and(code, 127)
        group = jnp.right_shift(code, 7)
        weight = weight_s[pl.ds(t, 1), :]
        cells = [jnp.zeros((8, 128), F32) for _ in range(FG)]
        for g in range(groups):
            here = group == g
            for k in range(FG):
                cells[k] = jnp.where(here, take(group_s[g, 8 * k : 8 * k + 8, :], index), cells[k])
        return [weight * c for c in cells]

    cycle_s[...] = jnp.zeros((2, LANES, 128), F32)

    def body(t):
        span = jnp.bitwise_and(t, 1)
        for k, cells in enumerate(cells_of(t)):
            cycle_s[span, 8 * k : 8 * k + 8, :] += cells

    chunks(6, UNROLL, body)
    for k, cells in enumerate(cells_of(6)):
        total = cells + pltpu.roll(cells, 96, 1) + pltpu.roll(cells, 64, 1)
        column_s[8 * k : 8 * k + 8, :] = total


def load_weights(weight_ref, weight_s, gx):
    weight_s[...] = jnp.zeros((8, 128), F32)
    for k in range(3):
        own = weight_ref[k, pl.ds(gx, 1), :]
        weight_s[2 * k : 2 * k + 1, :] = own[:, 0:128]
        weight_s[2 * k + 1 : 2 * k + 2, :] = own[:, 128:256]
        weight_s[6:7, 32 * k : 32 * k + 32] = own[:, 256:288]


def prescribe(out_ref, cycle_s, column_s, gx):
    lane = iota((ROWS, COLS), 1)

    @pl.when(jnp.logical_or(gx == 0, gx == GX - 1))
    def _():
        turned = jnp.concatenate([column_s[...], jnp.zeros((88, 128), F32)], axis=0).T
        column = jnp.where(gx == 0, turned[0:ROWS, :], turned[ROWS : 2 * ROWS, :])
        at = jnp.where(gx == 0, 0, COLS - 1)
        for f in range(LANES):
            out_ref[f] = jnp.where(lane == at, column[:, f : f + 1], out_ref[f])

    out_ref[:, 0, :] = cycle_s[0]
    out_ref[:, ROWS - 1, :] = cycle_s[1]


def coarse_values(out_ref):
    mean = jnp.where(iota((32, 128), 1) // 4 == iota((32, 128), 0), 1.0 / 16.0, 0.0)
    parts = []
    for i in range(4):
        total = (out_ref[:, 4 * i, :] + out_ref[:, 4 * i + 1, :]) + (
            out_ref[:, 4 * i + 2, :] + out_ref[:, 4 * i + 3, :]
        )
        wide = jnp.concatenate([total, total, total, jnp.zeros((8, 128), F32)], axis=0)
        high, low = halves(wide)
        weights = mean.astype(jnp.bfloat16)
        parts.append(product(weights, high, (1, 1)) + product(weights, low, (1, 1)))
    coarse = jnp.concatenate(parts, axis=0)
    plane_of = iota((128, 128), 1) // LANES
    placed = [jnp.where(plane_of == plane, coarse, 0.0) for plane in range(PLANES)]
    return jnp.concatenate(halves(jnp.concatenate(placed, axis=0)), axis=1)


def picked(pick, values):
    both = product(pick, values)
    return both[:, 0:128] + both[:, 128:256]


def unpack_entries(pick_ref, values):
    total = picked(pick_ref[...], jnp.concatenate(halves(values), axis=1))
    entries = total[0:ENTRIES]
    for plane in range(1, PLANES):
        part = total[plane * ENTRIES : (plane + 1) * ENTRIES]
        entries = entries + pltpu.roll(part, 128 - LANES * plane, 1)
    return entries


def place_rows(codes, turned, own):
    code = jnp.broadcast_to(codes, (8, 128))
    index = jnp.bitwise_and(code, 127)
    return [
        jnp.where(code >= 0, take(turned[8 * k : 8 * k + 8], index), own(slice(8 * k, 8 * k + 8)))
        for k in range(FG)
    ]


def feed_back(src_ref, out_ref, turned, map_ref):
    for r in range(ROWS):
        cells = place_rows(map_ref[r : r + 1, :], turned, lambda span: src_ref[span, r, :])
        for k in range(FG):
            out_ref[8 * k : 8 * k + 8, r, :] = cells[k]


def neighbours_of(owner, cell):
    row = jnp.right_shift(cell, 7)
    col = jnp.bitwise_and(cell, 127)
    at = jnp.bitwise_and(owner, GX - 1)
    left = owner - at + jnp.bitwise_and(at + GX - 1, GX - 1)
    right = owner - at + jnp.bitwise_and(at + 1, GX - 1)
    top = jnp.logical_and(row == 0, owner >= GX)
    low = jnp.logical_and(row == ROWS - 1, owner < 2 * GX)
    beside = jnp.where(col == 0, left, jnp.where(col == COLS - 1, right, -1))
    across = jnp.where(top, owner - GX, jnp.where(low, owner + GX, -1))
    diagonal = jnp.where(
        jnp.logical_and(low, col == 0),
        left + GX,
        jnp.where(jnp.logical_and(top, col == COLS - 1), right - GX, -1),
    )
    return owner, beside, across, diagonal


def feedback_routes(owner_ref, cell_ref, pick_ref, map_ref, halo_ref, me):
    cell = cell_ref[...]
    owner = owner_ref[...]
    row = jnp.right_shift(cell, 7)
    col = jnp.bitwise_and(cell, 127)
    own = owner == me
    left = me - lax.rem(me, GX) + lax.rem(me + GX - 1, GX)
    right = me - lax.rem(me, GX) + lax.rem(me + 1, GX)
    above = jnp.logical_and(owner == me - GX, row == ROWS - 1)
    below = jnp.logical_and(owner == me + GX, row == 0)
    target = jnp.where(jnp.logical_and(owner == left, col == COLS - 1), row, -1)
    target = jnp.where(jnp.logical_and(owner == right, col == 0), ROWS + row, target)
    corner = jnp.logical_and(row == ROWS - 1, col == 0)
    target = jnp.where(jnp.logical_and(owner == right - GX, corner), 2 * ROWS, target)
    corner = jnp.logical_and(row == 0, col == COLS - 1)
    target = jnp.where(jnp.logical_and(owner == left + GX, corner), 2 * ROWS + 1, target)
    taken = jnp.logical_or(jnp.logical_or(own, target >= 0), jnp.logical_or(above, below))
    found, total = ranks([taken])
    slot = jnp.minimum(found[0], float(MEANS - 1))
    before = jnp.where(iota((GX, GX), 1) < iota((GX, GX), 0), 1.0, 0.0).astype(jnp.bfloat16)
    entry = found[0] + product(before, total.astype(jnp.bfloat16))
    plane = jnp.floor(slot * (1.0 / DEPTH))
    place = iota((GX, 128), 0).astype(F32) * float(DEPTH) + (slot - float(DEPTH) * plane)
    line = jnp.where(own, row, jnp.where(above, ROWS, jnp.where(below, ROWS + 1, -1)))
    entry = jnp.where(taken, entry, -1.0)
    target = target.astype(F32)
    cells = jnp.zeros((2 * ROWS, 128), F32)
    codes = jnp.zeros((ENTRIES, 128), F32)
    for q in range(GX):
        one = slice(q, q + 1)
        here = jnp.where(iota((2 * ROWS, 128), 0) == line[one], entry[one] + 1.0, 0.0)
        hot = jnp.where(iota((128, 128), 0) == col[one], 1.0, 0.0)
        cells = cells + product(here.astype(jnp.bfloat16), hot.astype(jnp.bfloat16), (1, 1))
        hot = jnp.where(iota((ENTRIES, 128), 0).astype(F32) == entry[one], 1.0, 0.0)
        number = iota((128, 128), 0)
        facts = jnp.where(number == 1, plane[one] + 1.0, 0.0)
        facts = jnp.where(number == 0, place[one], jnp.where(number == 2, target[one] + 1.0, facts))
        codes = codes + product(hot.astype(jnp.bfloat16), facts.astype(jnp.bfloat16), (1, 1))
    map_ref[...] = cells.astype(jnp.int32) - 1
    at = codes[:, 0:1]
    level = codes[:, 1:2] - 1.0
    lane = iota((ENTRIES, 128), 1).astype(F32)
    for p in range(PLANES):
        hot = jnp.where(jnp.where(level == float(p), at, -1.0) == lane, 1.0, 0.0)
        pick_ref[p * ENTRIES : (p + 1) * ENTRIES, :] = hot.astype(jnp.bfloat16)
    goal = codes.T[2:3, :] - 1.0
    halo_ref[...] = jnp.where(iota((3 * ROWS, 128), 0).astype(F32) == goal, 1.0, 0.0).astype(
        jnp.bfloat16
    )


def load_terms(owner_ref, cell_ref, gid_s):
    gid_s[6] = jnp.full((GX, 128), -1, jnp.int32)
    for k in range(3):
        gid = owner_ref[k] * 2048 + cell_ref[k]
        gid_s[2 * k] = gid[:, 0:128]
        gid_s[2 * k + 1] = gid[:, 128:256]
        gid_s[6, :, 32 * k : 32 * k + 32] = gid[:, 256:288]


def flag_block(over):
    worst = jnp.max(over, axis=0, keepdims=True)
    flag = jnp.where(worst > 0.5, 1.0, 0.0)
    return jnp.where(iota((8, 128), 1) == 127, jnp.broadcast_to(flag, (8, 128)), 0.0)


def first_kernel(
    x_ref, owner_ref, cell_ref, send_ref, table_ref, last_row_ref, first_row_ref,
    x_s, owner_s, cell_s, gid_s, mark_s, value_s, rows_s, blocks_s, edges_s, in_sems, out_sems, edge_sems,
):
    grp = lax.axis_index("grp")
    gx = lax.axis_index("gx")
    fetch_x = pltpu.make_async_copy(x_ref, x_s, in_sems.at[0])
    fetch_index = [
        pltpu.make_async_copy(owner_ref, owner_s, in_sems.at[1]),
        pltpu.make_async_copy(cell_ref, cell_s, in_sems.at[2]),
    ]

    @pl.when(grp < 3)
    def _():
        for copy in fetch_index:
            copy.start()
        fetch_x.start()
        for copy in fetch_index:
            copy.wait()
        load_terms(owner_s, cell_s, gid_s)
        gids = [gid_s[t] for t in range(TILES)]
        masks = [jnp.right_shift(g, 11) == grp * GX + gx for g in gids]
        values = [jnp.bitwise_and(g, 2047).astype(F32) for g in gids]
        table, _ = slot_table(masks, values, SLOTS, mark_s, value_s)
        table_ref[...] = table.astype(jnp.int32)
        fetch_x.wait()
        send_edges(x_s, edges_s, send_ref, edge_sems, grp, gx)
        last_row_ref[...] = x_s[:, ROWS - 1, :]
        first_row_ref[...] = x_s[:, 0, :]
        for r in range(ROWS):
            rows_s[r] = x_s[:, r, :]
        for copy in send_cells(rows_s, table_ref, blocks_s, send_ref, out_sems):
            copy.wait()

    @pl.when(grp == 3)
    def _():
        fetch_x.start()
        fetch_x.wait()
        send_edges(x_s, edges_s, send_ref, edge_sems, grp, gx)

    wait_edges(edges_s, send_ref, edge_sems, grp, gx)


def tables_kernel(
    x_ref, diff_ref, cor_ref, mix_ref, owner_ref, cell_ref, weight_ref, fb_owner_ref, fb_cell_ref,
    fresh_ref, codes_ref, weights_ref, pick_ref, hits_ref, flag_ref, map_ref, entry_ref, halo_ref,
    near_diff_ref, gid_s, mark_s, value_s, found_s, seek_s,
):
    grp = lax.axis_index("grp")
    gx = lax.axis_index("gx")
    update(x_ref, fresh_ref, diff_ref, cor_ref, mix_ref)
    near_diff_ref[...] = diff_ref[...]

    @pl.when(grp < 3)
    def _():
        feedback_routes(
            fb_owner_ref, fb_cell_ref, entry_ref, map_ref, halo_ref, grp * GX + gx
        )

    @pl.when(grp == 3)
    def _():
        load_terms(owner_ref, cell_ref, gid_s)
        load_weights(weight_ref, weights_ref, gx)

        number = iota((PARENTS, 128), 0)
        everyone = neighbours_of(fb_owner_ref[...], fb_cell_ref[...])
        back = jnp.zeros((PARENTS, 128), F32)
        for q in range(GX):
            hit = number == everyone[0][q : q + 1, :]
            for other in everyone[1:]:
                hit = jnp.logical_or(hit, number == other[q : q + 1, :])
            back = back + jnp.where(hit, 1.0, 0.0)
        back = jnp.sum(back, axis=1, keepdims=True)

        own_cell = fb_cell_ref[pl.ds(gx, 1), :]
        goals = neighbours_of(fb_owner_ref[pl.ds(gx, 1), :], own_cell)
        number = iota((128, 128), 0)
        hots = [number == goal for goal in goals]
        anyone = jnp.logical_or(jnp.logical_or(hots[0], hots[1]), jnp.logical_or(hots[2], hots[3]))
        found, total = ranks([anyone])
        over = jnp.max(jnp.where(total > float(MEANS), 1.0, 0.0), axis=0, keepdims=True)
        over = jnp.maximum(
            over, jnp.max(jnp.where(back > float(ENTRIES), 1.0, 0.0), axis=0, keepdims=True)
        )
        most = jnp.minimum(jnp.max(total).astype(jnp.int32), 32)
        slots = [
            jnp.sum(jnp.where(h, found[0], 0.0), axis=0, keepdims=True).astype(jnp.int32)
            for h in hots
        ]
        for p in range(PLANES):
            wanted = [
                jnp.where(
                    jnp.logical_and(goal >= 0, slot // DEPTH == p), goal * DEPTH + slot % DEPTH, -1
                )
                for goal, slot in zip(goals, slots)
            ]
            for part in range(MEAN_ROWS // 128):
                line = number + 128 * part
                hit = line == wanted[0]
                for other in wanted[1:]:
                    hit = jnp.logical_or(hit, line == other)
                pick_ref[128 * part : 128 * part + 128, 128 * p : 128 * p + 128] = jnp.where(
                    hit, 1.0, 0.0
                ).astype(jnp.bfloat16)
        hot, rank = hots[0], slots[0]

        owners = [jnp.right_shift(gid_s[t, pl.ds(gx, 1), :], 11) for t in range(TILES)]
        hots = [iota((PARENTS, 128), 0) == o for o in owners]
        found, total = ranks(hots)
        over = jnp.maximum(
            over, jnp.max(jnp.where(total > float(SLOTS), 1.0, 0.0), axis=0, keepdims=True)
        )
        codes = []
        for t in range(TILES):
            slot = jnp.sum(jnp.where(hots[t], found[t], 0.0), axis=0, keepdims=True)
            slot = jnp.minimum(slot.astype(jnp.int32), SLOTS - 1)
            group = jnp.right_shift(owners[t] * 205, 10)
            codes.append(group * 128 + (owners[t] - 5 * group) * SLOTS + slot)
        for t, code in enumerate(codes):
            codes_ref[t : t + 1, :] = code

        hot = jnp.where(hot, 1.0, 0.0).astype(jnp.bfloat16)
        chosen = iota((32, 128), 0) == rank

        def by_owner(values):
            picked = jnp.where(chosen, values.astype(F32), 0.0).astype(jnp.bfloat16)
            return product(picked, hot, (1, 1)).astype(jnp.int32)

        number = by_owner(iota((1, 128), 1) + 1)
        cells = by_owner(jnp.right_shift(own_cell, 4)) * 16 + by_owner(jnp.bitwise_and(own_cell, 15))
        seek_s[...] = jnp.where(number > 0, cells * 256 + number - 1, -1)
        found_s[...] = jnp.full((TILES, GX, 128), -1, jnp.int32)

        def seek(j, carry):
            line = jnp.broadcast_to(seek_s[pl.ds(j, 1), :], (8, 128))
            for t in range(TILES):
                for part in range(GX // 8):
                    span = slice(8 * part, 8 * part + 8)
                    gid = gid_s[t, span, :]
                    entry = take(line, jnp.bitwise_and(jnp.right_shift(gid, 11), 127))
                    same = jnp.right_shift(entry, 8) == jnp.bitwise_and(gid, 2047)
                    found_s[t, span, :] = jnp.where(
                        same, jnp.bitwise_and(entry, 255), found_s[t, span, :]
                    )
            return carry

        lax.fori_loop(0, most, seek, 0)
        found_at = [found_s[t] for t in range(TILES)]
        table, total = slot_table(
            [f >= 0 for f in found_at], [f.astype(F32) for f in found_at], HITS, mark_s, value_s
        )
        over = jnp.maximum(
            over, jnp.max(jnp.where(total > float(HITS), 1.0, 0.0), axis=0, keepdims=True)
        )
        turned = jnp.concatenate([table, jnp.zeros((96, 128), F32)], axis=0).T
        lane = iota((8, 128), 1).astype(F32)
        for pair in range(GX // 2):
            hits = [
                jnp.where(turned[0:HITS, q : q + 1] == lane, 1.0, 0.0)
                for q in (2 * pair, 2 * pair + 1)
            ]
            line = slice(16 * pair, 16 * pair + 16)
            hits_ref[line, :] = jnp.concatenate(hits, axis=0).astype(jnp.bfloat16)
        flag_ref[...] = flag_block(over)


def second_kernel(
    recv_ref, fresh_ref, diff_ref, above_ref, below_ref, first_ref, last_ref, weights_ref, table_ref,
    codes_ref, pick_ref, hits_ref, flag_ref, out_ref, send_ref, last_row_ref, first_row_ref,
    rows_s, group_s, cycle_s, column_s, blocks_s, edges_s, out_sems, edge_sems,
):
    grp = lax.axis_index("grp")
    gx = lax.axis_index("gx")
    add_columns(fresh_ref, out_ref, gather_halo(recv_ref, grp, gx), diff_ref, grp, gx)

    @pl.when(grp < 3)
    def _():
        add_rows(first_ref, last_ref, out_ref, above_ref, below_ref, diff_ref, grp)
        send_edges(out_ref, edges_s, send_ref, edge_sems, grp, gx)
        last_row_ref[...] = out_ref[:, ROWS - 1, :]
        first_row_ref[...] = out_ref[:, 0, :]
        for r in range(ROWS):
            rows_s[r] = out_ref[:, r, :]
        for copy in send_cells(rows_s, table_ref, blocks_s, send_ref, out_sems):
            copy.wait()
        wait_edges(edges_s, send_ref, edge_sems, grp, gx)

    @pl.when(grp == 3)
    def _():
        regroup(recv_ref, group_s)
        interpolate(codes_ref, weights_ref, group_s, PGROUPS, cycle_s, column_s)
        prescribe(out_ref, cycle_s, column_s, gx)
        values = coarse_values(out_ref)
        base = flag_ref[0:1, :]
        sent = picked(pick_ref[...], values) + base
        for j in range(PARENTS // 2):
            tile = sent[8 * j : 8 * j + 8]
            blocks_s[16 * j : 16 * j + 8, :] = tile
            blocks_s[16 * j + 8 : 16 * j + 16, :] = pltpu.roll(tile, DEPTH, 0)
        copies = [
            pltpu.make_async_copy(blocks_s.at[rows, :], send_ref.at[rows, :], out_sems.at[i])
            for i, rows in enumerate((pl.ds(0, SENT), pl.ds(SENT, TAKEN)))
        ]
        copies[0].start()
        blocks_s[SENT : SENT + TAKEN, :] = picked(hits_ref[...], values[0:128]) + base
        right = rows_of(PARENTS + lax.rem(gx + 1, GX))
        left = rows_of(PARENTS + lax.rem(gx + GX - 1, GX))
        blocks_s[right, :] = blocks_s[right, :] + edge_block(out_ref, COLS - 1)
        blocks_s[left, :] = blocks_s[left, :] + edge_block(out_ref, 0)
        copies[1].start()
        for copy in copies:
            copy.wait()


def hits_kernel(
    x_ref, diff_ref, cor_ref, mix_ref, owner_ref, cell_ref, fb_owner_ref, fb_cell_ref, plain_ref,
    fresh_ref, codes_ref, gid_s, turned_s,
):
    gx = lax.axis_index("gx")

    @pl.when(lax.axis_index("grp") == 3)
    def _():
        update(x_ref, fresh_ref, diff_ref, cor_ref, mix_ref)
        load_terms(owner_ref, cell_ref, gid_s)
        terms = [gid_s[t, pl.ds(gx, 1), :] for t in range(TILES)]
        fed = (fb_owner_ref[...] * 2048 + fb_cell_ref[...]).astype(F32)
        turned_s[...] = jnp.concatenate([fed, jnp.full((96, 128), -2.0, F32)], axis=0).T
        wide = [jnp.broadcast_to(t.astype(F32), (8, 128)) for t in terms]

        def match(q, from_block):
            index = jnp.full((8, 128), q, jnp.int32)
            for s in range(16):
                part = take(turned_s[8 * s : 8 * s + 8, :], index)
                from_block = [jnp.where(part == w, q, f) for w, f in zip(wide, from_block)]
            return from_block

        none = [jnp.full((8, 128), -1, jnp.int32) for _ in terms]
        from_block = lax.fori_loop(0, GX // 2, lambda c, f: match(2 * c + 1, match(2 * c, f)), none)
        sources = [jnp.max(f, axis=0, keepdims=True) for f in from_block]
        hots = [iota((GX, 128), 0) == s for s in sources]
        found, _ = ranks(hots)
        codes = []
        for t in range(TILES):
            slot = jnp.sum(jnp.where(hots[t], found[t], 0.0), axis=0, keepdims=True)
            slot = jnp.minimum(slot.astype(jnp.int32), HITS - 1)
            code = (PGROUPS + jnp.right_shift(sources[t], 4)) * 128
            code = code + jnp.bitwise_and(sources[t], 15) * HITS + slot
            codes.append(jnp.where(sources[t] >= 0, code, -1))
        for t, code in enumerate(codes):
            plain = plain_ref[t : t + 1, :]
            codes_ref[t : t + 1, :] = jnp.where(code >= 0, code, plain)


def third_kernel(
    recv_ref, x_ref, fresh_ref, diff_ref, weights_ref, codes_ref, pick_ref, map_ref, entry_ref,
    halo_ref, above_ref, below_ref, out_ref, send_ref, flag_ref, rims_ref, halos_ref,
    group_s, cycle_s, column_s, blocks_s, out_sem,
):
    grp = lax.axis_index("grp")
    gx = lax.axis_index("gx")
    flag = recv_ref[SENT : SENT + 8, :]
    for q in range(1, GX):
        flag = jnp.maximum(flag, recv_ref[SENT + 8 * q : SENT + 8 * q + 8, :])
    flag_ref[...] = flag

    @pl.when(grp < 3)
    def _():
        upper = iota((8, 128), 0) < DEPTH
        tiles = []
        for j in range(GX // 2):
            even = recv_ref[SENT + 16 * j : SENT + 16 * j + 8, :]
            odd = recv_ref[SENT + 16 * j + 8 : SENT + 16 * j + 16, :]
            tiles.append(jnp.where(upper, even, pltpu.roll(odd, DEPTH, 0)))
        entries = unpack_entries(entry_ref, jnp.concatenate(tiles, axis=0))
        turned = entries.T
        feed_back(x_ref, out_ref, turned, map_ref)
        for k, cells in enumerate(
            place_rows(map_ref[ROWS : ROWS + 1, :], turned, lambda span: above_ref[span, :])
        ):
            rims_ref[0, 8 * k : 8 * k + 8, :] = cells
        for k, cells in enumerate(
            place_rows(map_ref[ROWS + 1 : ROWS + 2, :], turned, lambda span: below_ref[span, :])
        ):
            rims_ref[1, 8 * k : 8 * k + 8, :] = cells
        hot = halo_ref[...]
        moved = jnp.concatenate(halves(pltpu.roll(entries, EDGE, 1)), axis=1)
        fed = jnp.sum(hot.astype(F32), axis=1, keepdims=True) > 0.5
        before = jnp.concatenate(gather_halo(recv_ref, grp, gx), axis=0)
        halos_ref[...] = jnp.where(fed, picked(hot, moved), before)

    @pl.when(grp == 3)
    def _():
        add_columns(fresh_ref, out_ref, gather_halo(recv_ref, grp, gx), diff_ref, grp, gx)
        regroup(recv_ref, group_s)
        regroup_hits(recv_ref, group_s)
        interpolate(codes_ref, weights_ref, group_s, GROUPS, cycle_s, column_s)
        prescribe(out_ref, cycle_s, column_s, gx)
        blocks_s[...] = picked(pick_ref[...], coarse_values(out_ref))
        copy = pltpu.make_async_copy(blocks_s, send_ref.at[pl.ds(0, MEAN_ROWS), :], out_sem.at[0])
        copy.start()
        copy.wait()


def parents_kernel(x_ref, diff_ref, cor_ref, mix_ref, rims_ref, halos_ref, fresh_ref):
    grp = lax.axis_index("grp")

    @pl.when(grp < 3)
    def _():
        update(x_ref, fresh_ref, diff_ref, cor_ref, mix_ref)
        halo = (halos_ref[0:ROWS, :], halos_ref[ROWS : 2 * ROWS, :], halos_ref[2 * ROWS : 3 * ROWS, :])
        add_columns(fresh_ref, fresh_ref, halo, diff_ref, grp, lax.axis_index("gx"))
        first = x_ref[:, 0, :]
        last = x_ref[:, ROWS - 1, :]
        add_rows(first, last, fresh_ref, rims_ref[0], rims_ref[1], diff_ref, grp)


def fourth_kernel(recv_ref, x_ref, fresh_ref, map_ref, entry_ref, out_ref):
    grp = lax.axis_index("grp")

    @pl.when(grp < 3)
    def _():
        entries = unpack_entries(entry_ref, recv_ref[MEAN_ROWS : MEAN_ROWS + 128, :])
        feed_back(fresh_ref, out_ref, entries.T, map_ref)

    @pl.when(grp == 3)
    def _():
        out_ref[...] = x_ref[...]


def call(kernel, name, ins, spaces, outs, out_spaces, scratch, sems=()):
    space = {"s": pltpu.SMEM, "v": pltpu.VMEM, "a": pl.ANY}
    return pl.pallas_call(
        kernel,
        name=name,
        in_specs=[pl.BlockSpec(memory_space=space[s]) for s in spaces],
        out_specs=[pl.BlockSpec(memory_space=space[s]) for s in out_spaces],
        out_shape=[jax.ShapeDtypeStruct(s, d) for s, d in outs],
        scratch_shapes=[pltpu.VMEM(s, d) for s, d in scratch]
        + [pltpu.SemaphoreType.DMA((n,)) for n in sems],
        compiler_params=pltpu.CompilerParams(vmem_limit_bytes=VMEM_LIMIT),
        cost_estimate=pl.CostEstimate(flops=1000000, bytes_accessed=4000000, transcendentals=0),
    )(*ins)


STATE = ((LANES, ROWS, COLS), F32)
BLOCKS = ((DEVICES * 8, 128), F32)
BLOCK = ((8, 128), F32)
RIM = ((LANES, COLS), F32)
ROWMAJOR = ((ROWS, LANES, COLS), F32)
MAP = ((2 * ROWS, 128), jnp.int32)
GIDS = ((TILES, GX, 128), jnp.int32)
TERMS = ((TILES, GX, 128), F32)
PICK = ((MEAN_ROWS, PLANES * 128), jnp.bfloat16)
HIT = ((TAKEN, 128), jnp.bfloat16)
ENTRY = ((PLANES * ENTRIES, 128), jnp.bfloat16)
HALO = ((3 * ROWS, 128), jnp.bfloat16)
DIFFUSION = ((ROWS, COLS), F32)
HALOS = ((3 * ROWS, 128), F32)
RIMS = ((2, LANES, COLS), F32)
THIN = ((DEVICES * DEPTH, 128), F32)
GROUPED = ((GROUPS, LANES, 128), F32)
CYCLE = ((2, LANES, 128), F32)
TABLE = ((GX, 128), jnp.int32)
CODES = ((8, 128), jnp.int32)
INDEX = ((3, GX, PERIM), jnp.int32)
EDGES = ((16, 128), F32)
TO_NEST = ((TAKEN, 128), F32)


def exchange(blocks):
    return lax.all_to_all(blocks, ("grp", "gx"), 0, 0, tiled=True)


def rims(last_row, first_row):
    above = lax.ppermute(last_row, "grp", [(0, 1), (1, 2)])
    below = lax.ppermute(first_row, "grp", [(1, 0), (2, 1)])
    return above, below


def shards(atmosphere, diffusion, coriolis, mixing, owner, cell, weight, fb_owner, fb_cell):
    inputs = (atmosphere, diffusion, coriolis, mixing, owner, cell, weight, fb_owner, fb_cell)
    owner, cell, weight = (jnp.transpose(a, (1, 0, 2)) for a in (owner, cell, weight))
    physics = (diffusion, coriolis, mixing)
    send, table, last_row, first_row = call(
        first_kernel,
        "first_cells",
        (atmosphere, owner, cell),
        "aaa",
        (BLOCKS, TABLE, RIM, RIM),
        "avvv",
        (STATE, INDEX, INDEX, GIDS, TERMS, TERMS, ROWMAJOR, TO_NEST, EDGES),
        (3, 7, 4),
    )
    recv = exchange(send)
    above, below = rims(last_row, first_row)
    fresh, codes, weights, pick, hits, flag, place, entry, halo, near_diffusion = call(
        tables_kernel,
        "tables",
        (atmosphere,) + physics + (owner, cell, weight, fb_owner, fb_cell),
        "vvssvvvvv",
        (STATE, CODES, BLOCK, PICK, HIT, BLOCK, MAP, ENTRY, HALO, DIFFUSION),
        "v" * 10,
        (GIDS, TERMS, TERMS, GIDS, ((32, 128), jnp.int32)),
    )
    state, send, next_last, next_first = call(
        second_kernel,
        "substep_one",
        (recv, fresh, near_diffusion, above, below, first_row, last_row, weights, table, codes, pick, hits, flag),
        "v" * 13,
        (STATE, BLOCKS, RIM, RIM),
        "vavv",
        (ROWMAJOR, GROUPED, CYCLE, RIM, BLOCKS, EDGES),
        (7, 4),
    )
    recv = exchange(send)
    above, below = rims(next_last, next_first)
    fresh, codes = call(
        hits_kernel,
        "hits",
        (state,) + physics + (owner, cell, fb_owner, fb_cell, codes),
        "vvssvvvvv",
        (STATE, CODES),
        "vv",
        (GIDS, ((128, 128), F32)),
    )
    state, send, flag, edge_rows, halos = call(
        third_kernel,
        "substep_two",
        (recv, state, fresh, diffusion, weights, codes, pick, place, entry, halo, above, below),
        "v" * 12,
        (STATE, THIN, BLOCK, RIMS, HALOS),
        "vavvv",
        (GROUPED, CYCLE, RIM, ((MEAN_ROWS, 128), F32)),
        (1,),
    )
    recv = exchange(send)
    (fresh,) = call(
        parents_kernel,
        "parents",
        (state,) + physics + (edge_rows, halos),
        "vvssvv",
        (STATE,),
        "v",
        (),
    )

    def finish(received, *_):
        return call(fourth_kernel, "finish", received, "v" * 5, (STATE,), "v", ())[0]

    received = (recv, state, fresh, place, entry)
    return lax.cond(flag[0, 127] > 0.5, lambda _, *a: dense_plan(*a), finish, received, *inputs)


def solution(mesh):
    placed = (P(None, "grp", "gx"), P("grp", "gx"), P("grp"), P(), P(), P(), P(), P(), P())
    return jax.shard_map(
        shards, mesh=mesh, in_specs=placed, out_specs=P(None, "grp", "gx"), check_vma=False
    )
```

```python
import jax
import jax.numpy as jnp
from jax import lax
from jax.experimental import pallas as pl
from jax.experimental.pallas import tpu as pltpu
from jax.sharding import PartitionSpec as P

SUBSTEPS = 2
F32 = jnp.float32
LANES = 40
ROWS = 16
COLS = 128
LEVELS = 10
GX = 32
PARENTS = 96
DEVICES = 128
PERIM = 288
TILES = 7
SLOTS = 25
HITS = 8
EDGE = 40
FG = 5
UNROLL = 6
GROUP_UNROLL = 20
PGROUPS = 20
GROUPS = 22
ENTRIES = 128
PLANES = 3
DEPTH = 4
MEANS = DEPTH * PLANES
MEAN_ROWS = PARENTS * DEPTH
SENT = PARENTS * 8
TAKEN = GX * 8
VMEM_LIMIT = 24 * 1024 * 1024


def padded(cells, sides, width):
    for axis, dim in sides:
        count = lax.axis_size(axis)
        head = lax.slice_in_dim(cells, 0, width, axis=dim)
        tail = lax.slice_in_dim(cells, cells.shape[dim] - width, cells.shape[dim], axis=dim)
        cells = jnp.concatenate(
            [
                lax.ppermute(tail, axis, [(i, (i + 1) % count) for i in range(count)]),
                cells,
                lax.ppermute(head, axis, [((i + 1) % count, i) for i in range(count)]),
            ],
            axis=dim,
        )
    return cells


def broadcast(value, axis, source):
    kept = jnp.where(lax.axis_index(axis) == source, value, 0).astype(value.dtype)
    for other in range(lax.axis_size(axis)):
        if other != source:
            kept = kept + lax.ppermute(jnp.where(lax.axis_index(axis) == source, value, 0), axis, [(source, other)])
    return kept


def gather_columns(value, axis):
    count = lax.axis_size(axis)
    copies = jnp.broadcast_to(value[None], (count,) + value.shape)
    blocks = lax.all_to_all(copies, axis, 0, 0, tiled=True)
    return blocks.transpose(1, 0, 2).reshape(value.shape[0], -1)


def reduce_cycle(terms, column_count, group_count):
    blocks = terms.reshape(terms.shape[0], column_count, -1).transpose(1, 0, 2)
    partial = lax.all_to_all(blocks, "gx", 0, 0, tiled=True).sum(axis=0)
    total = partial
    for group in range(group_count - 1):
        total = total + lax.ppermute(partial, "grp", [(group, group_count - 1)])
    return total


def advance(extended, center, diffusion, coriolis, mixing):
    neighbours = (
        extended[:, 1:-1, :-2]
        + extended[:, 1:-1, 2:]
        + extended[:, :-2, 1:-1]
        + extended[:, 2:, 1:-1]
        + extended[:, :-2, 2:]
        + extended[:, 2:, :-2]
    )
    laplace = neighbours - 6.0 * center
    lane_count, row_count, col_count = center.shape
    level_count = mixing.shape[0]
    stacked = center.reshape(lane_count // level_count, level_count, row_count, col_count)
    upper = jnp.concatenate([stacked[:, 1:], stacked[:, -1:]], axis=1)
    lower = jnp.concatenate([stacked[:, :1], stacked[:, :-1]], axis=1)
    vertical = mixing[None, :, None, None] * (upper - 2.0 * stacked + lower)
    rotation = jnp.concatenate(
        [
            (coriolis[:, None] * stacked[1])[None],
            (-coriolis[:, None] * stacked[0])[None],
            jnp.zeros_like(stacked[2:]),
        ],
        axis=0,
    )
    return center + diffusion * laplace + (vertical + rotation).reshape(center.shape)


def dense_plan(
    atmosphere,
    diffusion,
    coriolis,
    mixing,
    stencil_owner,
    stencil_cell,
    stencil_weight,
    feedback_owner,
    feedback_cell,
):
    lane_count, row_count, col_count = atmosphere.shape
    cell_count = row_count * col_count
    column_count = lax.axis_size("gx")
    group_count = lax.axis_size("grp")
    group_index = lax.axis_index("grp")
    column_index = lax.axis_index("gx")
    own_rank = group_index * column_count + column_index
    is_nested = group_index == group_count - 1
    perimeter = stencil_owner.shape[2]
    owner_flat = feedback_owner.reshape(-1)
    target_flat = feedback_cell.reshape(-1)
    current = atmosphere
    for substep in range(SUBSTEPS):
        flat_now = current.reshape(lane_count, cell_count)
        cycle_terms = jnp.zeros((lane_count, column_count * perimeter), jnp.float32)
        for member in range(stencil_owner.shape[1]):
            mine = stencil_owner[:, member, :].reshape(-1) == own_rank
            positions = jnp.where(mine, stencil_cell[:, member, :].reshape(-1), 0)
            weights = jnp.where(mine, stencil_weight[:, member, :].reshape(-1), 0.0)
            cycle_terms = cycle_terms + jnp.take(flat_now, positions, axis=1) * weights
        cycle = reduce_cycle(cycle_terms, column_count, group_count)
        extended = padded(current, (("grp", 1), ("gx", 2)), 1)
        upper_rim = jnp.where(group_index == 0, extended[:, 1:2, :], extended[:, 0:1, :])
        lower_rim = jnp.where(
            group_index == group_count - 2, extended[:, -2:-1, :], extended[:, -1:, :]
        )
        extended = jnp.concatenate([upper_rim, extended[:, 1:-1, :], lower_rim], axis=1)
        fresh = advance(extended, current, diffusion, coriolis, mixing)
        left_edge = jnp.where(
            column_index == 0, cycle[:, 2 * col_count : 2 * col_count + row_count], fresh[:, :, 0]
        )
        right_edge = jnp.where(
            column_index == column_count - 1, cycle[:, 2 * col_count + row_count :], fresh[:, :, -1]
        )
        framed = fresh.at[:, :, 0].set(left_edge).at[:, :, -1].set(right_edge)
        framed = (
            framed.at[:, 0, :]
            .set(cycle[:, :col_count])
            .at[:, -1, :]
            .set(cycle[:, col_count : 2 * col_count])
        )
        fresh = jnp.where(is_nested, framed, fresh)
        coarse = fresh.reshape(lane_count, row_count // 4, 4, col_count // 4, 4).mean(axis=(2, 4))
        coarse = coarse.reshape(lane_count, -1)
        fresh_flat = fresh.reshape(lane_count, cell_count)
        shared = broadcast(coarse, "grp", group_count - 1)
        place_positions = jnp.where(owner_flat == own_rank, target_flat, cell_count)
        result_flat = fresh_flat.at[:, place_positions].set(
            gather_columns(shared, "gx"), mode="drop"
        )
        current = result_flat.reshape(lane_count, row_count, col_count)
    return current


def iota(shape, dim):
    return lax.broadcasted_iota(jnp.int32, shape, dim)


def rows_of(device):
    return pl.ds(pl.multiple_of(8 * device, 8), 8)


def take(tile, index):
    return jnp.take_along_axis(tile, index, axis=1, mode="promise_in_bounds")


def halves(values):
    high = values.astype(jnp.bfloat16)
    return high, (values - high.astype(F32)).astype(jnp.bfloat16)


def product(left, right, contract=(1, 0)):
    dims = (((contract[0],), (contract[1],)), ((), ()))
    return lax.dot_general(left, right, dims, preferred_element_type=F32)


def ranks(masks):
    rows = masks[0].shape[0]
    stacked = jnp.concatenate([jnp.where(m, 1.0, 0.0) for m in masks], axis=0)
    stacked = stacked.astype(jnp.bfloat16)
    before = jnp.where(iota((128, 128), 0) < iota((128, 128), 1), 1.0, 0.0).astype(jnp.bfloat16)
    ones = jnp.ones((128, 128), jnp.bfloat16)
    within = product(stacked, before)
    totals = product(stacked, ones)
    carry = jnp.zeros((rows, 128), F32)
    found = []
    for t in range(len(masks)):
        found.append(within[t * rows : (t + 1) * rows] + carry)
        carry = carry + totals[t * rows : (t + 1) * rows]
    return found, carry


def slot_table(masks, values, slots, mark_s, value_s):
    found, total = ranks(masks)
    for t in range(TILES):
        mark_s[t] = jnp.where(masks[t], found[t], -1.0)
        value_s[t] = values[t]
    slot_of = lax.rem(iota((8, 128), 1), slots)
    parts = []
    for part in range(GX // 8):
        span = slice(8 * part, 8 * part + 8)
        marks = [mark_s[t, span, :] for t in range(TILES)]
        vals = [value_s[t, span, :] for t in range(TILES)]
        table = jnp.zeros((8, 128), F32)
        for j in range(slots):
            picked = [jnp.where(m == float(j), v, 0.0) for m, v in zip(marks, vals)]
            while len(picked) > 1:
                picked = [sum(picked[k + 1 : k + 2], picked[k]) for k in range(0, len(picked), 2)]
            table = jnp.where(slot_of == j, jnp.sum(picked[0], axis=1, keepdims=True), table)
        parts.append(table)
    return jnp.concatenate(parts, axis=0), total


def swap_segments(tiles):
    segment = iota((8, 128), 1) // SLOTS
    moved = {}
    for shift in range(1 - FG, FG):
        diagonal = None
        for s in range(FG):
            if 0 <= s + shift < FG:
                tile = tiles[s + shift]
                diagonal = tile if diagonal is None else jnp.where(segment == s, tile, diagonal)
        by = (SLOTS * shift) % 128
        moved[shift] = diagonal if by == 0 else pltpu.roll(diagonal, by, 1)
    results = []
    for s in range(FG):
        result = moved[-s]
        for a in range(1, FG):
            result = jnp.where(segment == a, moved[a - s], result)
        results.append(result)
    return results


def send_cells(rows_s, table_ref, blocks_s, send_ref, sems):
    copies = []
    lane = iota((8, 128), 1)
    group_of = lane // SLOTS
    table = table_ref[0:GX, :]
    for g in range(7):
        index = jnp.zeros((1, 128), jnp.int32)
        members = [q for q in range(5 * g, 5 * g + 5) if q < GX]
        for q in members:
            index = jnp.where(group_of[0:1] == q - 5 * g, table[q : q + 1, :], index)
        index = jnp.broadcast_to(index, (8, 128))
        col = jnp.bitwise_and(index, 127)
        row = jnp.right_shift(index, 7)
        cells = [jnp.zeros((8, 128), F32) for _ in range(FG)]
        for r in range(ROWS):
            here = row == r
            for k in range(FG):
                cells[k] = jnp.where(here, take(rows_s[r, 8 * k : 8 * k + 8, :], col), cells[k])
        blocks = swap_segments(cells)
        for q in members:
            blocks_s[8 * q : 8 * q + 8, :] = blocks[q - 5 * g]
        span = pl.ds(8 * members[0], 8 * len(members))
        rows = pl.ds(SENT + 8 * members[0], 8 * len(members))
        copies.append(pltpu.make_async_copy(blocks_s.at[span, :], send_ref.at[rows, :], sems.at[g]))
        copies[-1].start()
    return copies


def edge_block(x_ref, col):
    lane = iota((8, 128), 1)
    block = jnp.zeros((8, 128), F32)
    for h in range(2):
        for f in range(LANES):
            edge = x_ref[f, 8 * h : 8 * h + 8, col : col + 1]
            block = jnp.where(lane == EDGE + h * LANES + f, edge, block)
    return block


def edge_copies(edges_s, send_ref, sems, grp, gx):
    right = lax.rem(gx + 1, GX)
    left = lax.rem(gx + GX - 1, GX)
    above = jnp.where(grp == 3, 3, jnp.maximum(grp - 1, 0))
    below = jnp.where(grp == 3, 3, jnp.minimum(grp + 1, 2))
    first, last = edges_s.at[0:8, :], edges_s.at[8:16, :]
    plan = [
        (last, grp * GX + right),
        (first, grp * GX + left),
        (last, above * GX + right),
        (first, below * GX + left),
    ]
    return [
        pltpu.make_async_copy(source, send_ref.at[rows_of(to), :], sems.at[i])
        for i, (source, to) in enumerate(plan)
    ]


def send_edges(x_ref, edges_s, send_ref, sems, grp, gx):
    edges_s[0:8, :] = edge_block(x_ref, 0)
    edges_s[8:16, :] = edge_block(x_ref, COLS - 1)
    near = edge_copies(edges_s, send_ref, sems, grp, gx)
    for copy in near[:2]:
        copy.start()

    @pl.when(jnp.logical_or(grp == 1, grp == 2))
    def _():
        near[2].start()

    @pl.when(grp < 2)
    def _():
        near[3].start()


def wait_edges(edges_s, send_ref, sems, grp, gx):
    near = edge_copies(edges_s, send_ref, sems, grp, gx)
    for copy in near[:2]:
        copy.wait()

    @pl.when(jnp.logical_or(grp == 1, grp == 2))
    def _():
        near[2].wait()

    @pl.when(grp < 2)
    def _():
        near[3].wait()


def unpack_edge(block):
    return jnp.concatenate([block, pltpu.roll(block, 128 - LANES, 1)], axis=0)


def update(x_ref, out_ref, diff_ref, cor_ref, mix_ref):
    lane = iota((ROWS, COLS), 1)
    row = iota((ROWS, COLS), 0)
    diff = diff_ref[...]
    cor = jnp.zeros((ROWS, COLS), F32)
    for r in range(ROWS):
        cor = jnp.where(row == r, cor_ref[r], cor)
    for f in range(LANES):
        level = f % LEVELS
        x = x_ref[f]
        up = jnp.where(row == 0, 0.0, pltpu.roll(x, 1, 0))
        down = jnp.where(row == ROWS - 1, 0.0, pltpu.roll(x, ROWS - 1, 0))
        westward = jnp.where(lane == 0, 0.0, pltpu.roll(x + down, 1, 1))
        eastward = jnp.where(lane == COLS - 1, 0.0, pltpu.roll(x + up, COLS - 1, 1))
        laplace = (westward + eastward) + (up + down) - 6.0 * x
        upper = x if level == LEVELS - 1 else x_ref[f + 1]
        lower = x if level == 0 else x_ref[f - 1]
        extra = mix_ref[level] * (upper - 2.0 * x + lower)
        if f < LEVELS:
            extra = extra + cor * x_ref[f + LEVELS]
        elif f < 2 * LEVELS:
            extra = extra - cor * x_ref[f - LEVELS]
        out_ref[f] = x + diff * laplace + extra


def gather_halo(recv_ref, grp, gx):
    right = lax.rem(gx + 1, GX)
    left = lax.rem(gx + GX - 1, GX)
    from_left = unpack_edge(recv_ref[rows_of(grp * GX + left), :])
    from_right = unpack_edge(recv_ref[rows_of(grp * GX + right), :])
    top_right = unpack_edge(recv_ref[rows_of(jnp.maximum(grp - 1, 0) * GX + right), :])
    low_left = unpack_edge(recv_ref[rows_of(jnp.minimum(grp + 1, 3) * GX + left), :])
    row = iota((ROWS, COLS), 0)
    corners = jnp.where(row == 0, top_right[ROWS - 1 : ROWS], low_left[0:1])
    return from_left, from_right, corners


def add_columns(from_ref, out_ref, halo, diff_ref, grp, gx):
    from_left, from_right, corners = halo
    nest = grp == 3
    lane = iota((ROWS, COLS), 1)
    row = iota((ROWS, COLS), 0)
    top_right = jnp.where(grp == 0, from_right[0:1], corners[0:1])
    low_left = jnp.where(grp == 2, from_left[ROWS - 1 : ROWS], corners[1:2])
    top_right = jnp.where(nest, 0.0, top_right)
    low_left = jnp.where(nest, 0.0, low_left)
    left_sum = from_left + jnp.where(row == ROWS - 1, low_left, pltpu.roll(from_left, ROWS - 1, 0))
    right_sum = from_right + jnp.where(row == 0, top_right, pltpu.roll(from_right, 1, 0))
    left_sum = jnp.where(jnp.logical_and(nest, gx == 0), 0.0, left_sum)
    right_sum = jnp.where(jnp.logical_and(nest, gx == GX - 1), 0.0, right_sum)
    diff = diff_ref[...]
    left_sum = left_sum * diff[:, 0:1]
    right_sum = right_sum * diff[:, COLS - 1 : COLS]
    source = jnp.bitwise_and(EDGE + jnp.right_shift(lane + 1, 1), 127)
    spread = jnp.concatenate(
        [
            jnp.where(
                jnp.bitwise_and(lane[0:8], 1) == 0,
                take(left_sum[h : h + 8], source[0:8]),
                take(right_sum[h : h + 8], jnp.where(lane[0:8] == 127, EDGE, source[0:8])),
            )
            for h in (0, 8)
        ],
        axis=0,
    )
    outer = jnp.logical_or(lane == 0, lane == COLS - 1)
    for f in range(LANES):
        moved = spread if f == 0 else pltpu.roll(spread, 128 - 2 * f, 1)
        out_ref[f] = from_ref[f] + jnp.where(outer, moved, 0.0)


def add_rows(first_ref, last_ref, out_ref, above_ref, below_ref, diff_ref, grp):
    lane = iota((LANES, COLS), 1)
    above = jnp.where(grp == 0, first_ref[...], above_ref[...])
    below = jnp.where(grp == 2, last_ref[...], below_ref[...])
    above = above + jnp.where(lane == COLS - 1, 0.0, pltpu.roll(above, COLS - 1, 1))
    below = below + jnp.where(lane == 0, 0.0, pltpu.roll(below, 1, 1))
    out_ref[:, 0, :] = out_ref[:, 0, :] + diff_ref[0:1, :] * above
    out_ref[:, ROWS - 1, :] = out_ref[:, ROWS - 1, :] + diff_ref[ROWS - 1 : ROWS, :] * below


def chunks(count, step, body):
    if count == step:
        for i in range(count):
            body(i)
        return

    def run(c, carry):
        for s in range(step):
            body(c * step + s)
        return carry

    lax.fori_loop(0, count // step, run, 0)


def regroup(recv_ref, group_s):
    def body(g):
        tiles = swap_segments([recv_ref[rows_of(g * 5 + i), :] for i in range(5)])
        for k in range(FG):
            group_s[g, 8 * k : 8 * k + 8, :] = tiles[k]

    chunks(PGROUPS, GROUP_UNROLL, body)


def regroup_hits(recv_ref, group_s):
    for h in range(2):
        first = SENT + 128 * h
        group_s[PGROUPS + h] = recv_ref[first : first + 128, :].T[0:LANES]


def interpolate(codes_ref, weight_s, group_s, groups, cycle_s, column_s):
    def cells_of(t):
        code = jnp.broadcast_to(codes_ref[pl.ds(t, 1), :], (8, 128))
        index = jnp.bitwise_and(code, 127)
        group = jnp.right_shift(code, 7)
        weight = weight_s[pl.ds(t, 1), :]
        cells = [jnp.zeros((8, 128), F32) for _ in range(FG)]
        for g in range(groups):
            here = group == g
            for k in range(FG):
                cells[k] = jnp.where(here, take(group_s[g, 8 * k : 8 * k + 8, :], index), cells[k])
        return [weight * c for c in cells]

    cycle_s[...] = jnp.zeros((2, LANES, 128), F32)

    def body(t):
        span = t % 2
        for k, cells in enumerate(cells_of(t)):
            cycle_s[span, 8 * k : 8 * k + 8, :] += cells

    chunks(6, UNROLL, body)
    for k, cells in enumerate(cells_of(6)):
        total = cells + pltpu.roll(cells, 96, 1) + pltpu.roll(cells, 64, 1)
        column_s[8 * k : 8 * k + 8, :] = total


def load_weights(weight_ref, weight_s, gx):
    weight_s[...] = jnp.zeros((8, 128), F32)
    for k in range(3):
        own = weight_ref[k, pl.ds(gx, 1), :]
        weight_s[2 * k : 2 * k + 1, :] = own[:, 0:128]
        weight_s[2 * k + 1 : 2 * k + 2, :] = own[:, 128:256]
        weight_s[6:7, 32 * k : 32 * k + 32] = own[:, 256:288]


def prescribe(out_ref, cycle_s, column_s, gx):
    lane = iota((ROWS, COLS), 1)

    @pl.when(jnp.logical_or(gx == 0, gx == GX - 1))
    def _():
        turned = jnp.concatenate([column_s[...], jnp.zeros((88, 128), F32)], axis=0).T
        column = jnp.where(gx == 0, turned[0:ROWS, :], turned[ROWS : 2 * ROWS, :])
        at = jnp.where(gx == 0, 0, COLS - 1)
        for f in range(LANES):
            out_ref[f] = jnp.where(lane == at, column[:, f : f + 1], out_ref[f])

    out_ref[:, 0, :] = cycle_s[0]
    out_ref[:, ROWS - 1, :] = cycle_s[1]


def coarse_values(out_ref):
    mean = jnp.where(iota((32, 128), 1) // 4 == iota((32, 128), 0), 1.0 / 16.0, 0.0)
    parts = []
    for i in range(4):
        total = (out_ref[:, 4 * i, :] + out_ref[:, 4 * i + 1, :]) + (
            out_ref[:, 4 * i + 2, :] + out_ref[:, 4 * i + 3, :]
        )
        wide = jnp.concatenate([total, total, total, jnp.zeros((8, 128), F32)], axis=0)
        high, low = halves(wide)
        weights = mean.astype(jnp.bfloat16)
        parts.append(product(weights, high, (1, 1)) + product(weights, low, (1, 1)))
    coarse = jnp.concatenate(parts, axis=0)
    plane_of = iota((128, 128), 1) // LANES
    placed = [jnp.where(plane_of == plane, coarse, 0.0) for plane in range(PLANES)]
    return jnp.concatenate(halves(jnp.concatenate(placed, axis=0)), axis=1)


def picked(pick, values):
    both = product(pick, values)
    return both[:, 0:128] + both[:, 128:256]


def unpack_entries(pick_ref, values):
    total = picked(pick_ref[...], jnp.concatenate(halves(values), axis=1))
    entries = total[0:ENTRIES]
    for plane in range(1, PLANES):
        part = total[plane * ENTRIES : (plane + 1) * ENTRIES]
        entries = entries + pltpu.roll(part, 128 - LANES * plane, 1)
    return entries


def place_rows(codes, turned, own):
    code = jnp.broadcast_to(codes, (8, 128))
    index = jnp.bitwise_and(code, 127)
    return [
        jnp.where(code >= 0, take(turned[8 * k : 8 * k + 8], index), own(slice(8 * k, 8 * k + 8)))
        for k in range(FG)
    ]


def feed_back(src_ref, out_ref, turned, map_ref):
    for r in range(ROWS):
        cells = place_rows(map_ref[r : r + 1, :], turned, lambda span: src_ref[span, r, :])
        for k in range(FG):
            out_ref[8 * k : 8 * k + 8, r, :] = cells[k]


def neighbours_of(owner, cell):
    row = jnp.right_shift(cell, 7)
    col = jnp.bitwise_and(cell, 127)
    at = jnp.bitwise_and(owner, GX - 1)
    left = owner - at + jnp.bitwise_and(at + GX - 1, GX - 1)
    right = owner - at + jnp.bitwise_and(at + 1, GX - 1)
    top = jnp.logical_and(row == 0, owner >= GX)
    low = jnp.logical_and(row == ROWS - 1, owner < 2 * GX)
    beside = jnp.where(col == 0, left, jnp.where(col == COLS - 1, right, -1))
    across = jnp.where(top, owner - GX, jnp.where(low, owner + GX, -1))
    diagonal = jnp.where(
        jnp.logical_and(low, col == 0),
        left + GX,
        jnp.where(jnp.logical_and(top, col == COLS - 1), right - GX, -1),
    )
    return owner, beside, across, diagonal


def feedback_routes(owner_ref, cell_ref, pick_ref, map_ref, halo_ref, me):
    cell = cell_ref[...]
    owner = owner_ref[...]
    row = jnp.right_shift(cell, 7)
    col = jnp.bitwise_and(cell, 127)
    own = owner == me
    left = me - lax.rem(me, GX) + lax.rem(me + GX - 1, GX)
    right = me - lax.rem(me, GX) + lax.rem(me + 1, GX)
    above = jnp.logical_and(owner == me - GX, row == ROWS - 1)
    below = jnp.logical_and(owner == me + GX, row == 0)
    target = jnp.where(jnp.logical_and(owner == left, col == COLS - 1), row, -1)
    target = jnp.where(jnp.logical_and(owner == right, col == 0), ROWS + row, target)
    corner = jnp.logical_and(row == ROWS - 1, col == 0)
    target = jnp.where(jnp.logical_and(owner == right - GX, corner), 2 * ROWS, target)
    corner = jnp.logical_and(row == 0, col == COLS - 1)
    target = jnp.where(jnp.logical_and(owner == left + GX, corner), 2 * ROWS + 1, target)
    taken = jnp.logical_or(jnp.logical_or(own, target >= 0), jnp.logical_or(above, below))
    found, total = ranks([taken])
    slot = jnp.minimum(found[0], float(MEANS - 1))
    before = jnp.where(iota((GX, GX), 1) < iota((GX, GX), 0), 1.0, 0.0).astype(jnp.bfloat16)
    entry = found[0] + product(before, total.astype(jnp.bfloat16))
    plane = jnp.floor(slot * (1.0 / DEPTH))
    place = iota((GX, 128), 0).astype(F32) * float(DEPTH) + (slot - float(DEPTH) * plane)
    line = jnp.where(own, row, jnp.where(above, ROWS, jnp.where(below, ROWS + 1, -1)))
    entry = jnp.where(taken, entry, -1.0)
    target = target.astype(F32)
    cells = jnp.zeros((2 * ROWS, 128), F32)
    codes = jnp.zeros((ENTRIES, 128), F32)
    for q in range(GX):
        one = slice(q, q + 1)
        here = jnp.where(iota((2 * ROWS, 128), 0) == line[one], entry[one] + 1.0, 0.0)
        hot = jnp.where(iota((128, 128), 0) == col[one], 1.0, 0.0)
        cells = cells + product(here.astype(jnp.bfloat16), hot.astype(jnp.bfloat16), (1, 1))
        hot = jnp.where(iota((ENTRIES, 128), 0).astype(F32) == entry[one], 1.0, 0.0)
        number = iota((128, 128), 0)
        facts = jnp.where(number == 1, plane[one] + 1.0, 0.0)
        facts = jnp.where(number == 0, place[one], jnp.where(number == 2, target[one] + 1.0, facts))
        codes = codes + product(hot.astype(jnp.bfloat16), facts.astype(jnp.bfloat16), (1, 1))
    map_ref[...] = cells.astype(jnp.int32) - 1
    at = codes[:, 0:1]
    level = codes[:, 1:2] - 1.0
    lane = iota((ENTRIES, 128), 1).astype(F32)
    for p in range(PLANES):
        hot = jnp.where(jnp.where(level == float(p), at, -1.0) == lane, 1.0, 0.0)
        pick_ref[p * ENTRIES : (p + 1) * ENTRIES, :] = hot.astype(jnp.bfloat16)
    goal = codes.T[2:3, :] - 1.0
    halo_ref[...] = jnp.where(iota((3 * ROWS, 128), 0).astype(F32) == goal, 1.0, 0.0).astype(
        jnp.bfloat16
    )


def load_terms(owner_ref, cell_ref, gid_s):
    gid_s[6] = jnp.full((GX, 128), -1, jnp.int32)
    for k in range(3):
        gid = owner_ref[k] * 2048 + cell_ref[k]
        gid_s[2 * k] = gid[:, 0:128]
        gid_s[2 * k + 1] = gid[:, 128:256]
        gid_s[6, :, 32 * k : 32 * k + 32] = gid[:, 256:288]


def flag_block(over):
    worst = jnp.max(over, axis=0, keepdims=True)
    flag = jnp.where(worst > 0.5, 1.0, 0.0)
    return jnp.where(iota((8, 128), 1) == 127, jnp.broadcast_to(flag, (8, 128)), 0.0)


def first_kernel(
    x_ref, owner_ref, cell_ref, send_ref, table_ref, last_row_ref, first_row_ref,
    x_s, owner_s, cell_s, gid_s, mark_s, value_s, rows_s, blocks_s, edges_s, in_sems, out_sems, edge_sems,
):
    grp = lax.axis_index("grp")
    gx = lax.axis_index("gx")
    fetch_x = pltpu.make_async_copy(x_ref, x_s, in_sems.at[0])
    fetch_index = [
        pltpu.make_async_copy(owner_ref, owner_s, in_sems.at[1]),
        pltpu.make_async_copy(cell_ref, cell_s, in_sems.at[2]),
    ]

    @pl.when(grp < 3)
    def _():
        for copy in fetch_index:
            copy.start()
        fetch_x.start()
        for copy in fetch_index:
            copy.wait()
        load_terms(owner_s, cell_s, gid_s)
        gids = [gid_s[t] for t in range(TILES)]
        masks = [jnp.right_shift(g, 11) == grp * GX + gx for g in gids]
        values = [jnp.bitwise_and(g, 2047).astype(F32) for g in gids]
        table, _ = slot_table(masks, values, SLOTS, mark_s, value_s)
        table_ref[...] = table.astype(jnp.int32)
        fetch_x.wait()
        send_edges(x_s, edges_s, send_ref, edge_sems, grp, gx)
        last_row_ref[...] = x_s[:, ROWS - 1, :]
        first_row_ref[...] = x_s[:, 0, :]
        for r in range(ROWS):
            rows_s[r] = x_s[:, r, :]
        for copy in send_cells(rows_s, table_ref, blocks_s, send_ref, out_sems):
            copy.wait()

    @pl.when(grp == 3)
    def _():
        fetch_x.start()
        fetch_x.wait()
        send_edges(x_s, edges_s, send_ref, edge_sems, grp, gx)

    wait_edges(edges_s, send_ref, edge_sems, grp, gx)


def tables_kernel(
    x_ref, diff_ref, cor_ref, mix_ref, owner_ref, cell_ref, weight_ref, fb_owner_ref, fb_cell_ref,
    fresh_ref, codes_ref, weights_ref, pick_ref, hits_ref, flag_ref, map_ref, entry_ref, halo_ref,
    near_diff_ref, gid_s, mark_s, value_s, found_s, seek_s,
):
    grp = lax.axis_index("grp")
    gx = lax.axis_index("gx")
    update(x_ref, fresh_ref, diff_ref, cor_ref, mix_ref)
    near_diff_ref[...] = diff_ref[...]

    @pl.when(grp < 3)
    def _():
        feedback_routes(
            fb_owner_ref, fb_cell_ref, entry_ref, map_ref, halo_ref, grp * GX + gx
        )

    @pl.when(grp == 3)
    def _():
        load_terms(owner_ref, cell_ref, gid_s)
        load_weights(weight_ref, weights_ref, gx)

        number = iota((PARENTS, 128), 0)
        everyone = neighbours_of(fb_owner_ref[...], fb_cell_ref[...])
        back = jnp.zeros((PARENTS, 128), F32)
        for q in range(GX):
            hit = number == everyone[0][q : q + 1, :]
            for other in everyone[1:]:
                hit = jnp.logical_or(hit, number == other[q : q + 1, :])
            back = back + jnp.where(hit, 1.0, 0.0)
        back = jnp.sum(back, axis=1, keepdims=True)

        own_cell = fb_cell_ref[pl.ds(gx, 1), :]
        goals = neighbours_of(fb_owner_ref[pl.ds(gx, 1), :], own_cell)
        number = iota((128, 128), 0)
        hots = [number == goal for goal in goals]
        anyone = jnp.logical_or(jnp.logical_or(hots[0], hots[1]), jnp.logical_or(hots[2], hots[3]))
        found, total = ranks([anyone])
        over = jnp.max(jnp.where(total > float(MEANS), 1.0, 0.0), axis=0, keepdims=True)
        over = jnp.maximum(
            over, jnp.max(jnp.where(back > float(ENTRIES), 1.0, 0.0), axis=0, keepdims=True)
        )
        most = jnp.minimum(jnp.max(total).astype(jnp.int32), 32)
        slots = [
            jnp.sum(jnp.where(h, found[0], 0.0), axis=0, keepdims=True).astype(jnp.int32)
            for h in hots
        ]
        for p in range(PLANES):
            wanted = [
                jnp.where(
                    jnp.logical_and(goal >= 0, slot // DEPTH == p), goal * DEPTH + slot % DEPTH, -1
                )
                for goal, slot in zip(goals, slots)
            ]
            for part in range(MEAN_ROWS // 128):
                line = number + 128 * part
                hit = line == wanted[0]
                for other in wanted[1:]:
                    hit = jnp.logical_or(hit, line == other)
                pick_ref[128 * part : 128 * part + 128, 128 * p : 128 * p + 128] = jnp.where(
                    hit, 1.0, 0.0
                ).astype(jnp.bfloat16)
        hot, rank = hots[0], slots[0]

        owners = [jnp.right_shift(gid_s[t, pl.ds(gx, 1), :], 11) for t in range(TILES)]
        hots = [iota((PARENTS, 128), 0) == o for o in owners]
        found, total = ranks(hots)
        over = jnp.maximum(
            over, jnp.max(jnp.where(total > float(SLOTS), 1.0, 0.0), axis=0, keepdims=True)
        )
        codes = []
        for t in range(TILES):
            slot = jnp.sum(jnp.where(hots[t], found[t], 0.0), axis=0, keepdims=True)
            slot = jnp.minimum(slot.astype(jnp.int32), SLOTS - 1)
            group = jnp.right_shift(owners[t] * 205, 10)
            codes.append(group * 128 + (owners[t] - 5 * group) * SLOTS + slot)
        for t, code in enumerate(codes):
            codes_ref[t : t + 1, :] = code

        hot = jnp.where(hot, 1.0, 0.0).astype(jnp.bfloat16)
        chosen = iota((32, 128), 0) == rank

        def by_owner(values):
            picked = jnp.where(chosen, values.astype(F32), 0.0).astype(jnp.bfloat16)
            return product(picked, hot, (1, 1)).astype(jnp.int32)

        number = by_owner(iota((1, 128), 1) + 1)
        cells = by_owner(jnp.right_shift(own_cell, 4)) * 16 + by_owner(jnp.bitwise_and(own_cell, 15))
        seek_s[...] = jnp.where(number > 0, cells * 256 + number - 1, -1)
        found_s[...] = jnp.full((TILES, GX, 128), -1, jnp.int32)

        def seek(j, carry):
            line = jnp.broadcast_to(seek_s[pl.ds(j, 1), :], (8, 128))
            for t in range(TILES):
                for part in range(GX // 8):
                    span = slice(8 * part, 8 * part + 8)
                    gid = gid_s[t, span, :]
                    entry = take(line, jnp.bitwise_and(jnp.right_shift(gid, 11), 127))
                    same = jnp.right_shift(entry, 8) == jnp.bitwise_and(gid, 2047)
                    found_s[t, span, :] = jnp.where(
                        same, jnp.bitwise_and(entry, 255), found_s[t, span, :]
                    )
            return carry

        lax.fori_loop(0, most, seek, 0)
        found_at = [found_s[t] for t in range(TILES)]
        table, total = slot_table(
            [f >= 0 for f in found_at], [f.astype(F32) for f in found_at], HITS, mark_s, value_s
        )
        over = jnp.maximum(
            over, jnp.max(jnp.where(total > float(HITS), 1.0, 0.0), axis=0, keepdims=True)
        )
        turned = jnp.concatenate([table, jnp.zeros((96, 128), F32)], axis=0).T
        lane = iota((8, 128), 1).astype(F32)
        for pair in range(GX // 2):
            hits = [
                jnp.where(turned[0:HITS, q : q + 1] == lane, 1.0, 0.0)
                for q in (2 * pair, 2 * pair + 1)
            ]
            line = slice(16 * pair, 16 * pair + 16)
            hits_ref[line, :] = jnp.concatenate(hits, axis=0).astype(jnp.bfloat16)
        flag_ref[...] = flag_block(over)


def second_kernel(
    recv_ref, fresh_ref, diff_ref, above_ref, below_ref, first_ref, last_ref, weights_ref, table_ref,
    codes_ref, pick_ref, hits_ref, flag_ref, out_ref, send_ref, last_row_ref, first_row_ref,
    rows_s, group_s, cycle_s, column_s, blocks_s, edges_s, out_sems, edge_sems,
):
    grp = lax.axis_index("grp")
    gx = lax.axis_index("gx")
    @pl.when(grp < 3)
    def _():
        add_columns(fresh_ref, out_ref, gather_halo(recv_ref, grp, gx), diff_ref, grp, gx)
        add_rows(first_ref, last_ref, out_ref, above_ref, below_ref, diff_ref, grp)
        send_edges(out_ref, edges_s, send_ref, edge_sems, grp, gx)
        last_row_ref[...] = out_ref[:, ROWS - 1, :]
        first_row_ref[...] = out_ref[:, 0, :]
        for r in range(ROWS):
            rows_s[r] = out_ref[:, r, :]
        for copy in send_cells(rows_s, table_ref, blocks_s, send_ref, out_sems):
            copy.wait()
        wait_edges(edges_s, send_ref, edge_sems, grp, gx)

    @pl.when(grp == 3)
    def _():
        add_columns(fresh_ref, out_ref, gather_halo(recv_ref, grp, gx), diff_ref, grp, gx)
        regroup(recv_ref, group_s)
        interpolate(codes_ref, weights_ref, group_s, PGROUPS, cycle_s, column_s)
        prescribe(out_ref, cycle_s, column_s, gx)
        values = coarse_values(out_ref)
        base = flag_ref[0:1, :]
        sent = picked(pick_ref[...], values) + base
        for j in range(PARENTS // 2):
            tile = sent[8 * j : 8 * j + 8]
            blocks_s[16 * j : 16 * j + 8, :] = tile
            blocks_s[16 * j + 8 : 16 * j + 16, :] = pltpu.roll(tile, DEPTH, 0)
        copies = [
            pltpu.make_async_copy(blocks_s.at[rows, :], send_ref.at[rows, :], out_sems.at[i])
            for i, rows in enumerate((pl.ds(0, SENT), pl.ds(SENT, TAKEN)))
        ]
        copies[0].start()
        blocks_s[SENT : SENT + TAKEN, :] = picked(hits_ref[...], values[0:128]) + base
        right = rows_of(PARENTS + lax.rem(gx + 1, GX))
        left = rows_of(PARENTS + lax.rem(gx + GX - 1, GX))
        blocks_s[right, :] = blocks_s[right, :] + edge_block(out_ref, COLS - 1)
        blocks_s[left, :] = blocks_s[left, :] + edge_block(out_ref, 0)
        copies[1].start()
        for copy in copies:
            copy.wait()


def hits_kernel(
    x_ref, diff_ref, cor_ref, mix_ref, owner_ref, cell_ref, fb_owner_ref, fb_cell_ref, plain_ref,
    fresh_ref, codes_ref, gid_s, turned_s,
):
    gx = lax.axis_index("gx")

    @pl.when(lax.axis_index("grp") == 3)
    def _():
        update(x_ref, fresh_ref, diff_ref, cor_ref, mix_ref)
        load_terms(owner_ref, cell_ref, gid_s)
        terms = [gid_s[t, pl.ds(gx, 1), :] for t in range(TILES)]
        fed = (fb_owner_ref[...] * 2048 + fb_cell_ref[...]).astype(F32)
        turned_s[...] = jnp.concatenate([fed, jnp.full((96, 128), -2.0, F32)], axis=0).T
        wide = [jnp.broadcast_to(t.astype(F32), (8, 128)) for t in terms]

        def match(q, from_block):
            index = jnp.full((8, 128), q, jnp.int32)
            for s in range(16):
                part = take(turned_s[8 * s : 8 * s + 8, :], index)
                from_block = [jnp.where(part == w, q, f) for w, f in zip(wide, from_block)]
            return from_block

        none = [jnp.full((8, 128), -1, jnp.int32) for _ in terms]
        from_block = lax.fori_loop(0, GX // 2, lambda c, f: match(2 * c + 1, match(2 * c, f)), none)
        sources = [jnp.max(f, axis=0, keepdims=True) for f in from_block]
        hots = [iota((GX, 128), 0) == s for s in sources]
        found, _ = ranks(hots)
        codes = []
        for t in range(TILES):
            slot = jnp.sum(jnp.where(hots[t], found[t], 0.0), axis=0, keepdims=True)
            slot = jnp.minimum(slot.astype(jnp.int32), HITS - 1)
            code = (PGROUPS + jnp.right_shift(sources[t], 4)) * 128
            code = code + jnp.bitwise_and(sources[t], 15) * HITS + slot
            codes.append(jnp.where(sources[t] >= 0, code, -1))
        for t, code in enumerate(codes):
            plain = plain_ref[t : t + 1, :]
            codes_ref[t : t + 1, :] = jnp.where(code >= 0, code, plain)


def third_kernel(
    recv_ref, x_ref, fresh_ref, diff_ref, weights_ref, codes_ref, pick_ref, map_ref, entry_ref,
    halo_ref, above_ref, below_ref, out_ref, send_ref, flag_ref, rims_ref, halos_ref,
    group_s, cycle_s, column_s, blocks_s, out_sem,
):
    grp = lax.axis_index("grp")
    gx = lax.axis_index("gx")
    flag = recv_ref[SENT : SENT + 8, :]
    for q in range(1, GX):
        flag = jnp.maximum(flag, recv_ref[SENT + 8 * q : SENT + 8 * q + 8, :])
    flag_ref[...] = flag

    @pl.when(grp < 3)
    def _():
        upper = iota((8, 128), 0) < DEPTH
        tiles = []
        for j in range(GX // 2):
            even = recv_ref[SENT + 16 * j : SENT + 16 * j + 8, :]
            odd = recv_ref[SENT + 16 * j + 8 : SENT + 16 * j + 16, :]
            tiles.append(jnp.where(upper, even, pltpu.roll(odd, DEPTH, 0)))
        entries = unpack_entries(entry_ref, jnp.concatenate(tiles, axis=0))
        turned = entries.T
        feed_back(x_ref, out_ref, turned, map_ref)
        for k, cells in enumerate(
            place_rows(map_ref[ROWS : ROWS + 1, :], turned, lambda span: above_ref[span, :])
        ):
            rims_ref[0, 8 * k : 8 * k + 8, :] = cells
        for k, cells in enumerate(
            place_rows(map_ref[ROWS + 1 : ROWS + 2, :], turned, lambda span: below_ref[span, :])
        ):
            rims_ref[1, 8 * k : 8 * k + 8, :] = cells
        hot = halo_ref[...]
        moved = jnp.concatenate(halves(pltpu.roll(entries, EDGE, 1)), axis=1)
        fed = jnp.sum(hot.astype(F32), axis=1, keepdims=True) > 0.5
        before = jnp.concatenate(gather_halo(recv_ref, grp, gx), axis=0)
        halos_ref[...] = jnp.where(fed, picked(hot, moved), before)

    @pl.when(grp == 3)
    def _():
        add_columns(fresh_ref, out_ref, gather_halo(recv_ref, grp, gx), diff_ref, grp, gx)
        regroup(recv_ref, group_s)
        regroup_hits(recv_ref, group_s)
        interpolate(codes_ref, weights_ref, group_s, GROUPS, cycle_s, column_s)
        prescribe(out_ref, cycle_s, column_s, gx)
        blocks_s[...] = picked(pick_ref[...], coarse_values(out_ref))
        copy = pltpu.make_async_copy(blocks_s, send_ref.at[pl.ds(0, MEAN_ROWS), :], out_sem.at[0])
        copy.start()
        copy.wait()


def parents_kernel(x_ref, diff_ref, cor_ref, mix_ref, rims_ref, halos_ref, fresh_ref):
    grp = lax.axis_index("grp")

    @pl.when(grp < 3)
    def _():
        update(x_ref, fresh_ref, diff_ref, cor_ref, mix_ref)
        halo = (halos_ref[0:ROWS, :], halos_ref[ROWS : 2 * ROWS, :], halos_ref[2 * ROWS : 3 * ROWS, :])
        add_columns(fresh_ref, fresh_ref, halo, diff_ref, grp, lax.axis_index("gx"))
        first = x_ref[:, 0, :]
        last = x_ref[:, ROWS - 1, :]
        add_rows(first, last, fresh_ref, rims_ref[0], rims_ref[1], diff_ref, grp)


def fourth_kernel(recv_ref, x_ref, fresh_ref, map_ref, entry_ref, out_ref):
    grp = lax.axis_index("grp")

    @pl.when(grp < 3)
    def _():
        entries = unpack_entries(entry_ref, recv_ref[MEAN_ROWS : MEAN_ROWS + 128, :])
        feed_back(fresh_ref, out_ref, entries.T, map_ref)

    @pl.when(grp == 3)
    def _():
        out_ref[...] = x_ref[...]


def call(kernel, name, ins, spaces, outs, out_spaces, scratch, sems=()):
    space = {"s": pltpu.SMEM, "v": pltpu.VMEM, "a": pl.ANY}
    return pl.pallas_call(
        kernel,
        name=name,
        in_specs=[pl.BlockSpec(memory_space=space[s]) for s in spaces],
        out_specs=[pl.BlockSpec(memory_space=space[s]) for s in out_spaces],
        out_shape=[jax.ShapeDtypeStruct(s, d) for s, d in outs],
        scratch_shapes=[pltpu.VMEM(s, d) for s, d in scratch]
        + [pltpu.SemaphoreType.DMA((n,)) for n in sems],
        compiler_params=pltpu.CompilerParams(vmem_limit_bytes=VMEM_LIMIT),
        cost_estimate=pl.CostEstimate(flops=1000000, bytes_accessed=4000000, transcendentals=0),
    )(*ins)


STATE = ((LANES, ROWS, COLS), F32)
BLOCKS = ((DEVICES * 8, 128), F32)
BLOCK = ((8, 128), F32)
RIM = ((LANES, COLS), F32)
ROWMAJOR = ((ROWS, LANES, COLS), F32)
MAP = ((2 * ROWS, 128), jnp.int32)
GIDS = ((TILES, GX, 128), jnp.int32)
TERMS = ((TILES, GX, 128), F32)
PICK = ((MEAN_ROWS, PLANES * 128), jnp.bfloat16)
HIT = ((TAKEN, 128), jnp.bfloat16)
ENTRY = ((PLANES * ENTRIES, 128), jnp.bfloat16)
HALO = ((3 * ROWS, 128), jnp.bfloat16)
DIFFUSION = ((ROWS, COLS), F32)
HALOS = ((3 * ROWS, 128), F32)
RIMS = ((2, LANES, COLS), F32)
THIN = ((DEVICES * DEPTH, 128), F32)
GROUPED = ((GROUPS, LANES, 128), F32)
CYCLE = ((2, LANES, 128), F32)
TABLE = ((GX, 128), jnp.int32)
CODES = ((8, 128), jnp.int32)
INDEX = ((3, GX, PERIM), jnp.int32)
EDGES = ((16, 128), F32)
TO_NEST = ((TAKEN, 128), F32)


def exchange(blocks):
    return lax.all_to_all(blocks, ("grp", "gx"), 0, 0, tiled=True)


def rims(last_row, first_row):
    above = lax.ppermute(last_row, "grp", [(0, 1), (1, 2)])
    below = lax.ppermute(first_row, "grp", [(1, 0), (2, 1)])
    return above, below


def shards(atmosphere, diffusion, coriolis, mixing, owner, cell, weight, fb_owner, fb_cell):
    inputs = (atmosphere, diffusion, coriolis, mixing, owner, cell, weight, fb_owner, fb_cell)
    owner, cell, weight = (jnp.transpose(a, (1, 0, 2)) for a in (owner, cell, weight))
    physics = (diffusion, coriolis, mixing)
    send, table, last_row, first_row = call(
        first_kernel,
        "first_cells",
        (atmosphere, owner, cell),
        "aaa",
        (BLOCKS, TABLE, RIM, RIM),
        "avvv",
        (STATE, INDEX, INDEX, GIDS, TERMS, TERMS, ROWMAJOR, TO_NEST, EDGES),
        (3, 7, 4),
    )
    recv = exchange(send)
    above, below = rims(last_row, first_row)
    fresh, codes, weights, pick, hits, flag, place, entry, halo, near_diffusion = call(
        tables_kernel,
        "tables",
        (atmosphere,) + physics + (owner, cell, weight, fb_owner, fb_cell),
        "vvssvvvvv",
        (STATE, CODES, BLOCK, PICK, HIT, BLOCK, MAP, ENTRY, HALO, DIFFUSION),
        "v" * 10,
        (GIDS, TERMS, TERMS, GIDS, ((32, 128), jnp.int32)),
    )
    state, send, next_last, next_first = call(
        second_kernel,
        "substep_one",
        (recv, fresh, near_diffusion, above, below, first_row, last_row, weights, table, codes, pick, hits, flag),
        "v" * 13,
        (STATE, BLOCKS, RIM, RIM),
        "vavv",
        (ROWMAJOR, GROUPED, CYCLE, RIM, BLOCKS, EDGES),
        (7, 4),
    )
    recv = exchange(send)
    above, below = rims(next_last, next_first)
    fresh, codes = call(
        hits_kernel,
        "hits",
        (state,) + physics + (owner, cell, fb_owner, fb_cell, codes),
        "vvssvvvvv",
        (STATE, CODES),
        "vv",
        (GIDS, ((128, 128), F32)),
    )
    state, send, flag, edge_rows, halos = call(
        third_kernel,
        "substep_two",
        (recv, state, fresh, diffusion, weights, codes, pick, place, entry, halo, above, below),
        "v" * 12,
        (STATE, THIN, BLOCK, RIMS, HALOS),
        "vavvv",
        (GROUPED, CYCLE, RIM, ((MEAN_ROWS, 128), F32)),
        (1,),
    )
    recv = exchange(send)
    (fresh,) = call(
        parents_kernel,
        "parents",
        (state,) + physics + (edge_rows, halos),
        "vvssvv",
        (STATE,),
        "v",
        (),
    )

    def finish(received, *_):
        return call(fourth_kernel, "finish", received, "v" * 5, (STATE,), "v", ())[0]

    received = (recv, state, fresh, place, entry)
    return lax.cond(flag[0, 127] > 0.5, lambda _, *a: dense_plan(*a), finish, received, *inputs)


def solution(mesh):
    placed = (P(None, "grp", "gx"), P("grp", "gx"), P("grp"), P(), P(), P(), P(), P(), P())
    return jax.shard_map(
        shards, mesh=mesh, in_specs=placed, out_specs=P(None, "grp", "gx"), check_vma=False
    )
```
